32 devices in a mesh: batch: 4 (over z), seq: 8 (over y, x, core).
Axes of the slice: x: 2, y: 2, z: 4, core: 2. Of those that a mesh axis runs over, the one named last changes fastest.
Arguments:
- latents: bfloat16 [4, 1024, 1024], P('batch', 'seq'), may hold values from -6 to 6
- pixels: bfloat16 [4, 3, 16384], P('batch', None, 'seq'), may hold values from -4 to 4
- counts: int32 [4, 33], P('batch'), may hold values from 1 to 1024, 16384 in all within a row
- latent_image: int32 [4, 1024], P('batch'), may hold values from 0 to 32, as said below
- query_gain: float32 [1024], replicated, may hold values from 0.5 to 1.5
- query_shift: float32 [1024], replicated, may hold values from -3 to 3
- query_weight: bfloat16 [1024, 1024], replicated, may hold values from -0.1875 to 0.1875
- input_gain: float32 [261], replicated, may hold values from 0.5 to 1.5
- input_shift: float32 [261], replicated, may hold values from -3 to 3
- kv_weight: bfloat16 [261, 2048], replicated, may hold values from -0.375 to 0.375
- out_weight: bfloat16 [1024, 1024], replicated, may hold values from -1.5 to 1.5
- mlp_gain: float32 [1024], replicated, may hold values from 0.5 to 1.5
- mlp_shift: float32 [1024], replicated, may hold values from -3 to 3
- up_weight: bfloat16 [1024, 1024], replicated, may hold values from -0.1875 to 0.1875
- down_weight: bfloat16 [1024, 1024], replicated, may hold values from -0.25 to 0.25
- cotangent: bfloat16 [4, 1024, 1024], P('batch', 'seq'), may hold values from -6 to 6
Outputs:
- mixed: bfloat16 [4, 1024, 1024], P('batch', 'seq')
- latent_grad: float32 [4, 1024, 1024], P('batch', 'seq')
- pixel_grad: float32 [4, 3, 16384], P('batch', None, 'seq')
- query_gain_grad: float32 [1024], P(('batch', 'seq'))
- query_shift_grad: float32 [1024], P(('batch', 'seq'))
- query_weight_grad: float32 [1024, 1024], P(('batch', 'seq'))
- input_gain_grad: float32 [261], replicated
- input_shift_grad: float32 [261], replicated
- kv_weight_grad: float32 [261, 2048], P(None, ('batch', 'seq'))
- out_weight_grad: float32 [1024, 1024], P(('batch', 'seq'))
- mlp_gain_grad: float32 [1024], P(('batch', 'seq'))
- mlp_shift_grad: float32 [1024], P(('batch', 'seq'))
- up_weight_grad: float32 [1024, 1024], P(('batch', 'seq'))
- down_weight_grad: float32 [1024, 1024], P(('batch', 'seq'))
The draws below stay inside these ranges and needn't reach their ends.
Inputs may be any that keep to these rules, and one draw needn't show every extreme that they name: The 33 counts of a packed row sum to 16384; images lie one after another in the row in the order of counts. `latent_image`: each latent may read any image of its packed row, in no particular order; every image has at least one latent.
All inputs are finite; a program needn't handle non-finite values.
Results may differ from the reference program's by a relative error of at most 0.015.
Values may be sent and summed in bfloat16 or wider, within the bound.
A program may use at most 256 MiB of HBM per device.

```python
import math
import jax
import jax.numpy as jnp
import numpy as np
from jax import lax

D = 1024
HID = 1024
BANDS = 64
IMG_W = 32
PIX_DEV = 2048
FEAT = 261
ROWS = 4
LAT_ROW = 1024
PIX_ROW = 16384
IMAGES = 33
N_SEQ = 8


def assign_latents(key):
    order_key = jax.random.fold_in(key, 11)
    pick_key = jax.random.fold_in(key, 12)
    order = jax.random.permutation(order_key, LAT_ROW).astype(jnp.int32)
    picks = jax.random.randint(pick_key, (LAT_ROW,), 0, IMAGES).astype(jnp.int32)
    return picks.at[order[:IMAGES]].set(jnp.arange(IMAGES, dtype=jnp.int32))


def draw_latent_image(key, part):
    row_keys = jax.random.split(jax.random.fold_in(key, 7), ROWS)
    return jax.vmap(assign_latents)(row_keys).astype(jnp.int32)


def block_levels(rng, extent, shards, low, largest):
    factor_of = 1.0
    for dim, shards_of in shards:
        steps = jax.random.uniform(jax.random.fold_in(jax.random.fold_in(rng, 6), dim), (shards_of,), jnp.float32, low / len(shards), largest / len(shards))
        factor_of = factor_of * jnp.repeat(jnp.exp(steps), extent[dim] // shards_of).reshape((-1,) + (1,) * (len(extent) - 1 - dim))
    return factor_of


def split_up(amount, total, bound, skew):
    portions = [(1 << 20) // math.isqrt(rank ** skew) + 1 for rank in range(2, amount + 1)]
    surplus, given = total - bound - (amount - 1), [1] * (amount - 1)
    while surplus > 0:
        candidates = [i for i in range(amount - 1) if given[i] < bound]
        pool, budget = sum([portions[i] for i in candidates]), surplus
        for i in candidates:
            extra = min(bound - given[i], max(1, budget * portions[i] // pool), surplus)
            given[i] = given[i] + extra
            surplus = surplus - extra
    return np.array([bound] + given)


def uneven_parts(stream_key, amount, total, bound, lean):
    if amount == 2:
        one = jax.random.randint(stream_key, (), max(1, total - bound), min(bound, total - 1) + 1)
        return jnp.stack([one, total - one])
    sizes = jnp.asarray(split_up(amount, total, bound, lean), jnp.int32)
    pairs = (amount - 1) // 2
    source_of, sink = sizes[1:1 + 2 * pairs:2], sizes[2:2 + 2 * pairs:2]
    margin = jnp.minimum(source_of - 1, bound - sink)
    moved = jax.random.randint(jax.random.fold_in(stream_key, 1), (pairs,), 0, 1 << 20) % (margin + 1)
    sizes = sizes.at[1:1 + 2 * pairs:2].set(source_of - moved).at[2:2 + 2 * pairs:2].set(sink + moved)
    return sizes[jax.random.permutation(jax.random.fold_in(stream_key, 2), amount)]


def normal_values(rng, shape, scale, limit, shards=(), held_as=jnp.bfloat16):
    array = scale * jax.random.normal(rng, shape, jnp.float32)
    if shards:
        array = array * block_levels(rng, shape, shards, -0.22, 0.18)
    return jnp.clip(array, -limit, limit).astype(held_as)


def setup_inputs(seed: int = 0) -> dict:
    keys = jax.random.split(jax.random.key(seed), 17)
    latents = normal_values(keys[0], (ROWS, LAT_ROW, D), 1.0, 6.0, ((0, 4), (1, 8)))
    pixels = normal_values(keys[1], (ROWS, 3, PIX_ROW), 1.0, 4.0, ((0, 4), (2, 8)))
    counts = jax.vmap(lambda own: uneven_parts(own, IMAGES, PIX_DEV * N_SEQ, IMG_W * IMG_W, 2))(jax.random.split(keys[2], ROWS)).reshape((ROWS, IMAGES)).astype(jnp.int32)
    latent_image = draw_latent_image(jax.random.fold_in(keys[16], 71), 0)
    query_gain = jnp.clip(1.0 + 0.1 * jax.random.normal(keys[4], (D,), jnp.float32), 0.5, 1.5)
    query_shift = normal_values(keys[5], (D,), 0.5, 3.0, (), jnp.float32)
    query_weight = normal_values(keys[6], (D, D), D ** -0.5, 0.1875)
    input_gain = jnp.clip(1.0 + 0.1 * jax.random.normal(keys[7], (FEAT,), jnp.float32), 0.5, 1.5)
    input_shift = normal_values(keys[8], (FEAT,), 0.5, 3.0, (), jnp.float32)
    kv_weight = normal_values(keys[9], (FEAT, 2 * D), FEAT ** -0.5, 0.375)
    out_weight = normal_values(keys[10], (D, D), (D // 64) ** -0.5, 1.5)
    mlp_gain = jnp.clip(1.0 + 0.1 * jax.random.normal(keys[11], (D,), jnp.float32), 0.5, 1.5)
    mlp_shift = normal_values(keys[12], (D,), 0.5, 3.0, (), jnp.float32)
    up_weight = normal_values(keys[13], (D, HID), D ** -0.5, 0.1875)
    down_weight = normal_values(keys[14], (HID, D), (HID // 2) ** -0.5, 0.25)
    cotangent = normal_values(keys[15], (ROWS, LAT_ROW, D), 1.0, 6.0, ((0, 4), (1, 8)))
    return dict(latents=latents, pixels=pixels, counts=counts, latent_image=latent_image, query_gain=query_gain, query_shift=query_shift, query_weight=query_weight, input_gain=input_gain, input_shift=input_shift, kv_weight=kv_weight, out_weight=out_weight, mlp_gain=mlp_gain, mlp_shift=mlp_shift, up_weight=up_weight, down_weight=down_weight, cotangent=cotangent)


top_freq = 112.0
tiny = 1e-05
floor_value = -1e+30

@jax.custom_vjp
def low(v):
    return lax.optimization_barrier(v.astype(jnp.bfloat16)).astype(jnp.float32)

@jax.custom_vjp
def low_back(v):
    return v

def low_keep(v):
    return (low(v), None)

def low_pass(kept, grad):
    return (grad,)

def back_keep(v):
    return (v, None)

def back_low(kept, grad):
    return (low(grad),)
low.defvjp(low_keep, low_pass)
low_back.defvjp(back_keep, back_low)

def product(operand, factor):
    return jnp.dot(operand, factor, precision=lax.Precision.HIGHEST, preferred_element_type=jnp.float32)

def norm_rows(values, gain_vec, shift_vec):
    center = values - lax.optimization_barrier(jnp.mean(values, axis=-1, keepdims=True))
    spread = lax.optimization_barrier(jnp.mean(center * center, axis=-1, keepdims=True))
    return center * lax.rsqrt(spread + tiny) * gain_vec + shift_vec

def features(colors, in_image):
    row_pos = (in_image // IMG_W).astype(jnp.float32)
    col_pos = (in_image % IMG_W).astype(jnp.float32)
    y_coord = 2.0 * row_pos / (IMG_W - 1) - 1.0
    x_coord = 2.0 * col_pos / (IMG_W - 1) - 1.0
    bands_vec = jnp.linspace(1.0, top_freq, BANDS).astype(jnp.float32)
    y_phase = math.pi * y_coord[:, None] * bands_vec[None, :]
    x_phase = math.pi * x_coord[:, None] * bands_vec[None, :]
    return jnp.concatenate([colors, y_coord[:, None], x_coord[:, None], jnp.sin(y_phase), jnp.sin(x_phase), jnp.cos(y_phase), jnp.cos(x_phase)], axis=1)

def image_of(places, lengths):
    ends = jnp.cumsum(lengths).astype(jnp.int32)
    image_ids = lax.optimization_barrier(jnp.sum((places[:, None] >= ends[None, :]).astype(jnp.int32), axis=1)).astype(jnp.int32)
    starts = (ends - lengths).astype(jnp.int32)
    number = jnp.arange(lengths.shape[0], dtype=jnp.int32)
    firsts = lax.optimization_barrier(jnp.sum(jnp.where(image_ids[:, None] == number[None, :], starts[None, :], 0), axis=1)).astype(jnp.int32)
    return (image_ids, (places - firsts).astype(jnp.int32))

def one_row(params, latent_row, color_row, length_row, owner_row):
    query_gain, query_shift, query_weight, input_gain, input_shift, kv_weight, out_weight, mlp_gain, mlp_shift, up_weight, down_weight = params
    places = jnp.arange(PIX_ROW, dtype=jnp.int32)
    image_ids, in_image = image_of(places, length_row)
    inputs = features(color_row.T, in_image)
    normed_in = low(norm_rows(inputs, input_gain, input_shift))
    key_value = low(low_back(product(normed_in, kv_weight)))
    key_rows = key_value[:, :D]
    value_rows = key_value[:, D:]
    normed_lat = low(norm_rows(latent_row, query_gain, query_shift))
    queries = low(low_back(product(normed_lat, query_weight)))
    block_rows = min(512, LAT_ROW)

    def attend(block_pair):
        query_block, owner_block = block_pair
        scores = low_back(product(query_block, key_rows.T) * D ** (-0.5))
        same_image = owner_block[:, None] == image_ids[None, :]
        row_top = lax.optimization_barrier(jnp.max(jnp.where(same_image, scores, floor_value), axis=1, keepdims=True))
        raised = jnp.exp(jnp.where(same_image, scores - row_top, floor_value))
        probs = raised / lax.optimization_barrier(jnp.sum(raised, axis=1, keepdims=True))
        return product(low(probs), value_rows)
    attended = lax.map(jax.checkpoint(attend), (queries.reshape(LAT_ROW // block_rows, block_rows, D), owner_row.reshape(LAT_ROW // block_rows, block_rows))).reshape(LAT_ROW, D)
    merged = low(low_back(attended))
    residual_mid = latent_row + low_back(product(merged, out_weight))
    normed_mid = low(norm_rows(residual_mid, mlp_gain, mlp_shift))
    hidden_pre = low_back(product(normed_mid, up_weight))
    hidden_act = low(jax.nn.gelu(hidden_pre, approximate=False))
    return residual_mid + product(hidden_act, down_weight)

def reference(latents, pixels, counts, latent_image, query_gain, query_shift, query_weight, input_gain, input_shift, kv_weight, out_weight, mlp_gain, mlp_shift, up_weight, down_weight, cotangent):
    params = tuple((weight.astype(jnp.float32) for weight in (query_gain, query_shift, query_weight, input_gain, input_shift, kv_weight, out_weight, mlp_gain, mlp_shift, up_weight, down_weight)))

    def forward(latent_all, color_all, param_set):

        def row_step(row_args):
            return one_row(param_set, row_args[0], row_args[1], row_args[2], row_args[3])
        return lax.map(jax.checkpoint(row_step), (latent_all, color_all, counts, latent_image))
    mixed, pull = jax.vjp(forward, latents.astype(jnp.float32), pixels.astype(jnp.float32), params)
    latent_grad, pixel_grad, grads = pull(cotangent.astype(jnp.float32))
    return (mixed.astype(jnp.bfloat16), latent_grad, pixel_grad, grads[0], grads[1], grads[2], grads[3], grads[4], grads[5], grads[6], grads[7], grads[8], grads[9], grads[10])
```

```python
import functools
import math
from types import SimpleNamespace

import jax
import jax.numpy as jnp
import numpy as np
from jax import lax
from jax.experimental import pallas as pl
from jax.experimental.pallas import tpu as pltpu
from jax.sharding import PartitionSpec as P

IMG_W = 32
TOP_FREQ = 112.0
TINY = 1e-05
FLOOR = -1e30
MESH = pl.DeviceIdType.MESH
F32 = jnp.float32
BF16 = jnp.bfloat16
LANES = 128
CELLS = IMG_W * IMG_W
SMALL_ORDER = ("c", "b", "a", "z")
COLOR = 2 * IMG_W
ONE = COLOR + 3


def position_tables(feat):
    bands = (feat - 5) // 4
    freq = np.linspace(1.0, TOP_FREQ, bands).astype(np.float32)
    grid = (np.float32(2.0) * np.arange(IMG_W, dtype=np.float32) / np.float32(IMG_W - 1) - np.float32(1.0)).astype(np.float32)
    phase = ((np.float32(math.pi) * grid)[:, None] * freq[None, :]).astype(np.float64)
    table = np.zeros((LANES, feat), np.float64)
    for axis in range(2):
        rows = slice(axis * IMG_W, (axis + 1) * IMG_W)
        table[rows, 3 + axis] = grid
        table[rows, 5 + axis * bands : 5 + (axis + 1) * bands] = np.sin(phase)
        table[rows, 5 + (2 + axis) * bands : 5 + (3 + axis) * bands] = np.cos(phase)
    for channel in range(3):
        table[COLOR + channel, channel] = 1.0
    centered = table - table.mean(axis=1, keepdims=True)
    gram = centered @ centered.T / feat
    place = np.arange(CELLS)
    row, col = place // IMG_W, IMG_W + place % IMG_W
    geometry = np.zeros((8, CELLS), np.float32)
    geometry[0] = gram[row, row] + gram[col, col] + 2.0 * gram[row, col]
    for channel in range(3):
        geometry[1 + channel] = gram[COLOR + channel, row] + gram[COLOR + channel, col]
    wide = -(-feat // LANES) * LANES
    padded = np.zeros((LANES, wide), np.float32)
    padded[:, :feat] = centered
    turned = np.zeros((wide + 8, LANES), np.float32)
    turned[:feat] = centered.T
    turned[wide, ONE] = 1.0
    high = turned.astype(jnp.bfloat16)
    low = (turned - high.astype(np.float32)).astype(jnp.bfloat16)
    colors = gram[COLOR : COLOR + 3, COLOR : COLOR + 3]
    return padded, geometry, np.concatenate([high, low], axis=1), [[float(v) for v in line] for line in colors]


def split(values):
    high = values.astype(BF16)
    return high, (values - high.astype(F32)).astype(BF16)


def dot_nn(left, right):
    return jnp.dot(left, right, preferred_element_type=F32)


def dot_nt(left, right):
    return lax.dot_general(left, right, (((1,), (1,)), ((), ())), preferred_element_type=F32)


def dot_tn(left, right):
    return lax.dot_general(left, right, (((0,), (0,)), ((), ())), preferred_element_type=F32)


def plan(n_batch, n_seq, width):
    core = 2
    fast = math.isqrt(n_seq // core)
    while (n_seq // core) % fast:
        fast -= 1
    slow = n_seq // core // fast
    sizes = {"z": n_batch, "a": slow, "b": fast, "c": core}
    parts, left = dict(sizes), width
    for name in ("c", "b", "a"):
        if width // math.prod(parts.values()) < 16:
            parts[name] = 1
    orders = (("b", "a") if parts["b"] > 1 else ("a", "b"), ("a", "b"))
    return sizes, parts, width // math.prod(parts.values()), orders


def shapes_of(n_batch, n_seq, width, pix_dev, n_img, feat):
    sizes, parts, rows, orders = plan(n_batch, n_seq, width)
    img = -(-n_img // 16) * 16
    blocks = pix_dev // LANES
    wide = -(-feat // LANES) * LANES
    factor_rows = (width // (2 * rows), 2, rows) if parts["c"] > 1 else (1, 1, width)
    S = SimpleNamespace()
    vm = lambda *shape, dtype=BF16: pltpu.VMEM(shape, dtype)
    S.wq, S.wo, S.wu, S.wd = [vm(width, width)] * 4
    S.tk = vm(3 * LANES, width)
    S.tv = vm(3 * LANES, width)
    S.ee = vm(2 * LANES, CELLS)
    S.mt = vm(LANES, wide, dtype=F32)
    S.xl, S.xm, S.res, S.ag = [vm(LANES, width, dtype=F32)] * 4
    S.rl = vm(LANES, LANES, dtype=F32)
    S.rm = vm(LANES, LANES, dtype=F32)
    S.nl, S.q, S.merged, S.nm, S.act, S.da = [vm(LANES, width)] * 6
    S.pb = vm(3, n_seq * blocks, LANES)
    S.sel = vm(9 * img, n_seq * blocks)
    S.xi = vm(3, img, CELLS)
    S.ri = vm(img, CELLS, dtype=F32)
    S.xx = vm(3, LANES, CELLS)
    S.rr = vm(LANES, CELLS, dtype=F32)
    S.ss = vm(LANES, CELLS, dtype=F32)
    S.pp = vm(LANES, CELLS, dtype=F32)
    S.low = vm(LANES, CELLS)
    S.dp = vm(2 * LANES, CELLS)
    S.ye = vm(LANES, CELLS)
    S.side = vm(LANES, LANES, dtype=F32)
    S.owner = vm(LANES, LANES, dtype=F32)
    S.pg = vm(9 * img, LANES, dtype=F32)
    S.pgs = vm(3, n_seq * blocks, LANES, dtype=F32)
    S.pgr = vm(n_seq - 1, 3, blocks, LANES, dtype=F32)
    S.at = vm(4, *factor_rows, 2 * LANES)
    S.bt = vm(4, 2 * LANES, width)
    S.zt = vm(2 * width, LANES)
    S.ms0 = vm(4, parts["z"], parts["a"], parts["b"], rows, width)
    S.zs0 = vm(1, parts["z"], parts["a"], parts["b"], 2 * rows, LANES)
    S.mr, S.zr = [], []
    for made, mats, across in ((S.mr, 4, width // 2), (S.zr, 1, LANES)):
        for first, other in orders:
            made.append([
                vm(mats, sizes[first] - 1, parts["z"], parts[other], rows, across),
                vm(mats, sizes[other] - 1, parts["z"], rows, across),
                vm(mats, sizes["z"] - 1, rows, across),
            ])
    S.zc = vm(parts["z"], parts["a"], parts["b"], parts["c"], 2 * rows, LANES)
    S.zcr = vm(parts["z"], parts["a"], parts["b"], 2 * rows, LANES)
    S.out = vm(4, rows, width, dtype=F32)
    S.zout = vm(2 * rows, LANES, dtype=F32)
    S.ar = vm(5, 8, width, dtype=F32)
    S.arr = [vm(sizes[name] - 1, 8, width, dtype=F32) for name in SMALL_ORDER]
    most = max(sizes.values()) - 1
    sem = lambda *shape: pltpu.SemaphoreType.DMA(shape)
    S.w_sem = sem(4)
    S.px_s, S.px_r = sem(n_seq - 1), sem(n_seq - 1)
    S.pg_s, S.pg_r = sem(n_seq - 1), sem(n_seq - 1)
    S.co_s, S.co_r = sem(9), sem(9)
    S.rs_s, S.rs_r = sem(5, 2, 3, most), sem(5, 2, 3, most)
    S.ar_s, S.ar_r = sem(4, most), sem(4, most)
    return S


def layer(
    n_batch, n_seq, width, n_img, feat, gram,
    lat, px, cnt, img_of, qgain, qshift, hwq, igain, ishift, kvw, hwo, mgain, mshift, hwu, hwd, cot, fc, geo, fct,
    o_mixed, o_lat, o_pix, o_vec, o_wq, o_in, o_kv, o_wo, o_wu, o_wd, r,
):
    r = SimpleNamespace(**r)
    sizes, parts, rows, orders = plan(n_batch, n_seq, width)
    img = r.xi.shape[1]
    blocks = px.shape[1]
    wide = r.mt.shape[1]
    span = CELLS + LANES
    scale = width ** (-0.5)

    z = lax.axis_index("batch")
    s = lax.axis_index("seq")
    c = lax.rem(s, 2)
    b = lax.rem(s // 2, sizes["b"])
    a = s // (2 * sizes["b"])
    here = {"z": z, "a": a, "b": b, "c": c}

    def device(**moved):
        at = {**here, **moved}
        return (at["z"], (at["a"] * sizes["b"] + at["b"]) * 2 + at["c"])

    def part(name, index):
        return index if parts[name] > 1 else 0

    def peer(name, offset):
        return lax.rem(here[name] + offset, sizes[name])

    barrier = pltpu.get_barrier_semaphore()
    for offset in range(1, n_seq):
        pl.semaphore_signal(barrier, inc=1, device_id=(z, lax.rem(s + offset, n_seq)), device_id_type=MESH)
    for offset in range(1, n_batch):
        pl.semaphore_signal(barrier, inc=1, device_id=(peer("z", offset), s), device_id_type=MESH)

    weights = []
    for i, (src, dst) in enumerate(((hwq, r.wq), (hwd, r.wd), (hwo, r.wo), (hwu, r.wu))):
        copy = pltpu.make_async_copy(src, dst, r.w_sem.at[i])
        copy.start()
        weights.append(copy)

    tile = 16

    def by_rows(step):
        def run(i, carry):
            step(pl.ds(pl.multiple_of(i * tile, tile), tile))
            return carry

        lax.fori_loop(0, LANES // tile, run, 0)

    mine = pl.ds(pl.multiple_of(c * LANES, LANES), LANES)

    def turn(which, factor):
        for j in range(width // LANES):
            block = factor[:, j * LANES : (j + 1) * LANES].astype(F32).T.astype(BF16)
            if parts["c"] > 1:
                deep = LANES // (2 * rows)
                r.at[which, j * deep : (j + 1) * deep, :, :, mine] = block.reshape(deep, 2, rows, LANES)
            else:
                r.at[which, 0, 0, j * LANES : (j + 1) * LANES, mine] = block

    core_copies = {}

    def to_core(key, index, src, dst):
        copy = pltpu.make_async_remote_copy(
            src_ref=src, dst_ref=dst, send_sem=r.co_s.at[index], recv_sem=r.co_r.at[index],
            device_id=device(c=1 - c), device_id_type=MESH,
        )
        copy.start()
        core_copies[key] = copy

    def send_left(which):
        ref = r.at.at[which, :, part("c", 1 - c), :, mine]
        to_core(("left", which), 2 * which, ref, ref)

    def send_right(which):
        ref = r.bt.at[which, mine, :]
        to_core(("right", which), 2 * which + 1, ref, ref)

    def norm_latents(at):
        x = lat[0, at, :].astype(F32)
        center = x - jnp.mean(x, axis=-1, keepdims=True)
        inv = lax.rsqrt(jnp.mean(center * center, axis=-1, keepdims=True) + TINY)
        hat = center * inv
        r.xl[at, :] = hat
        r.rl[at, :] = jnp.broadcast_to(inv, (tile, LANES))
        r.nl[at, :] = (hat * qgain[...] + qshift[...]).astype(BF16)

    by_rows(norm_latents)
    DOWN, UP, OUT, QUERY = 0, 1, 2, 3
    turn(QUERY, r.nl)
    r.bt[DOWN, mine, :] = cot[0]

    pl.semaphore_wait(barrier, n_seq - 1 + n_batch - 1)

    own = pl.ds(pl.multiple_of(s * blocks, blocks), blocks)
    pixel_copies = []
    for offset in range(1, n_seq):
        copy = pltpu.make_async_remote_copy(
            src_ref=px, dst_ref=r.pb.at[:, own, :],
            send_sem=r.px_s.at[offset - 1], recv_sem=r.px_r.at[n_seq - offset - 1],
            device_id=(z, lax.rem(s + offset, n_seq)), device_id_type=MESH,
        )
        copy.start()
        pixel_copies.append(copy)
    r.pb[:, own, :] = px[...]
    send_left(QUERY)
    send_right(DOWN)

    row_of = lax.broadcasted_iota(jnp.int32, (LANES, feat), 0)
    code = fc[:, :feat] * igain[...] + jnp.where(row_of == ONE, ishift[...], 0.0)
    r.mt[...] = jnp.zeros_like(r.mt)
    r.mt[:, :feat] = code
    code_high, code_low = split(code)
    code_both = jnp.concatenate([code_high, code_low], axis=0)
    for table, base in ((r.tk, 0), (r.tv, width)):
        for j in range(0, width, 256):
            both = dot_nn(code_both, kvw[:, base + j : base + j + 256])
            high, low = split(both[:LANES] + both[LANES:])
            table[:LANES, j : j + 256] = high
            table[LANES : 2 * LANES, j : j + 256] = low
            table[2 * LANES :, j : j + 256] = high
    cell = lax.broadcasted_iota(jnp.int32, (LANES, CELLS), 1)
    line = lax.broadcasted_iota(jnp.int32, (LANES, CELLS), 0)
    hit = (line == cell // IMG_W) | (line == IMG_W + lax.rem(cell, IMG_W))
    grid_code = jnp.where(hit, 1.0, 0.0).astype(BF16)
    r.ee[:LANES, :] = grid_code
    r.ee[LANES:, :] = grid_code

    weights[0].wait()
    for j in range(0, width, 256):
        r.q[:, j : j + 256] = dot_nn(r.nl[...], r.wq[:, j : j + 256]).astype(BF16)
    query_code = dot_nt(r.q[...], r.tk[: 2 * LANES, :])
    query_code = (query_code[:, :LANES] + query_code[:, LANES:]) * scale

    weights[1].wait()
    for j in range(0, width, 256):
        r.ag[:, j : j + 256] = dot_nt(cot[0], r.wd[j : j + 256, :])

    counts_row = cnt[...].astype(F32)
    number = lax.broadcasted_iota(jnp.int32, (img, n_img), 0)
    against = lax.broadcasted_iota(jnp.int32, (img, n_img), 1)
    counts_all = jnp.broadcast_to(counts_row, (img, n_img))
    first = jnp.sum(jnp.where(against < number, counts_all, 0.0), axis=1, keepdims=True).astype(jnp.int32)
    count = jnp.sum(jnp.where(against == number, counts_all, 0.0), axis=1, keepdims=True).astype(jnp.int32)
    block_of = first // LANES
    shift_of = lax.rem(first, LANES)
    block_id = lax.broadcasted_iota(jnp.int32, (img, n_seq * blocks), 1)
    for j in range(9):
        r.sel[j * img : (j + 1) * img, :] = jnp.where(block_id == block_of + j, 1.0, 0.0).astype(BF16)

    mine_lat = pl.ds(pl.multiple_of(s * LANES, LANES), LANES)
    owner_row = img_of[:, mine_lat].astype(F32)
    square0 = lax.broadcasted_iota(jnp.int32, (LANES, LANES), 0)
    square1 = lax.broadcasted_iota(jnp.int32, (LANES, LANES), 1)
    diagonal = square0 == square1
    owner = jnp.sum(jnp.where(diagonal, jnp.broadcast_to(owner_row, (LANES, LANES)), 0.0), axis=1, keepdims=True)
    owner_i = owner.astype(jnp.int32)
    pick = jnp.where(lax.broadcasted_iota(jnp.int32, (LANES, img), 1) == owner_i, 1.0, 0.0).astype(BF16)
    pick_t = jnp.where(
        lax.broadcasted_iota(jnp.int32, (img, LANES), 0) == owner_row.astype(jnp.int32), 1.0, 0.0
    )
    count_lat = jnp.sum(
        jnp.where(lax.broadcasted_iota(jnp.int32, (LANES, n_img), 1) == owner_i, jnp.broadcast_to(counts_row, (LANES, n_img)), 0.0),
        axis=1, keepdims=True,
    )
    r.owner[...] = jnp.broadcast_to(count_lat, (LANES, LANES))

    for copy in pixel_copies:
        copy.wait()

    inside = lax.broadcasted_iota(jnp.int32, (img, CELLS), 1) < count
    for channel in range(3):
        rows_of = dot_nn(r.sel[...], r.pb[channel])
        window = jnp.concatenate([rows_of[j * img : (j + 1) * img] for j in range(9)], axis=1)
        for bit in range(7):
            step = 1 << bit
            moved = pltpu.roll(window, span - step, 1)
            window = jnp.where((shift_of & step) != 0, moved, window)
        r.xi[channel] = jnp.where(inside, window[:, :CELLS], 0.0).astype(BF16)

    def gram_row(channel, x):
        base = geo[1 + channel : 2 + channel, :]
        return base, base + gram[channel][0] * x[0] + gram[channel][1] * x[1] + gram[channel][2] * x[2]

    for at in range(0, img, 16):
        x = [r.xi[channel, at : at + 16, :].astype(F32) for channel in range(3)]
        square = jnp.broadcast_to(geo[0:1, :], (16, CELLS))
        for channel in range(3):
            base, u = gram_row(channel, x)
            square = square + x[channel] * (base + u)
        r.ri[at : at + 16, :] = lax.rsqrt(square + TINY)
    for channel in range(3):
        r.xx[channel] = dot_nn(pick, r.xi[channel]).astype(BF16)
    inv_high, inv_low = split(r.ri[...])
    r.rr[...] = dot_nn(pick, inv_high) + dot_nn(pick, inv_low)

    def over_grid(code):
        return jnp.concatenate(split(code), axis=1)

    r.ss[...] = dot_nn(over_grid(query_code), r.ee[...])
    r.side[...] = query_code
    lane = lax.broadcasted_iota(jnp.int32, (tile, LANES), 1)
    place = lax.broadcasted_iota(jnp.int32, (tile, CELLS), 1).astype(F32)

    def side_columns(code, one, sums):
        made = jnp.where(lane == ONE, one, 0.0)
        for channel in range(3):
            made = made + jnp.where(lane == COLOR + channel, sums[channel], 0.0)
        return made

    def attend(at):
        code = r.side[at, :]
        x = [r.xx[channel, at, :].astype(F32) for channel in range(3)]
        inv = r.rr[at, :]
        raw = r.ss[at, :]
        for channel in range(3):
            raw = raw + code[:, COLOR + channel : COLOR + channel + 1] * x[channel]
        r.ss[at, :] = raw
        allowed = place < r.owner[at, :1]
        score = jnp.where(allowed, raw * inv + code[:, ONE : ONE + 1], FLOOR)
        top = jnp.max(score, axis=1, keepdims=True)
        raised = jnp.where(allowed, jnp.exp(score - top), 0.0)
        total = jnp.sum(raised, axis=1, keepdims=True)
        prob = raised / total
        r.pp[at, :] = prob
        weighted = prob * inv
        r.low[at, :] = weighted.astype(BF16)
        sums = [jnp.sum(weighted * x[channel], axis=1, keepdims=True) for channel in range(3)]
        r.side[at, :] = side_columns(code, jnp.sum(prob, axis=1, keepdims=True), sums)

    by_rows(attend)
    value_code = dot_nt(r.low[...], r.ee[:LANES, :]) + r.side[...]
    code_high, code_low = split(value_code)
    code_three = jnp.concatenate([code_high, code_high, code_low], axis=1)
    for j in range(0, width, 256):
        r.merged[:, j : j + 256] = dot_nn(code_three, r.tv[:, j : j + 256]).astype(BF16)
    value_code_low = code_high

    weights[2].wait()
    for j in range(0, width, 256):
        r.res[:, j : j + 256] = lat[0, :, j : j + 256].astype(F32) + dot_nn(r.merged[...], r.wo[:, j : j + 256])

    def norm_mid(at):
        x = r.res[at, :]
        center = x - jnp.mean(x, axis=-1, keepdims=True)
        inv = lax.rsqrt(jnp.mean(center * center, axis=-1, keepdims=True) + TINY)
        hat = center * inv
        r.xm[at, :] = hat
        r.rm[at, :] = jnp.broadcast_to(inv, (tile, LANES))
        r.nm[at, :] = (hat * mgain[...] + mshift[...]).astype(BF16)

    by_rows(norm_mid)
    weights[3].wait()
    for j in range(0, width, 256):
        pre = dot_nn(r.nm[...], r.wu[:, j : j + 256])
        phi = 0.5 * (1.0 + lax.erf(pre * math.sqrt(0.5)))
        r.act[:, j : j + 256] = (pre * phi).astype(BF16)
        slope = phi + pre * (jnp.exp(-0.5 * pre * pre) * (1.0 / math.sqrt(2.0 * math.pi)))
        r.bt[UP, mine, j : j + 256] = (r.ag[:, j : j + 256] * slope).astype(BF16)
    turn(DOWN, r.act)
    send_left(DOWN)
    turn(UP, r.nm)
    send_left(UP)
    send_right(UP)
    turn(OUT, r.merged)
    send_left(OUT)

    for j in range(0, width, 256):
        o_mixed[0, :, j : j + 256] = (r.res[:, j : j + 256] + dot_nn(r.act[...], r.wd[:, j : j + 256])).astype(BF16)
    for j in range(0, width, 256):
        r.ag[:, j : j + 256] = dot_nt(r.bt[UP, mine, :], r.wu[j : j + 256, :])
    r.ar[0] = jnp.zeros_like(r.ar[0])
    zero = jnp.zeros((1, width), F32)

    def norm_back(grad, hat, inv, gain):
        scaled = grad * gain
        return inv * (scaled - jnp.mean(scaled, axis=-1, keepdims=True) - hat * jnp.mean(scaled * hat, axis=-1, keepdims=True))

    def mid_back(i, carry):
        at = pl.ds(pl.multiple_of(i * tile, tile), tile)
        grad, hat = r.ag[at, :], r.xm[at, :]
        total = cot[0, at, :].astype(F32) + norm_back(grad, hat, r.rm[at, :1], mgain[...])
        r.res[at, :] = total
        r.bt[OUT, pl.ds(pl.multiple_of(c * LANES + i * tile, tile), tile), :] = total.astype(BF16)
        return carry[0] + jnp.sum(grad * hat, axis=0, keepdims=True), carry[1] + jnp.sum(grad, axis=0, keepdims=True)

    gain_sum, shift_sum = lax.fori_loop(0, LANES // tile, mid_back, (zero, zero))
    r.ar[0, 2:3, :] = gain_sum
    r.ar[0, 3:4, :] = shift_sum
    send_right(OUT)
    for j in range(0, width, 256):
        r.da[:, j : j + 256] = dot_nt(r.bt[OUT, mine, :], r.wo[j : j + 256, :]).astype(BF16)

    back_code = dot_nt(r.da[...], r.tv[: 2 * LANES, :])
    back_code = back_code[:, :LANES] + back_code[:, LANES:]
    r.ag[...] = dot_nn(over_grid(back_code), r.ee[...])
    r.side[...] = back_code

    def attend_back(at):
        code = r.side[at, :]
        x = [r.xx[channel, at, :].astype(F32) for channel in range(3)]
        inv = r.rr[at, :]
        prob = r.pp[at, :]
        raw = r.ag[at, :]
        for channel in range(3):
            raw = raw + code[:, COLOR + channel : COLOR + channel + 1] * x[channel]
        grad = raw * inv + code[:, ONE : ONE + 1]
        delta = jnp.sum(prob * grad, axis=1, keepdims=True)
        back = prob * (grad - delta)
        r.ye[at, :] = (back * r.ss[at, :] + prob * raw).astype(BF16)
        weighted = back * inv
        r.low[at, :] = weighted.astype(BF16)
        r.dp[at, :] = back.astype(BF16)
        sums = [jnp.sum(weighted * x[channel], axis=1, keepdims=True) for channel in range(3)]
        r.side[at, :] = side_columns(code, jnp.sum(back, axis=1, keepdims=True), sums)

    by_rows(attend_back)
    r.dp[LANES:, :] = r.pp[...].astype(BF16)
    key_code = (dot_nt(r.low[...], r.ee[:LANES, :]) + r.side[...]) * scale
    code_high, code_low = split(key_code)
    code_three = jnp.concatenate([code_high, code_high, code_low], axis=1)
    for j in range(0, width, 256):
        r.bt[QUERY, mine, j : j + 256] = dot_nn(code_three, r.tk[:, j : j + 256]).astype(BF16)
    send_right(QUERY)

    for j in range(0, width, 256):
        r.zt[j : j + 256, :] = dot_tn(r.q[:, j : j + 256], code_high).astype(BF16)
        r.zt[width + j : width + j + 256, :] = dot_tn(r.da[:, j : j + 256], value_code_low).astype(BF16)
    r.zc[...] = r.zt[...].reshape(r.zc.shape)
    if parts["c"] > 1:
        to_core("z", 8, r.zc.at[:, :, :, 1 - c], r.zcr)
    else:
        to_core("z", 8, r.zc.at[:, :, :, 0], r.zcr)

    query_t, back_t = query_code.T, back_code.T
    lifted = jnp.concatenate(
        [
            jnp.concatenate([pick_t * code_t[COLOR + channel : COLOR + channel + 1, :] for code_t in (query_t, back_t)], axis=1)
            for channel in range(3)
        ],
        axis=0,
    ).astype(BF16)
    along = dot_nn(pick_t.astype(BF16), r.ye[...])
    inv = r.ri[...]
    cube = inv * inv * inv * along
    colors = [r.xi[channel].astype(F32) for channel in range(3)]
    for channel in range(3):
        steep = dot_nn(lifted[channel * img : (channel + 1) * img], r.dp[...])
        own_grad = inv * steep - cube * gram_row(channel, colors)[1]
        window = jnp.concatenate([own_grad, jnp.zeros((img, LANES), F32)], axis=1)
        for bit in range(7):
            step = 1 << bit
            moved = pltpu.roll(window, step, 1)
            window = jnp.where((shift_of & step) != 0, moved, window)
        for j in range(9):
            r.pg[j * img : (j + 1) * img, :] = window[:, j * LANES : (j + 1) * LANES]
        grad_high, grad_low = split(r.pg[...])
        r.pgs[channel] = dot_tn(r.sel[...], grad_high) + dot_tn(r.sel[...], grad_low)
    grad_copies = []
    for offset in range(1, n_seq):
        target = lax.rem(s + offset, n_seq)
        copy = pltpu.make_async_remote_copy(
            src_ref=r.pgs.at[:, pl.ds(pl.multiple_of(target * blocks, blocks), blocks), :],
            dst_ref=r.pgr.at[n_seq - offset - 1],
            send_sem=r.pg_s.at[offset - 1], recv_sem=r.pg_r.at[n_seq - offset - 1],
            device_id=(z, target), device_id_type=MESH,
        )
        copy.start()
        grad_copies.append(copy)

    in_gain, in_shift = jnp.zeros((feat, 1), F32), jnp.zeros((feat, 1), F32)
    for j in range(0, 2 * width, 256):
        sums = r.zt[j : j + 256, :]
        spread = dot_nt(fct[...], jnp.concatenate([sums, sums], axis=1))
        factor = kvw[:, j : j + 256].astype(F32)
        in_gain = in_gain + jnp.sum(factor * spread[:feat], axis=1, keepdims=True)
        in_shift = in_shift + jnp.sum(factor * spread[wide : wide + 1], axis=1, keepdims=True)
    for at, column in ((4, in_gain), (5, in_shift)):
        for j in range(0, feat, LANES):
            tall = min(LANES, feat - j)
            eye = lax.broadcasted_iota(jnp.int32, (tall, LANES), 0) == lax.broadcasted_iota(jnp.int32, (tall, LANES), 1)
            r.ar[0, at : at + 1, j : j + LANES] = jnp.sum(jnp.where(eye, column[j : j + tall], 0.0), axis=0, keepdims=True)

    for j in range(0, width, 256):
        r.ag[:, j : j + 256] = dot_nt(r.bt[QUERY, mine, :], r.wq[j : j + 256, :])

    def latents_back(i, carry):
        at = pl.ds(pl.multiple_of(i * tile, tile), tile)
        grad, hat = r.ag[at, :], r.xl[at, :]
        o_lat[0, at, :] = r.res[at, :] + norm_back(grad, hat, r.rl[at, :1], qgain[...])
        return carry[0] + jnp.sum(grad * hat, axis=0, keepdims=True), carry[1] + jnp.sum(grad, axis=0, keepdims=True)

    gain_sum, shift_sum = lax.fori_loop(0, LANES // tile, latents_back, (zero, zero))
    r.ar[0, 0:1, :] = gain_sum
    r.ar[0, 1:2, :] = shift_sum

    def start_stage(key, stage, name, src_of, dst):
        mat, half = key
        copies = []
        for offset in range(1, sizes[name]):
            target = peer(name, offset)
            slot = sizes[name] - offset - 1
            copy = pltpu.make_async_remote_copy(
                src_ref=src_of(part(name, target)), dst_ref=dst.at[slot],
                send_sem=r.rs_s.at[mat, half, stage, offset - 1], recv_sem=r.rs_r.at[mat, half, stage, slot],
                device_id=device(**{name: target}), device_id_type=MESH,
            )
            copy.start()
            copies.append(copy)
        return copies

    def wait_all(copies):
        for copy in copies:
            copy.wait()

    def gathered(own, dst, n):
        total = own.astype(F32)
        for slot in range(n - 1):
            total = total + dst[slot].astype(F32)
        return total

    flying = {}

    def buffers_of(mat):
        return (r.zs0, r.zr, 0) if mat == 4 else (r.ms0, r.mr, mat)

    def cut(mat, half):
        if mat == 4:
            return pl.ds(half * rows, rows), slice(None)
        return slice(None), pl.ds(half * (width // 2), width // 2)

    def blocks_at(mat, half, stage, target=None):
        s0, received, i = buffers_of(mat)
        at = {"z": slice(None), "a": slice(None), "b": slice(None)}
        path = orders[half] + ("z",)
        for done in path[:stage]:
            at[done] = part(done, here[done])
        at[path[stage]] = part(path[stage], here[path[stage]]) if target is None else target
        return (i, at["z"], at["a"], at["b"]) + cut(mat, half)

    def start(mat, stage):
        s0, received, i = buffers_of(mat)
        for half in range(2):
            name = (orders[half] + ("z",))[stage]
            flying[mat, half] = start_stage(
                (mat, half), stage, name,
                lambda p: s0.at[blocks_at(mat, half, stage, p)],
                received[half][stage].at[i],
            )

    def step(mat, stage):
        s0, received, i = buffers_of(mat)
        for half in range(2):
            wait_all(flying[mat, half])
            name = (orders[half] + ("z",))[stage]
            keep = blocks_at(mat, half, stage)
            total = gathered(s0[keep], received[half][stage].at[i], sizes[name])
            if stage < 2:
                s0[keep] = total.astype(BF16)
            elif mat == 4:
                r.zout[cut(mat, half)] = total
            else:
                r.out[(mat,) + cut(mat, half)] = total
        if stage < 2:
            start(mat, stage + 1)

    def product(mat):
        core_copies.pop(("left", mat)).wait()
        core_copies.pop(("right", mat)).wait()
        left = r.at[mat, :, part("c", c)].reshape(-1, 2 * LANES)
        for j in range(0, width, 256):
            made = dot_nn(left, r.bt[mat, :, j : j + 256]).astype(BF16)
            r.ms0[mat, :, :, :, :, j : j + 256] = made.reshape(parts["z"], parts["a"], parts["b"], rows, 256)

    for mat in range(4):
        product(mat)
        start(mat, 0)
    core_copies.pop("z").wait()
    r.zs0[0] = (r.zc[:, :, :, part("c", c)].astype(F32) + r.zcr[...].astype(F32)).astype(BF16)
    start(4, 0)

    small = {}

    def small_start(stage):
        name = SMALL_ORDER[stage]
        copies = []
        for offset in range(1, sizes[name]):
            slot = sizes[name] - offset - 1
            copy = pltpu.make_async_remote_copy(
                src_ref=r.ar.at[stage], dst_ref=r.arr[stage].at[slot],
                send_sem=r.ar_s.at[stage, offset - 1], recv_sem=r.ar_r.at[stage, slot],
                device_id=device(**{name: peer(name, offset)}), device_id_type=MESH,
            )
            copy.start()
            copies.append(copy)
        small[stage] = copies

    def small_end(stage):
        name = SMALL_ORDER[stage]
        wait_all(small[stage])
        total = r.ar[stage]
        for slot in range(sizes[name] - 1):
            total = total + r.arr[stage][slot]
        r.ar[stage + 1] = total

    small_start(0)
    small_end(0)
    small_start(1)
    step(0, 0)
    small_end(1)
    small_start(2)
    step(1, 0)
    small_end(2)
    small_start(3)
    step(0, 1)
    step(2, 0)
    step(1, 1)
    step(3, 0)
    step(2, 1)
    step(4, 0)
    small_end(3)
    for copy in grad_copies:
        copy.wait()
    pixel = r.pgs[:, own, :]
    for slot in range(n_seq - 1):
        pixel = pixel + r.pgr[slot]
    for channel in range(3):
        for j in range(blocks):
            o_pix[0, channel : channel + 1, j * LANES : (j + 1) * LANES] = pixel[channel, j : j + 1, :]
    step(0, 2)
    step(1, 2)
    step(3, 1)
    step(4, 1)
    step(2, 2)
    step(3, 2)
    step(4, 2)

    total_rows = width // (n_batch * n_seq)
    inner = 0
    for name in ("a", "b", "c"):
        if parts[name] < sizes[name]:
            inner = inner * sizes[name] + here[name]
    for mat, made in enumerate((o_wd, o_wu, o_wo, o_wq)):
        if total_rows == rows:
            made[...] = r.out[mat]
        else:
            made[...] = pltpu.roll(r.out[mat], lax.rem(rows - inner * total_rows, rows), 0)[:total_rows]
    index = z * n_seq + s
    turned = pltpu.roll(r.ar[4], lax.rem(width - index * total_rows, width), 1)
    o_vec[...] = turned[:4, :total_rows]
    o_in[...] = r.ar[4, 4:6, :feat]
    code_high, code_low = split(r.mt[...].T)
    spread_left = jnp.concatenate([code_high, code_high, code_low], axis=1)
    if total_rows == rows:
        sums = r.zout[...]
    else:
        sums = pltpu.roll(r.zout[...], lax.rem(2 * (rows - inner * total_rows), 2 * rows), 0)[: 2 * total_rows]
    high, low = split(sums)
    o_kv[...] = dot_nt(spread_left, jnp.concatenate([high, low, high], axis=1))[:feat]


def solution(mesh):
    n_batch, n_seq = mesh.shape["batch"], mesh.shape["seq"]

    def body(latents, pixels, counts, latent_image, query_gain, query_shift, query_weight, input_gain, input_shift,
             kv_weight, out_weight, mlp_gain, mlp_shift, up_weight, down_weight, cotangent):
        width = query_weight.shape[0]
        feat = kv_weight.shape[0]
        pix_dev = pixels.shape[2]
        n_img = counts.shape[1]
        fc, geo, fct, gram = position_tables(feat)
        scratch = shapes_of(n_batch, n_seq, width, pix_dev, n_img, feat)
        rows = width // (n_batch * n_seq)
        vm = pl.BlockSpec(memory_space=pltpu.VMEM)
        hbm = pl.BlockSpec(memory_space=pl.ANY)
        out_shape = (
            jax.ShapeDtypeStruct(latents.shape, BF16),
            jax.ShapeDtypeStruct(latents.shape, F32),
            jax.ShapeDtypeStruct(pixels.shape, F32),
            jax.ShapeDtypeStruct((4, rows), F32),
            jax.ShapeDtypeStruct((rows, width), F32),
            jax.ShapeDtypeStruct((2, feat), F32),
            jax.ShapeDtypeStruct((feat, 2 * rows), F32),
            jax.ShapeDtypeStruct((rows, width), F32),
            jax.ShapeDtypeStruct((rows, width), F32),
            jax.ShapeDtypeStruct((rows, width), F32),
        )
        args = (
            latents, pixels.reshape(3, pix_dev // LANES, LANES), counts, latent_image,
            query_gain[None], query_shift[None], query_weight, input_gain[None], input_shift[None], kv_weight,
            out_weight, mlp_gain[None], mlp_shift[None], up_weight, down_weight, cotangent,
            jnp.asarray(fc), jnp.asarray(geo), jnp.asarray(fct),
        )
        made = pl.pallas_call(
            functools.partial(layer, n_batch, n_seq, width, n_img, feat, gram),
            out_shape=out_shape,
            in_specs=[hbm if getattr(arg, "shape", ()) == (width, width) else vm for arg in args],
            out_specs=[vm] * len(out_shape),
            scratch_shapes=[vars(scratch)],
            compiler_params=pltpu.CompilerParams(
                collective_id=0, has_side_effects=True, vmem_limit_bytes=60 * 1024 * 1024
            ),
            name="layer",
        )(*args)
        mixed, latent_grad, pixel_grad, vectors, wq, inner, kv, wo, wu, wd = made
        return (
            mixed, latent_grad, pixel_grad, vectors[0], vectors[1], wq, inner[0], inner[1], kv, wo,
            vectors[2], vectors[3], wu, wd,
        )

    whole, vec = P(("batch", "seq"), None), P(("batch", "seq"))
    rowed = P("batch", "seq", None)
    return jax.shard_map(
        body,
        mesh=mesh,
        in_specs=(rowed, P("batch", None, "seq"), P("batch", None), P("batch", None)) + (P(),) * 11 + (rowed,),
        out_specs=(
            rowed, rowed, P("batch", None, "seq"), vec, vec, whole, P(), P(), P(None, ("batch", "seq")), whole,
            vec, vec, whole, whole,
        ),
        check_vma=False,
    )
```

```python
import functools
import math
from types import SimpleNamespace

import jax
import jax.numpy as jnp
import numpy as np
from jax import lax
from jax.experimental import pallas as pl
from jax.experimental.pallas import tpu as pltpu
from jax.sharding import PartitionSpec as P

IMG_W = 32
TOP_FREQ = 112.0
TINY = 1e-05
FLOOR = -1e30
MESH = pl.DeviceIdType.MESH
F32 = jnp.float32
BF16 = jnp.bfloat16
LANES = 128
CELLS = IMG_W * IMG_W
COLOR = 2 * IMG_W
ONE = COLOR + 3


def position_tables(feat):
    bands = (feat - 5) // 4
    freq = np.linspace(1.0, TOP_FREQ, bands).astype(np.float32)
    grid = (np.float32(2.0) * np.arange(IMG_W, dtype=np.float32) / np.float32(IMG_W - 1) - np.float32(1.0)).astype(np.float32)
    phase = ((np.float32(math.pi) * grid)[:, None] * freq[None, :]).astype(np.float64)
    table = np.zeros((LANES, feat), np.float64)
    for axis in range(2):
        rows = slice(axis * IMG_W, (axis + 1) * IMG_W)
        table[rows, 3 + axis] = grid
        table[rows, 5 + axis * bands : 5 + (axis + 1) * bands] = np.sin(phase)
        table[rows, 5 + (2 + axis) * bands : 5 + (3 + axis) * bands] = np.cos(phase)
    for channel in range(3):
        table[COLOR + channel, channel] = 1.0
    centered = table - table.mean(axis=1, keepdims=True)
    gram = centered @ centered.T / feat
    place = np.arange(CELLS)
    row, col = place // IMG_W, IMG_W + place % IMG_W
    geometry = np.zeros((8, CELLS), np.float32)
    geometry[0] = gram[row, row] + gram[col, col] + 2.0 * gram[row, col]
    for channel in range(3):
        geometry[1 + channel] = gram[COLOR + channel, row] + gram[COLOR + channel, col]
    wide = -(-feat // LANES) * LANES
    padded = np.zeros((LANES, wide), np.float32)
    padded[:, :feat] = centered
    turned = np.zeros((wide + 8, LANES), np.float32)
    turned[:feat] = centered.T
    turned[wide, ONE] = 1.0
    high = turned.astype(jnp.bfloat16)
    low = (turned - high.astype(np.float32)).astype(jnp.bfloat16)
    colors = gram[COLOR : COLOR + 3, COLOR : COLOR + 3]
    return padded, geometry, np.concatenate([high, low], axis=1), [[float(v) for v in line] for line in colors]


def split(values):
    high = values.astype(BF16)
    return high, (values - high.astype(F32)).astype(BF16)


def dot_nn(left, right):
    return jnp.dot(left, right, preferred_element_type=F32)


def dot_nt(left, right):
    return lax.dot_general(left, right, (((1,), (1,)), ((), ())), preferred_element_type=F32)


def dot_tn(left, right):
    return lax.dot_general(left, right, (((0,), (0,)), ((), ())), preferred_element_type=F32)


def plan(n_batch, n_seq, width):
    core = 2
    fast = math.isqrt(n_seq // core)
    while (n_seq // core) % fast:
        fast -= 1
    slow = n_seq // core // fast
    sizes = {"z": n_batch, "a": slow, "b": fast, "c": core}
    parts, left = dict(sizes), width
    for name in ("c", "b", "a"):
        if width // math.prod(parts.values()) < 16:
            parts[name] = 1
    orders = (("b", "a") if parts["b"] > 1 else ("a", "b"), ("a", "b"))
    return sizes, parts, width // math.prod(parts.values()), orders


def shapes_of(n_batch, n_seq, width, pix_dev, n_img, feat):
    sizes, parts, rows, orders = plan(n_batch, n_seq, width)
    img = -(-n_img // 16) * 16
    blocks = pix_dev // LANES
    wide = -(-feat // LANES) * LANES
    factor_rows = (width // (2 * rows), 2, rows) if parts["c"] > 1 else (1, 1, width)
    S = SimpleNamespace()
    vm = lambda *shape, dtype=BF16: pltpu.VMEM(shape, dtype)
    S.wq, S.wo, S.wu, S.wd = [vm(width, width)] * 4
    S.tk = vm(3 * LANES, width)
    S.tv = vm(3 * LANES, width)
    S.ee = vm(2 * LANES, CELLS)
    S.mt = vm(LANES, wide, dtype=F32)
    S.xl, S.xm, S.res, S.ag = [vm(LANES, width, dtype=F32)] * 4
    S.rl = vm(LANES, LANES, dtype=F32)
    S.rm = vm(LANES, LANES, dtype=F32)
    S.nl, S.q, S.merged, S.nm, S.act, S.da = [vm(LANES, width)] * 6
    S.pb = vm(3, n_seq * blocks, LANES)
    S.sel = vm(9 * img, n_seq * blocks)
    S.xi = vm(3, img, CELLS)
    S.ri = vm(img, CELLS, dtype=F32)
    S.xx = vm(3, LANES, CELLS)
    S.rr = vm(LANES, CELLS, dtype=F32)
    S.ss = vm(LANES, CELLS, dtype=F32)
    S.pp = vm(LANES, CELLS, dtype=F32)
    S.low = vm(LANES, CELLS)
    S.dp = vm(2 * LANES, CELLS)
    S.ye = vm(LANES, CELLS)
    S.side = vm(LANES, LANES, dtype=F32)
    S.owner = vm(LANES, LANES, dtype=F32)
    S.pg = vm(9 * img, LANES, dtype=F32)
    S.pgs = vm(3, n_seq * blocks, LANES, dtype=F32)
    S.pgr = vm(n_seq - 1, 3, blocks, LANES, dtype=F32)
    S.at = vm(4, *factor_rows, 2 * LANES)
    S.bt = vm(4, 2 * LANES, width)
    S.ms0 = vm(4, parts["z"], parts["a"], parts["b"], rows, width)
    S.zs0 = vm(1, parts["z"], parts["a"], parts["b"], 2 * rows, LANES)
    S.mr, S.zr = [], []
    for made, mats, across in ((S.mr, 4, width // 2), (S.zr, 1, LANES)):
        for first, other in orders:
            made.append([
                vm(mats, sizes[first] - 1, parts["z"], parts[other], rows, across),
                vm(mats, sizes[other] - 1, parts["z"], rows, across),
                vm(mats, sizes["z"] - 1, rows, across),
            ])
    S.zc = vm(width // (rows * parts["c"]), parts["c"], 2 * rows, LANES)
    S.zcr = vm(width // (rows * parts["c"]), 2 * rows, LANES)
    S.vec = vm(LANES, width, dtype=F32)
    S.out = vm(4, rows, width, dtype=F32)
    S.zout = vm(2 * rows, LANES, dtype=F32)
    S.ar = vm(2, 2, wide, dtype=F32)
    S.ars = vm(n_seq - 1, 2, wide, dtype=F32)
    S.arz = vm(n_batch - 1, 2, wide, dtype=F32)
    S.lat, S.cot = [vm(LANES, width)] * 2
    S.kvw = vm(feat, 2 * width)
    S.fc = vm(LANES, wide, dtype=F32)
    S.fct = vm(wide + 8, 2 * LANES)
    most = max(sizes.values()) - 1
    sem = lambda *shape: pltpu.SemaphoreType.DMA(shape)
    S.w_sem = sem(9)
    S.o_sem = sem(6)
    S.px_s, S.px_r = sem(n_seq - 1), sem(n_seq - 1)
    S.pg_s, S.pg_r = sem(n_seq - 1), sem(n_seq - 1)
    S.co_s, S.co_r = sem(9), sem(9)
    S.rs_s, S.rs_r = sem(5, 2, 3, most), sem(5, 2, 3, most)
    S.as_s, S.as_r = sem(n_seq - 1), sem(n_seq - 1)
    S.az_s, S.az_r = sem(n_batch - 1), sem(n_batch - 1)
    return S


def layer(
    n_batch, n_seq, width, n_img, feat, gram,
    h_lat, px, cnt, img_of, qgain, qshift, h_wq, igain, ishift, h_kvw, h_wo, mgain, mshift, h_wu, h_wd, h_cot, h_fc, geo, h_fct,
    o_mixed, o_lat, o_pix, o_vec, o_wq, o_in, o_kv, o_wo, o_wu, o_wd, r,
):
    r = SimpleNamespace(**r)
    sizes, parts, rows, orders = plan(n_batch, n_seq, width)
    img = r.xi.shape[1]
    blocks = px.shape[2] // LANES
    wide = r.mt.shape[1]
    span = CELLS + LANES
    scale = width ** (-0.5)

    z = lax.axis_index("batch")
    s = lax.axis_index("seq")
    c = lax.rem(s, 2)
    b = lax.rem(s // 2, sizes["b"])
    a = s // (2 * sizes["b"])
    here = {"z": z, "a": a, "b": b, "c": c}

    def device(**moved):
        at = {**here, **moved}
        return (at["z"], (at["a"] * sizes["b"] + at["b"]) * 2 + at["c"])

    def part(name, index):
        return index if parts[name] > 1 else 0

    def peer(name, offset):
        return lax.rem(here[name] + offset, sizes[name])

    barrier = pltpu.get_barrier_semaphore()
    for offset in range(1, n_seq):
        pl.semaphore_signal(barrier, inc=1, device_id=(z, lax.rem(s + offset, n_seq)), device_id_type=MESH)
    for offset in range(1, n_batch):
        pl.semaphore_signal(barrier, inc=1, device_id=(peer("z", offset), s), device_id_type=MESH)

    arriving = []
    for i, (src, dst) in enumerate((
        (h_lat.at[0], r.lat), (h_fc, r.fc), (h_kvw, r.kvw), (h_wq, r.wq), (h_cot.at[0], r.cot), (h_wd, r.wd),
        (h_wo, r.wo), (h_wu, r.wu), (h_fct, r.fct),
    )):
        copy = pltpu.make_async_copy(src, dst, r.w_sem.at[i])
        copy.start()
        arriving.append(copy)
    LAT, FC, KVW, WQ, COT, WD, WO, WU, FCT = arriving
    leaving = []

    def leave(src, dst):
        copy = pltpu.make_async_copy(src, dst, r.o_sem.at[len(leaving)])
        copy.start()
        leaving.append(copy)

    tile = 16

    def by_rows(step):
        def run(i, carry):
            step(pl.ds(pl.multiple_of(i * tile, tile), tile))
            return carry

        lax.fori_loop(0, LANES // tile, run, 0)

    mine = pl.ds(pl.multiple_of(c * LANES, LANES), LANES)

    def turn(which, factor):
        for j in range(width // LANES):
            block = factor[:, j * LANES : (j + 1) * LANES].astype(F32).T.astype(BF16)
            if parts["c"] > 1:
                deep = LANES // (2 * rows)
                r.at[which, j * deep : (j + 1) * deep, :, :, mine] = block.reshape(deep, 2, rows, LANES)
            else:
                r.at[which, 0, 0, j * LANES : (j + 1) * LANES, mine] = block

    core_copies = {}

    def to_core(key, index, src, dst):
        copy = pltpu.make_async_remote_copy(
            src_ref=src, dst_ref=dst, send_sem=r.co_s.at[index], recv_sem=r.co_r.at[index],
            device_id=device(c=1 - c), device_id_type=MESH,
        )
        copy.start()
        core_copies[key] = copy

    def send_left(which):
        ref = r.at.at[which, :, part("c", 1 - c), :, mine]
        to_core(("left", which), 2 * which, ref, ref)

    def send_right(which):
        ref = r.bt.at[which, mine, :]
        to_core(("right", which), 2 * which + 1, ref, ref)

    def start_stage(key, stage, name, src_of, dst):
        mat, half = key
        copies = []
        for offset in range(1, sizes[name]):
            target = peer(name, offset)
            slot = sizes[name] - offset - 1
            copy = pltpu.make_async_remote_copy(
                src_ref=src_of(part(name, target)), dst_ref=dst.at[slot],
                send_sem=r.rs_s.at[mat, half, stage, offset - 1], recv_sem=r.rs_r.at[mat, half, stage, slot],
                device_id=device(**{name: target}), device_id_type=MESH,
            )
            copy.start()
            copies.append(copy)
        return copies

    def wait_all(copies):
        for copy in copies:
            copy.wait()

    def gathered(own, dst, n):
        total = own.astype(F32)
        for slot in range(n - 1):
            total = total + dst[slot].astype(F32)
        return total

    flying = {}

    def buffers_of(mat):
        return (r.zs0, r.zr, 0) if mat == 4 else (r.ms0, r.mr, mat)

    def cut(mat, half):
        if mat == 4:
            return pl.ds(half * rows, rows), slice(None)
        return slice(None), pl.ds(half * (width // 2), width // 2)

    def blocks_at(mat, half, stage, target=None):
        s0, received, i = buffers_of(mat)
        at = {"z": slice(None), "a": slice(None), "b": slice(None)}
        path = orders[half] + ("z",)
        for done in path[:stage]:
            at[done] = part(done, here[done])
        at[path[stage]] = part(path[stage], here[path[stage]]) if target is None else target
        return (i, at["z"], at["a"], at["b"]) + cut(mat, half)

    def start(mat, stage):
        s0, received, i = buffers_of(mat)
        for half in range(2):
            name = (orders[half] + ("z",))[stage]
            flying[mat, half] = start_stage(
                (mat, half), stage, name,
                lambda p: s0.at[blocks_at(mat, half, stage, p)],
                received[half][stage].at[i],
            )

    def step(mat, stage):
        s0, received, i = buffers_of(mat)
        for half in range(2):
            wait_all(flying[mat, half])
            name = (orders[half] + ("z",))[stage]
            keep = blocks_at(mat, half, stage)
            total = gathered(s0[keep], received[half][stage].at[i], sizes[name])
            if stage < 2:
                s0[keep] = total.astype(BF16)
            elif mat == 4:
                r.zout[cut(mat, half)] = total
            else:
                r.out[(mat,) + cut(mat, half)] = total
        if stage < 2:
            start(mat, stage + 1)

    def product(mat):
        core_copies.pop(("left", mat)).wait()
        core_copies.pop(("right", mat)).wait()
        left = r.at[mat, :, part("c", c)].reshape(-1, 2 * LANES)
        for j in range(0, width, 256):
            made = dot_nn(left, r.bt[mat, :, j : j + 256]).astype(BF16)
            r.ms0[mat, :, :, :, :, j : j + 256] = made.reshape(parts["z"], parts["a"], parts["b"], rows, 256)

    def norm_latents(at):
        x = r.lat[at, :].astype(F32)
        center = x - jnp.mean(x, axis=-1, keepdims=True)
        inv = lax.rsqrt(jnp.mean(center * center, axis=-1, keepdims=True) + TINY)
        hat = center * inv
        r.xl[at, :] = hat
        r.rl[at, :] = jnp.broadcast_to(inv, (tile, LANES))
        r.nl[at, :] = (hat * qgain[...] + qshift[...]).astype(BF16)

    LAT.wait()
    DOWN, UP, OUT, QUERY, SUMS = range(5)
    by_rows(norm_latents)
    turn(QUERY, r.nl)
    COT.wait()
    r.bt[DOWN, mine, :] = r.cot[...]

    own = pl.ds(pl.multiple_of(s * blocks, blocks), blocks)
    colors = px[0].astype(F32)
    for channel in range(3):
        line = colors[channel : channel + 1]
        stacked = jnp.concatenate([line[:, j * LANES : (j + 1) * LANES] for j in range(blocks)], axis=0)
        r.pb[channel, own, :] = stacked.astype(BF16)
    pl.semaphore_wait(barrier, n_seq - 1 + n_batch - 1)
    pixel_copies = []
    for offset in range(1, n_seq):
        copy = pltpu.make_async_remote_copy(
            src_ref=r.pb.at[:, own, :], dst_ref=r.pb.at[:, own, :],
            send_sem=r.px_s.at[offset - 1], recv_sem=r.px_r.at[n_seq - offset - 1],
            device_id=(z, lax.rem(s + offset, n_seq)), device_id_type=MESH,
        )
        copy.start()
        pixel_copies.append(copy)
    send_left(QUERY)
    send_right(DOWN)

    FCT.wait()
    FC.wait()
    KVW.wait()
    row_of = lax.broadcasted_iota(jnp.int32, (LANES, feat), 0)
    code = r.fc[:, :feat] * igain[...][None] + jnp.where(row_of == ONE, ishift[...][None], 0.0)
    r.mt[...] = jnp.zeros_like(r.mt)
    r.mt[:, :feat] = code
    code_high, code_low = split(code)
    code_both = jnp.concatenate([code_high, code_low], axis=0)
    for table, base in ((r.tk, 0), (r.tv, width)):
        for j in range(0, width, 256):
            both = dot_nn(code_both, r.kvw[:, base + j : base + j + 256])
            high, low = split(both[:LANES] + both[LANES:])
            table[:LANES, j : j + 256] = high
            table[LANES : 2 * LANES, j : j + 256] = low
            table[2 * LANES :, j : j + 256] = high
    cell = lax.broadcasted_iota(jnp.int32, (LANES, CELLS), 1)
    line = lax.broadcasted_iota(jnp.int32, (LANES, CELLS), 0)
    hit = (line == cell // IMG_W) | (line == IMG_W + lax.rem(cell, IMG_W))
    grid_code = jnp.where(hit, 1.0, 0.0).astype(BF16)
    r.ee[:LANES, :] = grid_code
    r.ee[LANES:, :] = grid_code

    WQ.wait()
    for j in range(0, width, 256):
        r.q[:, j : j + 256] = dot_nn(r.nl[...], r.wq[:, j : j + 256]).astype(BF16)
    query_code = dot_nt(r.q[...], r.tk[: 2 * LANES, :])
    query_code = (query_code[:, :LANES] + query_code[:, LANES:]) * scale

    WD.wait()
    for j in range(0, width, 256):
        r.ag[:, j : j + 256] = dot_nt(r.cot[...], r.wd[j : j + 256, :])

    counts_row = cnt[...].astype(F32)
    number = lax.broadcasted_iota(jnp.int32, (img, n_img), 0)
    against = lax.broadcasted_iota(jnp.int32, (img, n_img), 1)
    counts_all = jnp.broadcast_to(counts_row, (img, n_img))
    first = jnp.sum(jnp.where(against < number, counts_all, 0.0), axis=1, keepdims=True).astype(jnp.int32)
    count = jnp.sum(jnp.where(against == number, counts_all, 0.0), axis=1, keepdims=True).astype(jnp.int32)
    block_of = first // LANES
    shift_of = lax.rem(first, LANES)
    block_id = lax.broadcasted_iota(jnp.int32, (img, n_seq * blocks), 1)
    for j in range(9):
        r.sel[j * img : (j + 1) * img, :] = jnp.where(block_id == block_of + j, 1.0, 0.0).astype(BF16)

    mine_lat = pl.ds(pl.multiple_of(s * LANES, LANES), LANES)
    owner_row = img_of[:, mine_lat].astype(F32)
    square0 = lax.broadcasted_iota(jnp.int32, (LANES, LANES), 0)
    square1 = lax.broadcasted_iota(jnp.int32, (LANES, LANES), 1)
    diagonal = square0 == square1
    owner = jnp.sum(jnp.where(diagonal, jnp.broadcast_to(owner_row, (LANES, LANES)), 0.0), axis=1, keepdims=True)
    owner_i = owner.astype(jnp.int32)
    pick = jnp.where(lax.broadcasted_iota(jnp.int32, (LANES, img), 1) == owner_i, 1.0, 0.0).astype(BF16)
    pick_t = jnp.where(
        lax.broadcasted_iota(jnp.int32, (img, LANES), 0) == owner_row.astype(jnp.int32), 1.0, 0.0
    )
    count_lat = jnp.sum(
        jnp.where(lax.broadcasted_iota(jnp.int32, (LANES, n_img), 1) == owner_i, jnp.broadcast_to(counts_row, (LANES, n_img)), 0.0),
        axis=1, keepdims=True,
    )
    r.owner[...] = jnp.broadcast_to(count_lat, (LANES, LANES))

    for copy in pixel_copies:
        copy.wait()

    inside = lax.broadcasted_iota(jnp.int32, (img, CELLS), 1) < count
    for channel in range(3):
        rows_of = dot_nn(r.sel[...], r.pb[channel])
        window = jnp.concatenate([rows_of[j * img : (j + 1) * img] for j in range(9)], axis=1)
        for bit in range(7):
            hop = 1 << bit
            moved = pltpu.roll(window, span - hop, 1)
            window = jnp.where((shift_of & hop) != 0, moved, window)
        r.xi[channel] = jnp.where(inside, window[:, :CELLS], 0.0).astype(BF16)

    def gram_row(channel, x):
        base = geo[1 + channel : 2 + channel, :]
        return base, base + gram[channel][0] * x[0] + gram[channel][1] * x[1] + gram[channel][2] * x[2]

    for at in range(0, img, 16):
        x = [r.xi[channel, at : at + 16, :].astype(F32) for channel in range(3)]
        square = jnp.broadcast_to(geo[0:1, :], (16, CELLS))
        for channel in range(3):
            base, u = gram_row(channel, x)
            square = square + x[channel] * (base + u)
        r.ri[at : at + 16, :] = lax.rsqrt(square + TINY)
    for channel in range(3):
        r.xx[channel] = dot_nn(pick, r.xi[channel]).astype(BF16)
    inv_high, inv_low = split(r.ri[...])
    r.rr[...] = dot_nn(pick, inv_high) + dot_nn(pick, inv_low)

    def over_grid(code):
        return jnp.concatenate(split(code), axis=1)

    r.ss[...] = dot_nn(over_grid(query_code), r.ee[...])
    r.side[...] = query_code
    lane = lax.broadcasted_iota(jnp.int32, (tile, LANES), 1)
    place = lax.broadcasted_iota(jnp.int32, (tile, CELLS), 1).astype(F32)

    def side_columns(code, one, sums):
        made = jnp.where(lane == ONE, one, 0.0)
        for channel in range(3):
            made = made + jnp.where(lane == COLOR + channel, sums[channel], 0.0)
        return made

    def attend(at):
        code = r.side[at, :]
        x = [r.xx[channel, at, :].astype(F32) for channel in range(3)]
        inv = r.rr[at, :]
        raw = r.ss[at, :]
        for channel in range(3):
            raw = raw + code[:, COLOR + channel : COLOR + channel + 1] * x[channel]
        r.ss[at, :] = raw
        allowed = place < r.owner[at, :1]
        score = jnp.where(allowed, raw * inv + code[:, ONE : ONE + 1], FLOOR)
        top = jnp.max(score, axis=1, keepdims=True)
        raised = jnp.where(allowed, jnp.exp(score - top), 0.0)
        total = jnp.sum(raised, axis=1, keepdims=True)
        prob = raised / total
        r.pp[at, :] = prob
        weighted = prob * inv
        r.low[at, :] = weighted.astype(BF16)
        sums = [jnp.sum(weighted * x[channel], axis=1, keepdims=True) for channel in range(3)]
        r.side[at, :] = side_columns(code, jnp.sum(prob, axis=1, keepdims=True), sums)

    by_rows(attend)
    value_code = dot_nt(r.low[...], r.ee[:LANES, :]) + r.side[...]
    code_high, code_low = split(value_code)
    code_three = jnp.concatenate([code_high, code_high, code_low], axis=1)
    for j in range(0, width, 256):
        r.merged[:, j : j + 256] = dot_nn(code_three, r.tv[:, j : j + 256]).astype(BF16)
    value_code_low = code_high

    WO.wait()
    for j in range(0, width, 256):
        r.res[:, j : j + 256] = r.lat[:, j : j + 256].astype(F32) + dot_nn(r.merged[...], r.wo[:, j : j + 256])

    def norm_mid(at):
        x = r.res[at, :]
        center = x - jnp.mean(x, axis=-1, keepdims=True)
        inv = lax.rsqrt(jnp.mean(center * center, axis=-1, keepdims=True) + TINY)
        hat = center * inv
        r.xm[at, :] = hat
        r.rm[at, :] = jnp.broadcast_to(inv, (tile, LANES))
        r.nm[at, :] = (hat * mgain[...] + mshift[...]).astype(BF16)

    by_rows(norm_mid)
    WU.wait()
    for j in range(0, width, 256):
        pre = dot_nn(r.nm[...], r.wu[:, j : j + 256])
        phi = 0.5 * (1.0 + lax.erf(pre * math.sqrt(0.5)))
        r.act[:, j : j + 256] = (pre * phi).astype(BF16)
        slope = phi + pre * (jnp.exp(-0.5 * pre * pre) * (1.0 / math.sqrt(2.0 * math.pi)))
        r.bt[UP, mine, j : j + 256] = (r.ag[:, j : j + 256] * slope).astype(BF16)
    turn(DOWN, r.act)
    send_left(DOWN)
    turn(UP, r.nm)
    send_left(UP)
    send_right(UP)
    turn(OUT, r.merged)
    send_left(OUT)

    for j in range(0, width, 256):
        r.nm[:, j : j + 256] = (r.res[:, j : j + 256] + dot_nn(r.act[...], r.wd[:, j : j + 256])).astype(BF16)
    leave(r.nm, o_mixed.at[0])
    product(DOWN)
    start(DOWN, 0)
    for j in range(0, width, 256):
        r.ag[:, j : j + 256] = dot_nt(r.bt[UP, mine, :], r.wu[j : j + 256, :])
    product(UP)
    start(UP, 0)
    zero = jnp.zeros((1, width), F32)

    def norm_back(grad, hat, inv, gain):
        scaled = grad * gain
        return inv * (scaled - jnp.mean(scaled, axis=-1, keepdims=True) - hat * jnp.mean(scaled * hat, axis=-1, keepdims=True))

    def mid_back(i, carry):
        at = pl.ds(pl.multiple_of(i * tile, tile), tile)
        grad, hat = r.ag[at, :], r.xm[at, :]
        total = r.cot[at, :].astype(F32) + norm_back(grad, hat, r.rm[at, :1], mgain[...])
        r.res[at, :] = total
        r.bt[OUT, pl.ds(pl.multiple_of(c * LANES + i * tile, tile), tile), :] = total.astype(BF16)
        return carry[0] + jnp.sum(grad * hat, axis=0, keepdims=True), carry[1] + jnp.sum(grad, axis=0, keepdims=True)

    gain_sum, shift_sum = lax.fori_loop(0, LANES // tile, mid_back, (zero, zero))
    r.vec[...] = jnp.zeros_like(r.vec)
    r.vec[2:3, :] = gain_sum
    r.vec[3:4, :] = shift_sum
    send_right(OUT)
    for j in range(0, width, 256):
        r.da[:, j : j + 256] = dot_nt(r.bt[OUT, mine, :], r.wo[j : j + 256, :]).astype(BF16)

    product(OUT)
    start(OUT, 0)
    back_code = dot_nt(r.da[...], r.tv[: 2 * LANES, :])
    back_code = back_code[:, :LANES] + back_code[:, LANES:]
    r.ag[...] = dot_nn(over_grid(back_code), r.ee[...])
    r.side[...] = back_code

    def attend_back(at):
        code = r.side[at, :]
        x = [r.xx[channel, at, :].astype(F32) for channel in range(3)]
        inv = r.rr[at, :]
        prob = r.pp[at, :]
        raw = r.ag[at, :]
        for channel in range(3):
            raw = raw + code[:, COLOR + channel : COLOR + channel + 1] * x[channel]
        grad = raw * inv + code[:, ONE : ONE + 1]
        delta = jnp.sum(prob * grad, axis=1, keepdims=True)
        back = prob * (grad - delta)
        r.ye[at, :] = (back * r.ss[at, :] + prob * raw).astype(BF16)
        weighted = back * inv
        r.low[at, :] = weighted.astype(BF16)
        r.dp[at, :] = back.astype(BF16)
        sums = [jnp.sum(weighted * x[channel], axis=1, keepdims=True) for channel in range(3)]
        r.side[at, :] = side_columns(code, jnp.sum(back, axis=1, keepdims=True), sums)

    by_rows(attend_back)
    r.dp[LANES:, :] = r.pp[...].astype(BF16)
    key_code = (dot_nt(r.low[...], r.ee[:LANES, :]) + r.side[...]) * scale
    code_high, code_low = split(key_code)
    code_three = jnp.concatenate([code_high, code_high, code_low], axis=1)
    for j in range(0, width, 256):
        r.bt[QUERY, mine, j : j + 256] = dot_nn(code_three, r.tk[:, j : j + 256]).astype(BF16)
    send_right(QUERY)

    step(DOWN, 0)

    for j in range(0, width, 256):
        r.ag[:, j : j + 256] = dot_nt(r.bt[QUERY, mine, :], r.wq[j : j + 256, :])

    def latents_back(i, carry):
        at = pl.ds(pl.multiple_of(i * tile, tile), tile)
        grad, hat = r.ag[at, :], r.xl[at, :]
        r.res[at, :] = r.res[at, :] + norm_back(grad, hat, r.rl[at, :1], qgain[...])
        return carry[0] + jnp.sum(grad * hat, axis=0, keepdims=True), carry[1] + jnp.sum(grad, axis=0, keepdims=True)

    gain_sum, shift_sum = lax.fori_loop(0, LANES // tile, latents_back, (zero, zero))
    r.vec[0:1, :] = gain_sum
    r.vec[1:2, :] = shift_sum
    leave(r.res, o_lat.at[0])
    product(QUERY)
    start(QUERY, 0)

    heap = 256 // (2 * rows * parts["c"])
    for j in range(0, 2 * width, 256):
        if j < width:
            made = dot_tn(r.q[:, j : j + 256], code_high)
        else:
            made = dot_tn(r.da[:, j - width : j - width + 256], value_code_low)
        riding = pltpu.roll(r.vec[:, j // 2 : j // 2 + LANES].T, ONE + 1, 1).reshape(-1, rows, LANES)
        made = made.reshape(-1, 2 * rows, LANES)
        made = jnp.concatenate([made[:, :rows] + riding, made[:, rows:]], axis=1)
        r.zc[heap * (j // 256) : heap * (j // 256 + 1)] = made.astype(BF16).reshape(heap, parts["c"], 2 * rows, LANES)
    to_core("z", 8, r.zc.at[:, part("c", 1 - c)], r.zcr)
    step(UP, 0)

    in_gain, in_shift = jnp.zeros((feat, 1), F32), jnp.zeros((feat, 1), F32)
    for j in range(0, 2 * width, 256):
        sums = r.zc[heap * (j // 256) : heap * (j // 256 + 1)].reshape(256, LANES)
        spread = dot_nt(r.fct[...], jnp.concatenate([sums, sums], axis=1))
        factor = r.kvw[:, j : j + 256].astype(F32)
        in_gain = in_gain + jnp.sum(factor * spread[:feat], axis=1, keepdims=True)
        in_shift = in_shift + jnp.sum(factor * spread[wide : wide + 1], axis=1, keepdims=True)
    for at, column in ((0, in_gain), (1, in_shift)):
        for j in range(0, feat, LANES):
            tall = min(LANES, feat - j)
            eye = lax.broadcasted_iota(jnp.int32, (tall, LANES), 0) == lax.broadcasted_iota(jnp.int32, (tall, LANES), 1)
            r.ar[0, at : at + 1, j : j + LANES] = jnp.sum(jnp.where(eye, column[j : j + tall], 0.0), axis=0, keepdims=True)
    seq_copies = []
    for offset in range(1, n_seq):
        slot = n_seq - offset - 1
        copy = pltpu.make_async_remote_copy(
            src_ref=r.ar.at[0], dst_ref=r.ars.at[slot], send_sem=r.as_s.at[offset - 1], recv_sem=r.as_r.at[slot],
            device_id=(z, lax.rem(s + offset, n_seq)), device_id_type=MESH,
        )
        copy.start()
        seq_copies.append(copy)
    core_copies.pop("z").wait()
    both = r.zc[:, part("c", c)].astype(F32) + r.zcr[...].astype(F32)
    r.zs0[0] = both.astype(BF16).reshape(parts["z"], parts["a"], parts["b"], 2 * rows, LANES)
    start(SUMS, 0)

    query_t, back_t = query_code.T, back_code.T
    lifted = jnp.concatenate(
        [
            jnp.concatenate([pick_t * code_t[COLOR + channel : COLOR + channel + 1, :] for code_t in (query_t, back_t)], axis=1)
            for channel in range(3)
        ],
        axis=0,
    ).astype(BF16)
    along = dot_nn(pick_t.astype(BF16), r.ye[...])
    inv = r.ri[...]
    cube = inv * inv * inv * along
    colors = [r.xi[channel].astype(F32) for channel in range(3)]
    for channel in range(3):
        steep = dot_nn(lifted[channel * img : (channel + 1) * img], r.dp[...])
        own_grad = inv * steep - cube * gram_row(channel, colors)[1]
        window = jnp.concatenate([own_grad, jnp.zeros((img, LANES), F32)], axis=1)
        for bit in range(7):
            hop = 1 << bit
            moved = pltpu.roll(window, hop, 1)
            window = jnp.where((shift_of & hop) != 0, moved, window)
        for j in range(9):
            r.pg[j * img : (j + 1) * img, :] = window[:, j * LANES : (j + 1) * LANES]
        grad_high, grad_low = split(r.pg[...])
        r.pgs[channel] = dot_tn(r.sel[...], grad_high) + dot_tn(r.sel[...], grad_low)
    grad_copies = []
    for offset in range(1, n_seq):
        target = lax.rem(s + offset, n_seq)
        copy = pltpu.make_async_remote_copy(
            src_ref=r.pgs.at[:, pl.ds(pl.multiple_of(target * blocks, blocks), blocks), :],
            dst_ref=r.pgr.at[n_seq - offset - 1],
            send_sem=r.pg_s.at[offset - 1], recv_sem=r.pg_r.at[n_seq - offset - 1],
            device_id=(z, target), device_id_type=MESH,
        )
        copy.start()
        grad_copies.append(copy)

    step(DOWN, 1)
    step(OUT, 0)
    step(UP, 1)
    wait_all(seq_copies)
    r.ar[1] = gathered(r.ar[0], r.ars, n_seq)
    z_copies = []
    for offset in range(1, n_batch):
        slot = n_batch - offset - 1
        copy = pltpu.make_async_remote_copy(
            src_ref=r.ar.at[1], dst_ref=r.arz.at[slot], send_sem=r.az_s.at[offset - 1], recv_sem=r.az_r.at[slot],
            device_id=(peer("z", offset), s), device_id_type=MESH,
        )
        copy.start()
        z_copies.append(copy)
    step(QUERY, 0)
    step(OUT, 1)
    step(SUMS, 0)

    total_rows = width // (n_batch * n_seq)
    inner = 0
    for name in ("a", "b", "c"):
        if parts[name] < sizes[name]:
            inner = inner * sizes[name] + here[name]

    def finish(mat, made):
        step(mat, 2)
        if total_rows < rows:
            r.out[mat] = pltpu.roll(r.out[mat], lax.rem(rows - inner * total_rows, rows), 0)
        leave(r.out.at[mat, :total_rows], made)

    finish(DOWN, o_wd)
    step(QUERY, 1)
    step(SUMS, 1)
    wait_all(grad_copies)
    o_pix[...] = gathered(r.pgs[:, own, :], r.pgr, n_seq)
    finish(UP, o_wu)
    wait_all(z_copies)
    o_in[...] = gathered(r.ar[1], r.arz, n_batch)[:, :feat]
    finish(OUT, o_wo)
    finish(QUERY, o_wq)
    step(SUMS, 2)
    sums = r.zout[...]
    turned = sums
    if total_rows < rows:
        turned = pltpu.roll(sums, lax.rem(rows - inner * total_rows, rows), 0)
        sums = pltpu.roll(sums, lax.rem(2 * (rows - inner * total_rows), 2 * rows), 0)
    high, low = split(sums)
    code_high, code_low = split(r.mt[...].T)
    spread_left = jnp.concatenate([code_high, code_high, code_low], axis=1)
    o_kv[...] = dot_nt(jnp.concatenate([high, low, high], axis=1), spread_left)[: 2 * total_rows, :feat]
    square = jnp.concatenate([turned, jnp.zeros((LANES - 2 * rows, LANES), F32)], axis=0)
    o_vec[...] = square.T[COLOR : COLOR + 8, :total_rows]
    wait_all(leaving)


def hand_over(mixed, lat, pix, vec, wq, inner, kv, wo, wu, wd, *refs):
    o_mixed, o_lat, o_pix, o_qg, o_qs, o_wq, o_ig, o_is, o_kv, o_wo, o_mg, o_ms, o_wu, o_wd = refs
    for src, dst in ((mixed, o_mixed), (lat, o_lat), (wq, o_wq), (wo, o_wo), (wu, o_wu), (wd, o_wd), (kv, o_kv)):
        dst[...] = src[...]
    for channel in range(3):
        for j in range(pix.shape[1]):
            o_pix[channel, 0:1, j * LANES : (j + 1) * LANES] = pix[channel, j : j + 1, :]
    for i, dst in enumerate((o_qg, o_qs, o_mg, o_ms)):
        dst[...] = vec[4 + i, :]
    for i, dst in enumerate((o_ig, o_is)):
        dst[...] = inner[i, :]


def solution(mesh):
    n_batch, n_seq = mesh.shape["batch"], mesh.shape["seq"]

    def body(latents, pixels, counts, latent_image, query_gain, query_shift, query_weight, input_gain, input_shift,
             kv_weight, out_weight, mlp_gain, mlp_shift, up_weight, down_weight, cotangent):
        width = query_weight.shape[0]
        feat = kv_weight.shape[0]
        pix_dev = pixels.shape[2]
        n_img = counts.shape[1]
        fc, geo, fct, gram = position_tables(feat)
        scratch = shapes_of(n_batch, n_seq, width, pix_dev, n_img, feat)
        rows = width // (n_batch * n_seq)
        vm = pl.BlockSpec(memory_space=pltpu.VMEM)
        hbm = pl.BlockSpec(memory_space=pl.ANY)
        f32 = lambda *shape: jax.ShapeDtypeStruct(shape, F32)
        mixed, latent_grad, square = jax.ShapeDtypeStruct(latents.shape, BF16), f32(*latents.shape), f32(rows, width)
        kv = f32(2 * rows, feat)
        args = (
            latents, pixels, counts, latent_image,
            query_gain[None], query_shift[None], query_weight, input_gain, input_shift, kv_weight,
            out_weight, mlp_gain[None], mlp_shift[None], up_weight, down_weight, cotangent,
            jnp.asarray(fc), jnp.asarray(geo), jnp.asarray(fct),
        )
        in_hbm = (0, 6, 9, 10, 13, 14, 15, 16, 18)
        big = (0, 1, 4, 7, 8, 9)
        made = pl.pallas_call(
            functools.partial(layer, n_batch, n_seq, width, n_img, feat, gram),
            out_shape=(
                mixed, latent_grad, f32(3, pix_dev // LANES, LANES), f32(8, rows), square, f32(2, feat), kv, square, square, square,
            ),
            in_specs=[hbm if i in in_hbm else vm for i in range(len(args))],
            out_specs=[hbm if i in big else vm for i in range(10)],
            scratch_shapes=[vars(scratch)],
            compiler_params=pltpu.CompilerParams(
                collective_id=0, has_side_effects=True, vmem_limit_bytes=60 * 1024 * 1024
            ),
            name="layer",
        )(*args)
        out_shape = (
            mixed, latent_grad, f32(3, 1, pix_dev), f32(rows), f32(rows), square, f32(feat), f32(feat), kv, square,
            f32(rows), f32(rows), square, square,
        )
        out = pl.pallas_call(
            hand_over,
            out_shape=out_shape,
            in_specs=[vm] * len(made),
            out_specs=[vm] * len(out_shape),
            name="hand_over",
        )(*made)
        return (*out[:2], out[2].transpose(1, 0, 2), *out[3:8], out[8].T, *out[9:])

    whole, vec = P(("batch", "seq"), None), P(("batch", "seq"))
    rowed = P("batch", "seq", None)
    return jax.shard_map(
        body,
        mesh=mesh,
        in_specs=(rowed, P("batch", None, "seq"), P("batch", None), P("batch", None)) + (P(),) * 11 + (rowed,),
        out_specs=(
            rowed, rowed, P("batch", None, "seq"), vec, vec, whole, P(), P(), P(None, ("batch", "seq")), whole,
            vec, vec, whole, whole,
        ),
        check_vma=False,
    )
```

```python
import functools
import math
from types import SimpleNamespace

import jax
import jax.numpy as jnp
import numpy as np
from jax import lax
from jax.experimental import pallas as pl
from jax.experimental.pallas import tpu as pltpu
from jax.sharding import PartitionSpec as P

IMG_W = 32
TOP_FREQ = 112.0
TINY = 1e-05
FLOOR = -1e30
MESH = pl.DeviceIdType.MESH
F32 = jnp.float32
BF16 = jnp.bfloat16
LANES = 128
CELLS = IMG_W * IMG_W
COLOR = 2 * IMG_W
ONE = COLOR + 3


def position_tables(feat):
    bands = (feat - 5) // 4
    freq = np.linspace(1.0, TOP_FREQ, bands).astype(np.float32)
    grid = (np.float32(2.0) * np.arange(IMG_W, dtype=np.float32) / np.float32(IMG_W - 1) - np.float32(1.0)).astype(np.float32)
    phase = ((np.float32(math.pi) * grid)[:, None] * freq[None, :]).astype(np.float64)
    table = np.zeros((LANES, feat), np.float64)
    for axis in range(2):
        rows = slice(axis * IMG_W, (axis + 1) * IMG_W)
        table[rows, 3 + axis] = grid
        table[rows, 5 + axis * bands : 5 + (axis + 1) * bands] = np.sin(phase)
        table[rows, 5 + (2 + axis) * bands : 5 + (3 + axis) * bands] = np.cos(phase)
    for channel in range(3):
        table[COLOR + channel, channel] = 1.0
    centered = table - table.mean(axis=1, keepdims=True)
    gram = centered @ centered.T / feat
    place = np.arange(CELLS)
    row, col = place // IMG_W, IMG_W + place % IMG_W
    geometry = np.zeros((8, CELLS), np.float32)
    geometry[0] = gram[row, row] + gram[col, col] + 2.0 * gram[row, col]
    for channel in range(3):
        geometry[1 + channel] = gram[COLOR + channel, row] + gram[COLOR + channel, col]
    wide = -(-feat // LANES) * LANES
    padded = np.zeros((LANES, wide), np.float32)
    padded[:, :feat] = centered
    turned = np.zeros((wide + 8, LANES), np.float32)
    turned[:feat] = centered.T
    turned[wide, ONE] = 1.0
    high = turned.astype(jnp.bfloat16)
    low = (turned - high.astype(np.float32)).astype(jnp.bfloat16)
    colors = gram[COLOR : COLOR + 3, COLOR : COLOR + 3]
    return padded, geometry, np.concatenate([high, low], axis=1), [[float(v) for v in line] for line in colors]


def split(values):
    high = values.astype(BF16)
    return high, (values - high.astype(F32)).astype(BF16)


def dot_nn(left, right):
    return jnp.dot(left, right, preferred_element_type=F32)


def dot_nt(left, right):
    return lax.dot_general(left, right, (((1,), (1,)), ((), ())), preferred_element_type=F32)


def dot_tn(left, right):
    return lax.dot_general(left, right, (((0,), (0,)), ((), ())), preferred_element_type=F32)


def plan(n_batch, n_seq, width):
    core = 2
    fast = math.isqrt(n_seq // core)
    while (n_seq // core) % fast:
        fast -= 1
    slow = n_seq // core // fast
    sizes = {"z": n_batch, "a": slow, "b": fast, "c": core}
    parts, left = dict(sizes), width
    for name in ("c", "b", "a"):
        if width // math.prod(parts.values()) < 16:
            parts[name] = 1
    orders = (("b", "a") if parts["b"] > 1 else ("a", "b"), ("a", "b"))
    return sizes, parts, width // math.prod(parts.values()), orders


def by_columns(n_seq, width):
    return width // n_seq % LANES == 0


def shapes_of(n_batch, n_seq, width, pix_dev, n_img, feat):
    sizes, parts, rows, orders = plan(n_batch, n_seq, width)
    img = -(-n_img // 16) * 16
    blocks = pix_dev // LANES
    wide = -(-feat // LANES) * LANES
    factor_rows = (width // (2 * rows), 2, rows) if parts["c"] > 1 else (1, 1, width)
    S = SimpleNamespace()
    vm = lambda *shape, dtype=BF16: pltpu.VMEM(shape, dtype)
    S.wq, S.wo, S.wu, S.wd = [vm(width, width)] * 4
    S.tk = vm(3 * LANES, width)
    S.tv = vm(3 * LANES, width)
    S.ee = vm(2 * LANES, CELLS)
    S.mt = vm(LANES, wide, dtype=F32)
    S.xl, S.xm, S.res, S.ag = [vm(LANES, width, dtype=F32)] * 4
    S.rl = vm(LANES, LANES, dtype=F32)
    S.rm = vm(LANES, LANES, dtype=F32)
    S.nl, S.q, S.merged, S.nm, S.act, S.da = [vm(LANES, width)] * 6
    S.pb = vm(3, n_seq * blocks, LANES)
    S.sel = vm(9 * img, n_seq * blocks)
    S.xi = vm(3, img, CELLS)
    S.ri = vm(img, CELLS, dtype=F32)
    S.xx = vm(3, LANES, CELLS)
    S.rr = vm(LANES, CELLS, dtype=F32)
    S.ss = vm(LANES, CELLS, dtype=F32)
    S.pp = vm(LANES, CELLS, dtype=F32)
    S.low = vm(LANES, CELLS)
    S.dp = vm(2 * LANES, CELLS)
    S.ye = vm(LANES, CELLS)
    S.side = vm(LANES, LANES, dtype=F32)
    S.owner = vm(LANES, LANES, dtype=F32)
    S.pg = vm(9 * img, LANES, dtype=F32)
    S.pgs = vm(3, n_seq * blocks, LANES, dtype=F32)
    S.pgr = vm(n_seq - 1, 3, blocks, LANES, dtype=F32)
    tall, plane, apart = width // n_batch, n_seq // 2, by_columns(n_seq, width)
    full = 2 if apart else 3
    S.at = vm(full, *factor_rows, 2 * LANES)
    S.bt = vm(3, 2 * LANES, width)
    S.ms0 = vm(full, parts["z"], parts["a"], parts["b"], rows, width)
    S.ds0 = vm(1, 1, parts["a"], parts["b"], rows, width)
    S.zs0 = vm(1, parts["z"], parts["a"], parts["b"], 2 * rows, LANES)
    S.mr, S.dr, S.zr = [], [], []
    for made, mats, deep, across in ((S.mr, full, parts["z"], width // 2), (S.dr, 1, 1, width // 2), (S.zr, 1, parts["z"], LANES)):
        for first, other in orders:
            made.append([
                vm(mats, sizes[first] - 1, deep, parts[other], rows, across),
                vm(mats, sizes[other] - 1, deep, rows, across),
            ] + [vm(mats, sizes["z"] - 1, rows, across)] * (deep > 1))
    S.gz, S.az = vm(n_batch * LANES, width), vm(n_batch * LANES, tall)
    S.dc = vm(parts["a"], parts["b"], parts["c"], rows, width)
    S.dcr = vm(parts["a"], parts["b"], rows, width)
    if apart:
        S.np, S.qp = vm(plane * LANES, width), vm(plane * LANES, width // plane)
        S.qc, S.qcr = vm(2, width // n_seq, width), vm(width // n_seq, width)
        S.qz = vm(n_batch - 1, width // n_seq, tall)
        S.qt = vm(tall, width // n_seq, dtype=F32)
        S.qo = vm(tall // n_seq, width, dtype=F32)
    S.zc = vm(width // (rows * parts["c"]), parts["c"], 2 * rows, LANES)
    S.zcr = vm(width // (rows * parts["c"]), 2 * rows, LANES)
    S.vec = vm(LANES, width, dtype=F32)
    S.out = vm(4, rows, width, dtype=F32)
    S.zout = vm(2 * rows, LANES, dtype=F32)
    S.ar = vm(2, 2, wide, dtype=F32)
    S.ars = vm(n_seq - 1, 2, wide, dtype=F32)
    S.arz = vm(n_batch - 1, 2, wide, dtype=F32)
    S.lat, S.cot = [vm(LANES, width)] * 2
    S.kvw = vm(feat, 2 * width)
    S.fc = vm(LANES, wide, dtype=F32)
    S.fct = vm(wide + 8, 2 * LANES)
    most = max(sizes.values()) - 1
    sem = lambda *shape: pltpu.SemaphoreType.DMA(shape)
    S.w_sem = sem(9)
    S.o_sem = sem(6)
    S.px_s, S.px_r = sem(n_seq - 1), sem(n_seq - 1)
    S.pg_s, S.pg_r = sem(n_seq - 1), sem(n_seq - 1)
    S.co_s, S.co_r = sem(9), sem(9)
    S.gz_s, S.gz_r, S.az_s, S.az_r, S.qz_s, S.qz_r = [sem(n_batch - 1)] * 6
    S.np_s, S.np_r, S.qp_s, S.qp_r = [sem(plane - 1)] * 4
    S.qo_s, S.qo_r = [sem(n_seq - 1)] * 2
    S.rs_s, S.rs_r = sem(5, 2, 3, most), sem(5, 2, 3, most)
    S.as_s, S.as_r = sem(n_seq - 1), sem(n_seq - 1)
    S.ab_s, S.ab_r = sem(n_batch - 1), sem(n_batch - 1)
    return S


def layer(
    n_batch, n_seq, width, n_img, feat, gram,
    h_lat, px, cnt, img_of, qgain, qshift, h_wq, igain, ishift, h_kvw, h_wo, mgain, mshift, h_wu, h_wd, h_cot, h_fc, geo, h_fct,
    o_mixed, o_lat, o_pix, o_vec, o_wq, o_in, o_kv, o_wo, o_wu, o_wd, r,
):
    r = SimpleNamespace(**r)
    sizes, parts, rows, orders = plan(n_batch, n_seq, width)
    img = r.xi.shape[1]
    blocks = px.shape[2] // LANES
    wide = r.mt.shape[1]
    span = CELLS + LANES
    scale = width ** (-0.5)

    z = lax.axis_index("batch")
    s = lax.axis_index("seq")
    c = lax.rem(s, 2)
    b = lax.rem(s // 2, sizes["b"])
    a = s // (2 * sizes["b"])
    here = {"z": z, "a": a, "b": b, "c": c}

    def device(**moved):
        at = {**here, **moved}
        return (at["z"], (at["a"] * sizes["b"] + at["b"]) * 2 + at["c"])

    def part(name, index):
        return index if parts[name] > 1 else 0

    def peer(name, offset):
        return lax.rem(here[name] + offset, sizes[name])

    barrier = pltpu.get_barrier_semaphore()
    for offset in range(1, n_seq):
        pl.semaphore_signal(barrier, inc=1, device_id=(z, lax.rem(s + offset, n_seq)), device_id_type=MESH)
    for offset in range(1, n_batch):
        pl.semaphore_signal(barrier, inc=1, device_id=(peer("z", offset), s), device_id_type=MESH)

    arriving = []
    for i, (src, dst) in enumerate((
        (h_lat.at[0], r.lat), (h_fc, r.fc), (h_kvw, r.kvw), (h_wq, r.wq), (h_cot.at[0], r.cot), (h_wd, r.wd),
        (h_wo, r.wo), (h_wu, r.wu), (h_fct, r.fct),
    )):
        copy = pltpu.make_async_copy(src, dst, r.w_sem.at[i])
        copy.start()
        arriving.append(copy)
    LAT, FC, KVW, WQ, COT, WD, WO, WU, FCT = arriving
    leaving = []

    def leave(src, dst):
        copy = pltpu.make_async_copy(src, dst, r.o_sem.at[len(leaving)])
        copy.start()
        leaving.append(copy)

    UP, OUT, QUERY, DOWN, SUMS = range(5)
    apart = by_columns(n_seq, width)
    tall, plane = width // n_batch, n_seq // 2
    tile = 16

    def by_rows(step):
        def run(i, carry):
            step(pl.ds(pl.multiple_of(i * tile, tile), tile))
            return carry

        lax.fori_loop(0, LANES // tile, run, 0)

    mine = pl.ds(pl.multiple_of(c * LANES, LANES), LANES)

    def turn(which, factor):
        for j in range(width // LANES):
            block = factor[:, j * LANES : (j + 1) * LANES].astype(F32).T.astype(BF16)
            if parts["c"] > 1:
                deep = LANES // (2 * rows)
                r.at[which, j * deep : (j + 1) * deep, :, :, mine] = block.reshape(deep, 2, rows, LANES)
            else:
                r.at[which, 0, 0, j * LANES : (j + 1) * LANES, mine] = block

    core_copies = {}

    def to_core(key, index, src, dst):
        copy = pltpu.make_async_remote_copy(
            src_ref=src, dst_ref=dst, send_sem=r.co_s.at[index], recv_sem=r.co_r.at[index],
            device_id=device(c=1 - c), device_id_type=MESH,
        )
        copy.start()
        core_copies[key] = copy

    def send_left(which):
        ref = r.at.at[which, :, part("c", 1 - c), :, mine]
        to_core(("left", which), 2 * which, ref, ref)

    def send_right(which):
        ref = r.bt.at[which, mine, :]
        to_core(("right", which), 2 * which + 1, ref, ref)

    def start_stage(key, stage, name, src_of, dst):
        mat, half = key
        copies = []
        for offset in range(1, sizes[name]):
            target = peer(name, offset)
            slot = sizes[name] - offset - 1
            copy = pltpu.make_async_remote_copy(
                src_ref=src_of(part(name, target)), dst_ref=dst.at[slot],
                send_sem=r.rs_s.at[mat, half, stage, offset - 1], recv_sem=r.rs_r.at[mat, half, stage, slot],
                device_id=device(**{name: target}), device_id_type=MESH,
            )
            copy.start()
            copies.append(copy)
        return copies

    def wait_all(copies):
        for copy in copies:
            copy.wait()

    def gathered(own, dst, n):
        total = own.astype(F32)
        for slot in range(n - 1):
            total = total + dst[slot].astype(F32)
        return total

    flying = {}

    def buffers_of(mat):
        if mat == DOWN:
            return r.ds0, r.dr, 0
        return (r.zs0, r.zr, 0) if mat == SUMS else (r.ms0, r.mr, mat)

    def cut(mat, half):
        if mat == SUMS:
            return pl.ds(half * rows, rows), slice(None)
        return slice(None), pl.ds(half * (width // 2), width // 2)

    def blocks_at(mat, half, stage, target=None):
        s0, received, i = buffers_of(mat)
        at = {"z": slice(None), "a": slice(None), "b": slice(None)}
        path = orders[half] + ("z",)
        for done in path[:stage]:
            at[done] = part(done, here[done])
        at[path[stage]] = part(path[stage], here[path[stage]]) if target is None else target
        return (i, at["z"], at["a"], at["b"]) + cut(mat, half)

    def start(mat, stage):
        s0, received, i = buffers_of(mat)
        for half in range(2):
            name = (orders[half] + ("z",))[stage]
            flying[mat, half] = start_stage(
                (mat, half), stage, name,
                lambda p: s0.at[blocks_at(mat, half, stage, p)],
                received[half][stage].at[i],
            )

    def step(mat, stage):
        s0, received, i = buffers_of(mat)
        last = 1 if mat == DOWN else 2
        for half in range(2):
            wait_all(flying[mat, half])
            name = (orders[half] + ("z",))[stage]
            keep = blocks_at(mat, half, stage)
            total = gathered(s0[keep], received[half][stage].at[i], sizes[name])
            if stage < last:
                s0[keep] = total.astype(BF16)
            elif mat == SUMS:
                r.zout[cut(mat, half)] = total
            else:
                r.out[(mat,) + cut(mat, half)] = total[0] if mat == DOWN else total
        if stage < last:
            start(mat, stage + 1)

    def exchange(n, index, device_at, src_of, dst, sends, receives):
        copies = []
        for offset in range(1, n):
            target = lax.rem(index + offset, n)
            copy = pltpu.make_async_remote_copy(
                src_ref=src_of(target), dst_ref=dst(n - offset - 1), send_sem=sends.at[offset - 1],
                recv_sem=receives.at[n - offset - 1], device_id=device_at(target), device_id_type=MESH,
            )
            copy.start()
            copies.append(copy)
        return copies

    def span_of(index, size):
        return pl.ds(pl.multiple_of(index * size, size), size)

    on_z = lambda target: (target, s)
    in_plane = lambda target: (z, target * 2 + c)
    in_row = lambda target: (z, target)
    spot = s // 2

    def product(mat):
        core_copies.pop(("left", mat)).wait()
        core_copies.pop(("right", mat)).wait()
        left = r.at[mat, :, part("c", c)].reshape(-1, 2 * LANES)
        for j in range(0, width, 256):
            made = dot_nn(left, r.bt[mat, :, j : j + 256]).astype(BF16)
            r.ms0[mat, :, :, :, :, j : j + 256] = made.reshape(parts["z"], parts["a"], parts["b"], rows, 256)

    def norm_latents(at):
        x = r.lat[at, :].astype(F32)
        center = x - jnp.mean(x, axis=-1, keepdims=True)
        inv = lax.rsqrt(jnp.mean(center * center, axis=-1, keepdims=True) + TINY)
        hat = center * inv
        r.xl[at, :] = hat
        r.rl[at, :] = jnp.broadcast_to(inv, (tile, LANES))
        r.nl[at, :] = (hat * qgain[...] + qshift[...]).astype(BF16)

    LAT.wait()
    by_rows(norm_latents)
    COT.wait()
    r.gz[span_of(z, LANES), :] = r.cot[...]
    if apart:
        r.np[span_of(spot, LANES), :] = r.nl[...]
    else:
        turn(QUERY, r.nl)

    own = pl.ds(pl.multiple_of(s * blocks, blocks), blocks)
    colors = px[0].astype(F32)
    for channel in range(3):
        line = colors[channel : channel + 1]
        stacked = jnp.concatenate([line[:, j * LANES : (j + 1) * LANES] for j in range(blocks)], axis=0)
        r.pb[channel, own, :] = stacked.astype(BF16)
    pl.semaphore_wait(barrier, n_seq - 1 + n_batch - 1)
    pixel_copies = []
    for offset in range(1, n_seq):
        copy = pltpu.make_async_remote_copy(
            src_ref=r.pb.at[:, own, :], dst_ref=r.pb.at[:, own, :],
            send_sem=r.px_s.at[offset - 1], recv_sem=r.px_r.at[n_seq - offset - 1],
            device_id=(z, lax.rem(s + offset, n_seq)), device_id_type=MESH,
        )
        copy.start()
        pixel_copies.append(copy)
    if apart:
        own_norm = r.np.at[span_of(spot, LANES), :]
        norm_copies = exchange(plane, spot, in_plane, lambda target: own_norm, lambda slot: own_norm, r.np_s, r.np_r)
    else:
        send_left(QUERY)
    own_cot = r.gz.at[span_of(z, LANES), :]
    cot_copies = exchange(n_batch, z, on_z, lambda target: own_cot, lambda slot: own_cot, r.gz_s, r.gz_r)

    FCT.wait()
    FC.wait()
    KVW.wait()
    row_of = lax.broadcasted_iota(jnp.int32, (LANES, feat), 0)
    code = r.fc[:, :feat] * igain[...][None] + jnp.where(row_of == ONE, ishift[...][None], 0.0)
    r.mt[...] = jnp.zeros_like(r.mt)
    r.mt[:, :feat] = code
    code_high, code_low = split(code)
    code_both = jnp.concatenate([code_high, code_low], axis=0)
    for table, base in ((r.tk, 0), (r.tv, width)):
        for j in range(0, width, 256):
            both = dot_nn(code_both, r.kvw[:, base + j : base + j + 256])
            high, low = split(both[:LANES] + both[LANES:])
            table[:LANES, j : j + 256] = high
            table[LANES : 2 * LANES, j : j + 256] = low
            table[2 * LANES :, j : j + 256] = high
    cell = lax.broadcasted_iota(jnp.int32, (LANES, CELLS), 1)
    line = lax.broadcasted_iota(jnp.int32, (LANES, CELLS), 0)
    hit = (line == cell // IMG_W) | (line == IMG_W + lax.rem(cell, IMG_W))
    grid_code = jnp.where(hit, 1.0, 0.0).astype(BF16)
    r.ee[:LANES, :] = grid_code
    r.ee[LANES:, :] = grid_code

    WQ.wait()
    for j in range(0, width, 256):
        r.q[:, j : j + 256] = dot_nn(r.nl[...], r.wq[:, j : j + 256]).astype(BF16)
    query_code = dot_nt(r.q[...], r.tk[: 2 * LANES, :])
    query_code = (query_code[:, :LANES] + query_code[:, LANES:]) * scale

    WD.wait()
    for j in range(0, width, 256):
        r.ag[:, j : j + 256] = dot_nt(r.cot[...], r.wd[j : j + 256, :])

    counts_row = cnt[...].astype(F32)
    number = lax.broadcasted_iota(jnp.int32, (img, n_img), 0)
    against = lax.broadcasted_iota(jnp.int32, (img, n_img), 1)
    counts_all = jnp.broadcast_to(counts_row, (img, n_img))
    first = jnp.sum(jnp.where(against < number, counts_all, 0.0), axis=1, keepdims=True).astype(jnp.int32)
    count = jnp.sum(jnp.where(against == number, counts_all, 0.0), axis=1, keepdims=True).astype(jnp.int32)
    block_of = first // LANES
    shift_of = lax.rem(first, LANES)
    block_id = lax.broadcasted_iota(jnp.int32, (img, n_seq * blocks), 1)
    for j in range(9):
        r.sel[j * img : (j + 1) * img, :] = jnp.where(block_id == block_of + j, 1.0, 0.0).astype(BF16)

    mine_lat = pl.ds(pl.multiple_of(s * LANES, LANES), LANES)
    owner_row = img_of[:, mine_lat].astype(F32)
    square0 = lax.broadcasted_iota(jnp.int32, (LANES, LANES), 0)
    square1 = lax.broadcasted_iota(jnp.int32, (LANES, LANES), 1)
    diagonal = square0 == square1
    owner = jnp.sum(jnp.where(diagonal, jnp.broadcast_to(owner_row, (LANES, LANES)), 0.0), axis=1, keepdims=True)
    owner_i = owner.astype(jnp.int32)
    pick = jnp.where(lax.broadcasted_iota(jnp.int32, (LANES, img), 1) == owner_i, 1.0, 0.0).astype(BF16)
    pick_t = jnp.where(
        lax.broadcasted_iota(jnp.int32, (img, LANES), 0) == owner_row.astype(jnp.int32), 1.0, 0.0
    )
    count_lat = jnp.sum(
        jnp.where(lax.broadcasted_iota(jnp.int32, (LANES, n_img), 1) == owner_i, jnp.broadcast_to(counts_row, (LANES, n_img)), 0.0),
        axis=1, keepdims=True,
    )
    r.owner[...] = jnp.broadcast_to(count_lat, (LANES, LANES))

    for copy in pixel_copies:
        copy.wait()

    inside = lax.broadcasted_iota(jnp.int32, (img, CELLS), 1) < count
    for channel in range(3):
        rows_of = dot_nn(r.sel[...], r.pb[channel])
        window = jnp.concatenate([rows_of[j * img : (j + 1) * img] for j in range(9)], axis=1)
        for bit in range(7):
            hop = 1 << bit
            moved = pltpu.roll(window, span - hop, 1)
            window = jnp.where((shift_of & hop) != 0, moved, window)
        r.xi[channel] = jnp.where(inside, window[:, :CELLS], 0.0).astype(BF16)

    def gram_row(channel, x):
        base = geo[1 + channel : 2 + channel, :]
        return base, base + gram[channel][0] * x[0] + gram[channel][1] * x[1] + gram[channel][2] * x[2]

    for at in range(0, img, 16):
        x = [r.xi[channel, at : at + 16, :].astype(F32) for channel in range(3)]
        square = jnp.broadcast_to(geo[0:1, :], (16, CELLS))
        for channel in range(3):
            base, u = gram_row(channel, x)
            square = square + x[channel] * (base + u)
        r.ri[at : at + 16, :] = lax.rsqrt(square + TINY)
    for channel in range(3):
        r.xx[channel] = dot_nn(pick, r.xi[channel]).astype(BF16)
    inv_high, inv_low = split(r.ri[...])
    r.rr[...] = dot_nn(pick, inv_high) + dot_nn(pick, inv_low)

    def over_grid(code):
        return jnp.concatenate(split(code), axis=1)

    r.ss[...] = dot_nn(over_grid(query_code), r.ee[...])
    r.side[...] = query_code
    lane = lax.broadcasted_iota(jnp.int32, (tile, LANES), 1)
    place = lax.broadcasted_iota(jnp.int32, (tile, CELLS), 1).astype(F32)

    def side_columns(code, one, sums):
        made = jnp.where(lane == ONE, one, 0.0)
        for channel in range(3):
            made = made + jnp.where(lane == COLOR + channel, sums[channel], 0.0)
        return made

    def attend(at):
        code = r.side[at, :]
        x = [r.xx[channel, at, :].astype(F32) for channel in range(3)]
        inv = r.rr[at, :]
        raw = r.ss[at, :]
        for channel in range(3):
            raw = raw + code[:, COLOR + channel : COLOR + channel + 1] * x[channel]
        r.ss[at, :] = raw
        allowed = place < r.owner[at, :1]
        score = jnp.where(allowed, raw * inv + code[:, ONE : ONE + 1], FLOOR)
        top = jnp.max(score, axis=1, keepdims=True)
        raised = jnp.where(allowed, jnp.exp(score - top), 0.0)
        total = jnp.sum(raised, axis=1, keepdims=True)
        prob = raised / total
        r.pp[at, :] = prob
        weighted = prob * inv
        r.low[at, :] = weighted.astype(BF16)
        sums = [jnp.sum(weighted * x[channel], axis=1, keepdims=True) for channel in range(3)]
        r.side[at, :] = side_columns(code, jnp.sum(prob, axis=1, keepdims=True), sums)

    by_rows(attend)
    value_code = dot_nt(r.low[...], r.ee[:LANES, :]) + r.side[...]
    code_high, code_low = split(value_code)
    code_three = jnp.concatenate([code_high, code_high, code_low], axis=1)
    for j in range(0, width, 256):
        r.merged[:, j : j + 256] = dot_nn(code_three, r.tv[:, j : j + 256]).astype(BF16)
    value_code_low = code_high

    WO.wait()
    for j in range(0, width, 256):
        r.res[:, j : j + 256] = r.lat[:, j : j + 256].astype(F32) + dot_nn(r.merged[...], r.wo[:, j : j + 256])

    def norm_mid(at):
        x = r.res[at, :]
        center = x - jnp.mean(x, axis=-1, keepdims=True)
        inv = lax.rsqrt(jnp.mean(center * center, axis=-1, keepdims=True) + TINY)
        hat = center * inv
        r.xm[at, :] = hat
        r.rm[at, :] = jnp.broadcast_to(inv, (tile, LANES))
        r.nm[at, :] = (hat * mgain[...] + mshift[...]).astype(BF16)

    by_rows(norm_mid)
    WU.wait()
    for j in range(0, width, 256):
        pre = dot_nn(r.nm[...], r.wu[:, j : j + 256])
        phi = 0.5 * (1.0 + lax.erf(pre * math.sqrt(0.5)))
        r.act[:, j : j + 256] = (pre * phi).astype(BF16)
        slope = phi + pre * (jnp.exp(-0.5 * pre * pre) * (1.0 / math.sqrt(2.0 * math.pi)))
        r.bt[UP, mine, j : j + 256] = (r.ag[:, j : j + 256] * slope).astype(BF16)
    part_z = span_of(z, LANES)
    act_copies = exchange(
        n_batch, z, on_z, lambda target: r.act.at[:, span_of(target, tall)], lambda slot: r.az.at[part_z, :], r.az_s, r.az_r
    )
    r.az[part_z, :] = r.act[:, span_of(z, tall)]
    turn(UP, r.nm)
    send_left(UP)
    send_right(UP)
    turn(OUT, r.merged)
    send_left(OUT)

    for j in range(0, width, 256):
        r.nm[:, j : j + 256] = (r.res[:, j : j + 256] + dot_nn(r.act[...], r.wd[:, j : j + 256])).astype(BF16)
    leave(r.nm, o_mixed.at[0])
    for j in range(0, width, 256):
        r.ag[:, j : j + 256] = dot_nt(r.bt[UP, mine, :], r.wu[j : j + 256, :])
    product(UP)
    start(UP, 0)
    zero = jnp.zeros((1, width), F32)

    def norm_back(grad, hat, inv, gain):
        scaled = grad * gain
        return inv * (scaled - jnp.mean(scaled, axis=-1, keepdims=True) - hat * jnp.mean(scaled * hat, axis=-1, keepdims=True))

    def mid_back(i, carry):
        at = pl.ds(pl.multiple_of(i * tile, tile), tile)
        grad, hat = r.ag[at, :], r.xm[at, :]
        total = r.cot[at, :].astype(F32) + norm_back(grad, hat, r.rm[at, :1], mgain[...])
        r.res[at, :] = total
        r.bt[OUT, pl.ds(pl.multiple_of(c * LANES + i * tile, tile), tile), :] = total.astype(BF16)
        return carry[0] + jnp.sum(grad * hat, axis=0, keepdims=True), carry[1] + jnp.sum(grad, axis=0, keepdims=True)

    gain_sum, shift_sum = lax.fori_loop(0, LANES // tile, mid_back, (zero, zero))
    r.vec[...] = jnp.zeros_like(r.vec)
    r.vec[2:3, :] = gain_sum
    r.vec[3:4, :] = shift_sum
    send_right(OUT)
    for j in range(0, width, 256):
        r.da[:, j : j + 256] = dot_nt(r.bt[OUT, mine, :], r.wo[j : j + 256, :]).astype(BF16)

    back_code = dot_nt(r.da[...], r.tv[: 2 * LANES, :])
    back_code = back_code[:, :LANES] + back_code[:, LANES:]
    r.ag[...] = dot_nn(over_grid(back_code), r.ee[...])
    r.side[...] = back_code

    def attend_back(at):
        code = r.side[at, :]
        x = [r.xx[channel, at, :].astype(F32) for channel in range(3)]
        inv = r.rr[at, :]
        prob = r.pp[at, :]
        raw = r.ag[at, :]
        for channel in range(3):
            raw = raw + code[:, COLOR + channel : COLOR + channel + 1] * x[channel]
        grad = raw * inv + code[:, ONE : ONE + 1]
        delta = jnp.sum(prob * grad, axis=1, keepdims=True)
        back = prob * (grad - delta)
        r.ye[at, :] = (back * r.ss[at, :] + prob * raw).astype(BF16)
        weighted = back * inv
        r.low[at, :] = weighted.astype(BF16)
        r.dp[at, :] = back.astype(BF16)
        sums = [jnp.sum(weighted * x[channel], axis=1, keepdims=True) for channel in range(3)]
        r.side[at, :] = side_columns(code, jnp.sum(back, axis=1, keepdims=True), sums)

    by_rows(attend_back)
    r.dp[LANES:, :] = r.pp[...].astype(BF16)
    key_code = (dot_nt(r.low[...], r.ee[:LANES, :]) + r.side[...]) * scale
    code_high, code_low = split(key_code)
    code_three = jnp.concatenate([code_high, code_high, code_low], axis=1)
    for j in range(0, width, 256):
        r.bt[QUERY, mine, j : j + 256] = dot_nn(code_three, r.tk[:, j : j + 256]).astype(BF16)
    if apart:
        part_p = span_of(spot, LANES)
        piece = width // plane
        query_copies = exchange(
            plane, spot, in_plane, lambda target: r.bt.at[QUERY, mine, span_of(target, piece)], lambda slot: r.qp.at[part_p, :],
            r.qp_s, r.qp_r,
        )
        r.qp[part_p, :] = r.bt[QUERY, mine, span_of(spot, piece)]
    else:
        send_right(QUERY)
    product(OUT)
    start(OUT, 0)
    step(UP, 0)

    for j in range(0, width, 256):
        r.ag[:, j : j + 256] = dot_nt(r.bt[QUERY, mine, :], r.wq[j : j + 256, :])

    def latents_back(i, carry):
        at = pl.ds(pl.multiple_of(i * tile, tile), tile)
        grad, hat = r.ag[at, :], r.xl[at, :]
        r.res[at, :] = r.res[at, :] + norm_back(grad, hat, r.rl[at, :1], qgain[...])
        return carry[0] + jnp.sum(grad * hat, axis=0, keepdims=True), carry[1] + jnp.sum(grad, axis=0, keepdims=True)

    gain_sum, shift_sum = lax.fori_loop(0, LANES // tile, latents_back, (zero, zero))
    r.vec[0:1, :] = gain_sum
    r.vec[1:2, :] = shift_sum
    leave(r.res, o_lat.at[0])
    if apart:
        wait_all(norm_copies)
        wait_all(query_copies)
        for j in range(0, width, 256):
            made = dot_tn(r.qp[...], r.np[:, j : j + 256]).astype(BF16)
            r.qc[:, :, j : j + 256] = made.reshape(2, width // n_seq, 256)
        to_core("q", 6, r.qc.at[1 - c], r.qcr)
    else:
        product(QUERY)
        start(QUERY, 0)

    heap = 256 // (2 * rows * parts["c"])
    for j in range(0, 2 * width, 256):
        if j < width:
            made = dot_tn(r.q[:, j : j + 256], code_high)
        else:
            made = dot_tn(r.da[:, j - width : j - width + 256], value_code_low)
        riding = pltpu.roll(r.vec[:, j // 2 : j // 2 + LANES].T, ONE + 1, 1).reshape(-1, rows, LANES)
        made = made.reshape(-1, 2 * rows, LANES)
        made = jnp.concatenate([made[:, :rows] + riding, made[:, rows:]], axis=1)
        r.zc[heap * (j // 256) : heap * (j // 256 + 1)] = made.astype(BF16).reshape(heap, parts["c"], 2 * rows, LANES)
    to_core("z", 8, r.zc.at[:, part("c", 1 - c)], r.zcr)
    if apart:
        core_copies.pop("q").wait()
        r.qcr[...] = (r.qc[c].astype(F32) + r.qcr[...].astype(F32)).astype(BF16)
        sum_copies = exchange(
            n_batch, z, on_z, lambda target: r.qcr.at[:, span_of(target, tall)], lambda slot: r.qz.at[slot], r.qz_s, r.qz_r
        )
    wait_all(cot_copies)
    wait_all(act_copies)
    for j in range(0, width, 256):
        made = dot_tn(r.az[...], r.gz[:, j : j + 256]).astype(BF16)
        r.dc[:, :, :, :, j : j + 256] = made.reshape(parts["a"], parts["b"], parts["c"], rows, 256)
    to_core("d", 7, r.dc.at[:, :, part("c", 1 - c)], r.dcr)

    in_gain, in_shift = jnp.zeros((feat, 1), F32), jnp.zeros((feat, 1), F32)
    for j in range(0, 2 * width, 256):
        sums = r.zc[heap * (j // 256) : heap * (j // 256 + 1)].reshape(256, LANES)
        spread = dot_nt(r.fct[...], jnp.concatenate([sums, sums], axis=1))
        factor = r.kvw[:, j : j + 256].astype(F32)
        in_gain = in_gain + jnp.sum(factor * spread[:feat], axis=1, keepdims=True)
        in_shift = in_shift + jnp.sum(factor * spread[wide : wide + 1], axis=1, keepdims=True)
    for at, column in ((0, in_gain), (1, in_shift)):
        for j in range(0, feat, LANES):
            some = min(LANES, feat - j)
            eye = lax.broadcasted_iota(jnp.int32, (some, LANES), 0) == lax.broadcasted_iota(jnp.int32, (some, LANES), 1)
            r.ar[0, at : at + 1, j : j + LANES] = jnp.sum(jnp.where(eye, column[j : j + some], 0.0), axis=0, keepdims=True)
    seq_copies = []
    for offset in range(1, n_seq):
        slot = n_seq - offset - 1
        copy = pltpu.make_async_remote_copy(
            src_ref=r.ar.at[0], dst_ref=r.ars.at[slot], send_sem=r.as_s.at[offset - 1], recv_sem=r.as_r.at[slot],
            device_id=(z, lax.rem(s + offset, n_seq)), device_id_type=MESH,
        )
        copy.start()
        seq_copies.append(copy)
    core_copies.pop("z").wait()
    both = r.zc[:, part("c", c)].astype(F32) + r.zcr[...].astype(F32)
    r.zs0[0] = both.astype(BF16).reshape(parts["z"], parts["a"], parts["b"], 2 * rows, LANES)
    start(SUMS, 0)
    core_copies.pop("d").wait()
    r.ds0[0, 0] = (r.dc[:, :, part("c", c)].astype(F32) + r.dcr[...].astype(F32)).astype(BF16)
    start(DOWN, 0)

    query_t, back_t = query_code.T, back_code.T
    lifted = jnp.concatenate(
        [
            jnp.concatenate([pick_t * code_t[COLOR + channel : COLOR + channel + 1, :] for code_t in (query_t, back_t)], axis=1)
            for channel in range(3)
        ],
        axis=0,
    ).astype(BF16)
    along = dot_nn(pick_t.astype(BF16), r.ye[...])
    inv = r.ri[...]
    cube = inv * inv * inv * along
    colors = [r.xi[channel].astype(F32) for channel in range(3)]
    for channel in range(3):
        steep = dot_nn(lifted[channel * img : (channel + 1) * img], r.dp[...])
        own_grad = inv * steep - cube * gram_row(channel, colors)[1]
        window = jnp.concatenate([own_grad, jnp.zeros((img, LANES), F32)], axis=1)
        for bit in range(7):
            hop = 1 << bit
            moved = pltpu.roll(window, hop, 1)
            window = jnp.where((shift_of & hop) != 0, moved, window)
        for j in range(9):
            r.pg[j * img : (j + 1) * img, :] = window[:, j * LANES : (j + 1) * LANES]
        grad_high, grad_low = split(r.pg[...])
        r.pgs[channel] = dot_tn(r.sel[...], grad_high) + dot_tn(r.sel[...], grad_low)
    grad_copies = []
    for offset in range(1, n_seq):
        target = lax.rem(s + offset, n_seq)
        copy = pltpu.make_async_remote_copy(
            src_ref=r.pgs.at[:, pl.ds(pl.multiple_of(target * blocks, blocks), blocks), :],
            dst_ref=r.pgr.at[n_seq - offset - 1],
            send_sem=r.pg_s.at[offset - 1], recv_sem=r.pg_r.at[n_seq - offset - 1],
            device_id=(z, target), device_id_type=MESH,
        )
        copy.start()
        grad_copies.append(copy)

    step(UP, 1)
    if apart:
        wait_all(sum_copies)
        made = gathered(r.qcr[:, span_of(z, tall)], r.qz, n_batch)
        for j in range(0, tall, LANES):
            r.qt[j : j + LANES, :] = made[:, j : j + LANES].T
        few = tall // n_seq
        part_q = r.qo.at[:, span_of(s, LANES)]
        last_copies = exchange(
            n_seq, s, in_row, lambda target: r.qt.at[span_of(target, few), :], lambda slot: part_q, r.qo_s, r.qo_r
        )
        r.qo[:, span_of(s, LANES)] = r.qt[span_of(s, few), :]
    else:
        step(QUERY, 0)
    step(OUT, 0)
    step(SUMS, 0)
    step(DOWN, 0)
    wait_all(seq_copies)
    r.ar[1] = gathered(r.ar[0], r.ars, n_seq)
    z_copies = exchange(n_batch, z, on_z, lambda target: r.ar.at[1], lambda slot: r.arz.at[slot], r.ab_s, r.ab_r)
    step(OUT, 1)
    step(SUMS, 1)
    if not apart:
        step(QUERY, 1)

    total_rows = width // (n_batch * n_seq)
    inner = 0
    for name in ("a", "b", "c"):
        if parts[name] < sizes[name]:
            inner = inner * sizes[name] + here[name]

    def finish(mat, made):
        step(mat, 1 if mat == DOWN else 2)
        if total_rows < rows:
            r.out[mat] = pltpu.roll(r.out[mat], lax.rem(rows - inner * total_rows, rows), 0)
        leave(r.out.at[mat, :total_rows], made)

    wait_all(grad_copies)
    o_pix[...] = gathered(r.pgs[:, own, :], r.pgr, n_seq)
    finish(DOWN, o_wd)
    finish(UP, o_wu)
    if apart:
        wait_all(last_copies)
        leave(r.qo, o_wq)
    else:
        finish(QUERY, o_wq)
    wait_all(z_copies)
    o_in[...] = gathered(r.ar[1], r.arz, n_batch)[:, :feat]
    finish(OUT, o_wo)
    step(SUMS, 2)
    sums = r.zout[...]
    turned = sums
    if total_rows < rows:
        turned = pltpu.roll(sums, lax.rem(rows - inner * total_rows, rows), 0)
        sums = pltpu.roll(sums, lax.rem(2 * (rows - inner * total_rows), 2 * rows), 0)
    high, low = split(sums)
    code_high, code_low = split(r.mt[...].T)
    spread_left = jnp.concatenate([code_high, code_high, code_low], axis=1)
    o_kv[...] = dot_nt(jnp.concatenate([high, low, high], axis=1), spread_left)[: 2 * total_rows, :feat]
    square = jnp.concatenate([turned, jnp.zeros((LANES - 2 * rows, LANES), F32)], axis=0)
    o_vec[...] = square.T[COLOR : COLOR + 8, :total_rows]
    wait_all(leaving)


def hand_over(mixed, lat, pix, vec, wq, inner, kv, wo, wu, wd, *refs):
    o_mixed, o_lat, o_pix, o_qg, o_qs, o_wq, o_ig, o_is, o_kv, o_wo, o_mg, o_ms, o_wu, o_wd = refs
    for src, dst in ((mixed, o_mixed), (lat, o_lat), (wq, o_wq), (wo, o_wo), (wu, o_wu), (wd, o_wd), (kv, o_kv)):
        dst[...] = src[...]
    for channel in range(3):
        for j in range(pix.shape[1]):
            o_pix[channel, 0:1, j * LANES : (j + 1) * LANES] = pix[channel, j : j + 1, :]
    for i, dst in enumerate((o_qg, o_qs, o_mg, o_ms)):
        dst[...] = vec[4 + i, :]
    for i, dst in enumerate((o_ig, o_is)):
        dst[...] = inner[i, :]


def solution(mesh):
    n_batch, n_seq = mesh.shape["batch"], mesh.shape["seq"]

    def body(latents, pixels, counts, latent_image, query_gain, query_shift, query_weight, input_gain, input_shift,
             kv_weight, out_weight, mlp_gain, mlp_shift, up_weight, down_weight, cotangent):
        width = query_weight.shape[0]
        feat = kv_weight.shape[0]
        pix_dev = pixels.shape[2]
        n_img = counts.shape[1]
        fc, geo, fct, gram = position_tables(feat)
        scratch = shapes_of(n_batch, n_seq, width, pix_dev, n_img, feat)
        rows = width // (n_batch * n_seq)
        vm = pl.BlockSpec(memory_space=pltpu.VMEM)
        hbm = pl.BlockSpec(memory_space=pl.ANY)
        f32 = lambda *shape: jax.ShapeDtypeStruct(shape, F32)
        mixed, latent_grad, square = jax.ShapeDtypeStruct(latents.shape, BF16), f32(*latents.shape), f32(rows, width)
        kv = f32(2 * rows, feat)
        args = (
            latents, pixels, counts, latent_image,
            query_gain[None], query_shift[None], query_weight, input_gain, input_shift, kv_weight,
            out_weight, mlp_gain[None], mlp_shift[None], up_weight, down_weight, cotangent,
            jnp.asarray(fc), jnp.asarray(geo), jnp.asarray(fct),
        )
        in_hbm = (0, 6, 9, 10, 13, 14, 15, 16, 18)
        big = (0, 1, 4, 7, 8, 9)
        made = pl.pallas_call(
            functools.partial(layer, n_batch, n_seq, width, n_img, feat, gram),
            out_shape=(
                mixed, latent_grad, f32(3, pix_dev // LANES, LANES), f32(8, rows), square, f32(2, feat), kv, square, square, square,
            ),
            in_specs=[hbm if i in in_hbm else vm for i in range(len(args))],
            out_specs=[hbm if i in big else vm for i in range(10)],
            scratch_shapes=[vars(scratch)],
            compiler_params=pltpu.CompilerParams(
                collective_id=0, has_side_effects=True, vmem_limit_bytes=60 * 1024 * 1024
            ),
            name="layer",
        )(*args)
        out_shape = (
            mixed, latent_grad, f32(3, 1, pix_dev), f32(rows), f32(rows), square, f32(feat), f32(feat), kv, square,
            f32(rows), f32(rows), square, square,
        )
        out = pl.pallas_call(
            hand_over,
            out_shape=out_shape,
            in_specs=[vm] * len(made),
            out_specs=[vm] * len(out_shape),
            name="hand_over",
        )(*made)
        return (*out[:2], out[2].transpose(1, 0, 2), *out[3:8], out[8].T, *out[9:])

    whole, vec = P(("batch", "seq"), None), P(("batch", "seq"))
    rowed = P("batch", "seq", None)
    return jax.shard_map(
        body,
        mesh=mesh,
        in_specs=(rowed, P("batch", None, "seq"), P("batch", None), P("batch", None)) + (P(),) * 11 + (rowed,),
        out_specs=(
            rowed, rowed, P("batch", None, "seq"), vec, vec, whole, P(), P(), P(None, ("batch", "seq")), whole,
            vec, vec, whole, whole,
        ),
        check_vma=False,
    )
```

```python
import functools
import math
from types import SimpleNamespace

import jax
import jax.numpy as jnp
import numpy as np
from jax import lax
from jax.experimental import pallas as pl
from jax.experimental.pallas import tpu as pltpu
from jax.sharding import PartitionSpec as P

IMG_W = 32
TOP_FREQ = 112.0
TINY = 1e-05
FLOOR = -1e30
MESH = pl.DeviceIdType.MESH
F32 = jnp.float32
BF16 = jnp.bfloat16
LANES = 128
CELLS = IMG_W * IMG_W
COLOR = 2 * IMG_W
ONE = COLOR + 3


def position_tables(feat):
    bands = (feat - 5) // 4
    freq = np.linspace(1.0, TOP_FREQ, bands).astype(np.float32)
    grid = (np.float32(2.0) * np.arange(IMG_W, dtype=np.float32) / np.float32(IMG_W - 1) - np.float32(1.0)).astype(np.float32)
    phase = ((np.float32(math.pi) * grid)[:, None] * freq[None, :]).astype(np.float64)
    table = np.zeros((LANES, feat), np.float64)
    for axis in range(2):
        rows = slice(axis * IMG_W, (axis + 1) * IMG_W)
        table[rows, 3 + axis] = grid
        table[rows, 5 + axis * bands : 5 + (axis + 1) * bands] = np.sin(phase)
        table[rows, 5 + (2 + axis) * bands : 5 + (3 + axis) * bands] = np.cos(phase)
    for channel in range(3):
        table[COLOR + channel, channel] = 1.0
    centered = table - table.mean(axis=1, keepdims=True)
    gram = centered @ centered.T / feat
    place = np.arange(CELLS)
    row, col = place // IMG_W, IMG_W + place % IMG_W
    geometry = np.zeros((8, CELLS), np.float32)
    geometry[0] = gram[row, row] + gram[col, col] + 2.0 * gram[row, col]
    for channel in range(3):
        geometry[1 + channel] = gram[COLOR + channel, row] + gram[COLOR + channel, col]
    wide = -(-feat // LANES) * LANES
    padded = np.zeros((LANES, wide), np.float32)
    padded[:, :feat] = centered
    turned = np.zeros((wide + 8, LANES), np.float32)
    turned[:feat] = centered.T
    turned[wide, ONE] = 1.0
    high = turned.astype(jnp.bfloat16)
    low = (turned - high.astype(np.float32)).astype(jnp.bfloat16)
    colors = gram[COLOR : COLOR + 3, COLOR : COLOR + 3]
    return padded, geometry, np.concatenate([high, low], axis=1), [[float(v) for v in line] for line in colors]


def split(values):
    high = values.astype(BF16)
    return high, (values - high.astype(F32)).astype(BF16)


def dot_nn(left, right):
    return jnp.dot(left, right, preferred_element_type=F32)


def dot_nt(left, right):
    return lax.dot_general(left, right, (((1,), (1,)), ((), ())), preferred_element_type=F32)


def dot_tn(left, right):
    return lax.dot_general(left, right, (((0,), (0,)), ((), ())), preferred_element_type=F32)


def plan(n_batch, n_seq, width):
    core = 2
    fast = math.isqrt(n_seq // core)
    while (n_seq // core) % fast:
        fast -= 1
    slow = n_seq // core // fast
    sizes = {"z": n_batch, "a": slow, "b": fast, "c": core}
    parts, left = dict(sizes), width
    for name in ("c", "b", "a"):
        if width // math.prod(parts.values()) < 16:
            parts[name] = 1
    orders = (("b", "a") if parts["b"] > 1 else ("a", "b"), ("a", "b"))
    return sizes, parts, width // math.prod(parts.values()), orders


def by_columns(n_seq, width):
    return width // n_seq % LANES == 0


def shapes_of(n_batch, n_seq, width, pix_dev, n_img, feat):
    sizes, parts, rows, orders = plan(n_batch, n_seq, width)
    img = -(-n_img // 16) * 16
    blocks = pix_dev // LANES
    wide = -(-feat // LANES) * LANES
    factor_rows = (width // (2 * rows), 2, rows) if parts["c"] > 1 else (1, 1, width)
    S = SimpleNamespace()
    vm = lambda *shape, dtype=BF16: pltpu.VMEM(shape, dtype)
    S.wq, S.wo, S.wu, S.wd = [vm(width, width)] * 4
    S.tk = vm(3 * LANES, width)
    S.tv = vm(3 * LANES, width)
    S.ee = vm(2 * LANES, CELLS)
    S.mt = vm(LANES, wide, dtype=F32)
    S.xl, S.xm, S.res, S.ag = [vm(LANES, width, dtype=F32)] * 4
    S.rl = vm(LANES, LANES, dtype=F32)
    S.rm = vm(LANES, LANES, dtype=F32)
    S.nl, S.q, S.merged, S.nm, S.act, S.da = [vm(LANES, width)] * 6
    S.pb = vm(3, n_seq * blocks, LANES)
    S.sel = vm(9 * img, n_seq * blocks)
    S.xi = vm(3, img, CELLS)
    S.ri = vm(img, CELLS, dtype=F32)
    S.xx = vm(3, LANES, CELLS)
    S.rr = vm(LANES, CELLS, dtype=F32)
    S.ss = vm(LANES, CELLS, dtype=F32)
    S.pp = vm(LANES, CELLS, dtype=F32)
    S.low = vm(LANES, CELLS)
    S.dp = vm(2 * LANES, CELLS)
    S.ye = vm(LANES, CELLS)
    S.side = vm(LANES, LANES, dtype=F32)
    S.owner = vm(LANES, LANES, dtype=F32)
    S.pg = vm(9 * img, LANES, dtype=F32)
    S.pgs = vm(3, n_seq * blocks, LANES, dtype=F32)
    S.pgr = vm(n_seq - 1, 3, blocks, LANES, dtype=F32)
    tall, plane, apart = width // n_batch, n_seq // 2, by_columns(n_seq, width)
    full = 2 if apart else 3
    S.at = vm(full, *factor_rows, 2 * LANES)
    S.bt = vm(3, 2 * LANES, width)
    S.ms0 = vm(full, parts["z"], parts["a"], parts["b"], rows, width)
    S.ds0 = vm(1, 1, parts["a"], parts["b"], rows, width)
    S.zs0 = vm(1, parts["z"], parts["a"], parts["b"], 2 * rows, LANES)
    S.mr, S.dr, S.zr = [], [], []
    for made, mats, deep, across in ((S.mr, full, parts["z"], width // 2), (S.dr, 1, 1, width // 2), (S.zr, 1, parts["z"], LANES)):
        for first, other in orders:
            made.append([
                vm(mats, sizes[first] - 1, deep, parts[other], rows, across),
                vm(mats, sizes[other] - 1, deep, rows, across),
            ] + [vm(mats, sizes["z"] - 1, rows, across)] * (deep > 1))
    S.gz, S.az = vm(n_batch * LANES, width), vm(n_batch * LANES, tall)
    S.dc = vm(parts["a"], parts["b"], parts["c"], rows, width)
    S.dcr = vm(parts["a"], parts["b"], rows, width)
    if apart:
        S.np, S.qp = vm(plane * LANES, width), vm(plane * LANES, width // plane)
        S.qc, S.qcr = vm(2, width // n_seq, width), vm(width // n_seq, width)
        S.qz = vm(n_batch - 1, width // n_seq, tall)
        S.qt = vm(tall, width // n_seq, dtype=F32)
        S.qo = vm(tall // n_seq, width, dtype=F32)
    S.zc = vm(width // (rows * parts["c"]), parts["c"], 2 * rows, LANES)
    S.zcr = vm(width // (rows * parts["c"]), 2 * rows, LANES)
    S.vec = vm(LANES, width, dtype=F32)
    S.out = vm(4, rows, width, dtype=F32)
    S.zout = vm(2 * rows, LANES, dtype=F32)
    S.ar = vm(2, 2, wide, dtype=F32)
    S.ars = vm(n_seq - 1, 2, wide, dtype=F32)
    S.arz = vm(n_batch - 1, 2, wide, dtype=F32)
    S.lat, S.cot = [vm(LANES, width)] * 2
    S.kvw = vm(feat, 2 * width)
    S.fc = vm(LANES, wide, dtype=F32)
    S.fct = vm(wide + 8, 2 * LANES)
    most = max(sizes.values()) - 1
    sem = lambda *shape: pltpu.SemaphoreType.DMA(shape)
    S.w_sem = sem(9)
    S.o_sem = sem(6)
    S.px_s, S.px_r = sem(n_seq - 1), sem(n_seq - 1)
    S.pg_s, S.pg_r = sem(n_seq - 1), sem(n_seq - 1)
    S.co_s, S.co_r = sem(9), sem(9)
    S.gz_s, S.gz_r, S.az_s, S.az_r, S.qz_s, S.qz_r = [sem(n_batch - 1)] * 6
    S.np_s, S.np_r, S.qp_s, S.qp_r = [sem(plane - 1)] * 4
    S.qo_s, S.qo_r = [sem(n_seq - 1)] * 2
    S.rs_s, S.rs_r = sem(5, 2, 3, most), sem(5, 2, 3, most)
    S.as_s, S.as_r = sem(n_seq - 1), sem(n_seq - 1)
    S.ab_s, S.ab_r = sem(n_batch - 1), sem(n_batch - 1)
    return S


def layer(
    n_batch, n_seq, width, n_img, feat, gram,
    h_lat, px, cnt, img_of, qgain, qshift, h_wq, igain, ishift, h_kvw, h_wo, mgain, mshift, h_wu, h_wd, h_cot, h_fc, geo, h_fct,
    o_mixed, o_lat, o_pix, o_vec, o_wq, o_in, o_kv, o_wo, o_wu, o_wd, r,
):
    r = SimpleNamespace(**r)
    sizes, parts, rows, orders = plan(n_batch, n_seq, width)
    img = r.xi.shape[1]
    blocks = px.shape[2] // LANES
    wide = r.mt.shape[1]
    span = CELLS + LANES
    scale = width ** (-0.5)

    z = lax.axis_index("batch")
    s = lax.axis_index("seq")
    c = lax.rem(s, 2)
    b = lax.rem(s // 2, sizes["b"])
    a = s // (2 * sizes["b"])
    here = {"z": z, "a": a, "b": b, "c": c}

    def device(**moved):
        at = {**here, **moved}
        return (at["z"], (at["a"] * sizes["b"] + at["b"]) * 2 + at["c"])

    def part(name, index):
        return index if parts[name] > 1 else 0

    def peer(name, offset):
        return lax.rem(here[name] + offset, sizes[name])

    barrier = pltpu.get_barrier_semaphore()
    for offset in range(1, n_seq):
        pl.semaphore_signal(barrier, inc=1, device_id=(z, lax.rem(s + offset, n_seq)), device_id_type=MESH)
    for offset in range(1, n_batch):
        pl.semaphore_signal(barrier, inc=1, device_id=(peer("z", offset), s), device_id_type=MESH)

    arriving = []
    for i, (src, dst) in enumerate((
        (h_lat.at[0], r.lat), (h_fc, r.fc), (h_kvw, r.kvw), (h_wq, r.wq), (h_cot.at[0], r.cot), (h_wd, r.wd),
        (h_wo, r.wo), (h_wu, r.wu), (h_fct, r.fct),
    )):
        copy = pltpu.make_async_copy(src, dst, r.w_sem.at[i])
        copy.start()
        arriving.append(copy)
    LAT, FC, KVW, WQ, COT, WD, WO, WU, FCT = arriving
    leaving = []

    def leave(src, dst):
        copy = pltpu.make_async_copy(src, dst, r.o_sem.at[len(leaving)])
        copy.start()
        leaving.append(copy)

    UP, OUT, QUERY, DOWN, SUMS = range(5)
    apart = by_columns(n_seq, width)
    tall, plane = width // n_batch, n_seq // 2
    tile = 16

    def by_rows(step):
        def run(i, carry):
            step(pl.ds(pl.multiple_of(i * tile, tile), tile))
            return carry

        lax.fori_loop(0, LANES // tile, run, 0, unroll=8)

    mine = pl.ds(pl.multiple_of(c * LANES, LANES), LANES)

    def turn(which, factor):
        for j in range(width // LANES):
            block = factor[:, j * LANES : (j + 1) * LANES].astype(F32).T.astype(BF16)
            if parts["c"] > 1:
                deep = LANES // (2 * rows)
                r.at[which, j * deep : (j + 1) * deep, :, :, mine] = block.reshape(deep, 2, rows, LANES)
            else:
                r.at[which, 0, 0, j * LANES : (j + 1) * LANES, mine] = block

    core_copies = {}

    def to_core(key, index, src, dst):
        copy = pltpu.make_async_remote_copy(
            src_ref=src, dst_ref=dst, send_sem=r.co_s.at[index], recv_sem=r.co_r.at[index],
            device_id=device(c=1 - c), device_id_type=MESH,
        )
        copy.start()
        core_copies[key] = copy

    def send_left(which):
        ref = r.at.at[which, :, part("c", 1 - c), :, mine]
        to_core(("left", which), 2 * which, ref, ref)

    def send_right(which):
        ref = r.bt.at[which, mine, :]
        to_core(("right", which), 2 * which + 1, ref, ref)

    def start_stage(key, stage, name, src_of, dst):
        mat, half = key
        copies = []
        for offset in range(1, sizes[name]):
            target = peer(name, offset)
            slot = sizes[name] - offset - 1
            copy = pltpu.make_async_remote_copy(
                src_ref=src_of(part(name, target)), dst_ref=dst.at[slot],
                send_sem=r.rs_s.at[mat, half, stage, offset - 1], recv_sem=r.rs_r.at[mat, half, stage, slot],
                device_id=device(**{name: target}), device_id_type=MESH,
            )
            copy.start()
            copies.append(copy)
        return copies

    def wait_all(copies):
        for copy in copies:
            copy.wait()

    def gathered(own, dst, n):
        total = own.astype(F32)
        for slot in range(n - 1):
            total = total + dst[slot].astype(F32)
        return total

    flying = {}

    def buffers_of(mat):
        if mat == DOWN:
            return r.ds0, r.dr, 0
        return (r.zs0, r.zr, 0) if mat == SUMS else (r.ms0, r.mr, mat)

    def cut(mat, half):
        if mat == SUMS:
            return pl.ds(half * rows, rows), slice(None)
        return slice(None), pl.ds(half * (width // 2), width // 2)

    def blocks_at(mat, half, stage, target=None):
        s0, received, i = buffers_of(mat)
        at = {"z": slice(None), "a": slice(None), "b": slice(None)}
        path = orders[half] + ("z",)
        for done in path[:stage]:
            at[done] = part(done, here[done])
        at[path[stage]] = part(path[stage], here[path[stage]]) if target is None else target
        return (i, at["z"], at["a"], at["b"]) + cut(mat, half)

    def start(mat, stage):
        s0, received, i = buffers_of(mat)
        for half in range(2):
            name = (orders[half] + ("z",))[stage]
            flying[mat, half] = start_stage(
                (mat, half), stage, name,
                lambda p: s0.at[blocks_at(mat, half, stage, p)],
                received[half][stage].at[i],
            )

    def step(mat, stage):
        s0, received, i = buffers_of(mat)
        last = 1 if mat == DOWN else 2
        for half in range(2):
            wait_all(flying[mat, half])
            name = (orders[half] + ("z",))[stage]
            keep = blocks_at(mat, half, stage)
            total = gathered(s0[keep], received[half][stage].at[i], sizes[name])
            if stage < last:
                s0[keep] = total.astype(BF16)
            elif mat == SUMS:
                r.zout[cut(mat, half)] = total
            else:
                r.out[(mat,) + cut(mat, half)] = total[0] if mat == DOWN else total
        if stage < last:
            start(mat, stage + 1)

    def exchange(n, index, device_at, src_of, dst, sends, receives):
        copies = []
        for offset in range(1, n):
            target = lax.rem(index + offset, n)
            copy = pltpu.make_async_remote_copy(
                src_ref=src_of(target), dst_ref=dst(n - offset - 1), send_sem=sends.at[offset - 1],
                recv_sem=receives.at[n - offset - 1], device_id=device_at(target), device_id_type=MESH,
            )
            copy.start()
            copies.append(copy)
        return copies

    def span_of(index, size):
        return pl.ds(pl.multiple_of(index * size, size), size)

    on_z = lambda target: (target, s)
    in_plane = lambda target: (z, target * 2 + c)
    in_row = lambda target: (z, target)
    spot = s // 2

    def product(mat):
        core_copies.pop(("left", mat)).wait()
        core_copies.pop(("right", mat)).wait()
        left = r.at[mat, :, part("c", c)].reshape(-1, 2 * LANES)
        for j in range(0, width, 256):
            made = dot_nn(left, r.bt[mat, :, j : j + 256]).astype(BF16)
            r.ms0[mat, :, :, :, :, j : j + 256] = made.reshape(parts["z"], parts["a"], parts["b"], rows, 256)

    def norm_latents(at):
        x = r.lat[at, :].astype(F32)
        center = x - jnp.mean(x, axis=-1, keepdims=True)
        inv = lax.rsqrt(jnp.mean(center * center, axis=-1, keepdims=True) + TINY)
        hat = center * inv
        r.xl[at, :] = hat
        r.rl[at, :] = jnp.broadcast_to(inv, (tile, LANES))
        r.nl[at, :] = (hat * qgain[...] + qshift[...]).astype(BF16)

    LAT.wait()
    by_rows(norm_latents)
    COT.wait()
    r.gz[span_of(z, LANES), :] = r.cot[...]
    if apart:
        r.np[span_of(spot, LANES), :] = r.nl[...]
    else:
        turn(QUERY, r.nl)

    own = pl.ds(pl.multiple_of(s * blocks, blocks), blocks)
    colors = px[0].astype(F32)
    for channel in range(3):
        line = colors[channel : channel + 1]
        stacked = jnp.concatenate([line[:, j * LANES : (j + 1) * LANES] for j in range(blocks)], axis=0)
        r.pb[channel, own, :] = stacked.astype(BF16)
    pl.semaphore_wait(barrier, n_seq - 1 + n_batch - 1)
    pixel_copies = []
    for offset in range(1, n_seq):
        copy = pltpu.make_async_remote_copy(
            src_ref=r.pb.at[:, own, :], dst_ref=r.pb.at[:, own, :],
            send_sem=r.px_s.at[offset - 1], recv_sem=r.px_r.at[n_seq - offset - 1],
            device_id=(z, lax.rem(s + offset, n_seq)), device_id_type=MESH,
        )
        copy.start()
        pixel_copies.append(copy)
    if apart:
        own_norm = r.np.at[span_of(spot, LANES), :]
        norm_copies = exchange(plane, spot, in_plane, lambda target: own_norm, lambda slot: own_norm, r.np_s, r.np_r)
    else:
        send_left(QUERY)
    own_cot = r.gz.at[span_of(z, LANES), :]
    cot_copies = exchange(n_batch, z, on_z, lambda target: own_cot, lambda slot: own_cot, r.gz_s, r.gz_r)

    FCT.wait()
    FC.wait()
    KVW.wait()
    row_of = lax.broadcasted_iota(jnp.int32, (LANES, feat), 0)
    code = r.fc[:, :feat] * igain[...][None] + jnp.where(row_of == ONE, ishift[...][None], 0.0)
    r.mt[...] = jnp.zeros_like(r.mt)
    r.mt[:, :feat] = code
    code_high, code_low = split(code)
    code_both = jnp.concatenate([code_high, code_low], axis=0)
    for table, base in ((r.tk, 0), (r.tv, width)):
        for j in range(0, width, 256):
            both = dot_nn(code_both, r.kvw[:, base + j : base + j + 256])
            high, low = split(both[:LANES] + both[LANES:])
            table[:LANES, j : j + 256] = high
            table[LANES : 2 * LANES, j : j + 256] = low
            table[2 * LANES :, j : j + 256] = high
    cell = lax.broadcasted_iota(jnp.int32, (LANES, CELLS), 1)
    line = lax.broadcasted_iota(jnp.int32, (LANES, CELLS), 0)
    hit = (line == cell // IMG_W) | (line == IMG_W + lax.rem(cell, IMG_W))
    grid_code = jnp.where(hit, 1.0, 0.0).astype(BF16)
    r.ee[:LANES, :] = grid_code
    r.ee[LANES:, :] = grid_code

    WQ.wait()
    for j in range(0, width, 256):
        r.q[:, j : j + 256] = dot_nn(r.nl[...], r.wq[:, j : j + 256]).astype(BF16)
    query_code = dot_nt(r.q[...], r.tk[: 2 * LANES, :])
    query_code = (query_code[:, :LANES] + query_code[:, LANES:]) * scale

    WD.wait()
    for j in range(0, width, 256):
        r.ag[:, j : j + 256] = dot_nt(r.cot[...], r.wd[j : j + 256, :])

    counts_row = cnt[...].astype(F32)
    number = lax.broadcasted_iota(jnp.int32, (img, n_img), 0)
    against = lax.broadcasted_iota(jnp.int32, (img, n_img), 1)
    counts_all = jnp.broadcast_to(counts_row, (img, n_img))
    first = jnp.sum(jnp.where(against < number, counts_all, 0.0), axis=1, keepdims=True).astype(jnp.int32)
    count = jnp.sum(jnp.where(against == number, counts_all, 0.0), axis=1, keepdims=True).astype(jnp.int32)
    block_of = first // LANES
    shift_of = lax.rem(first, LANES)
    block_id = lax.broadcasted_iota(jnp.int32, (img, n_seq * blocks), 1)
    for j in range(9):
        r.sel[j * img : (j + 1) * img, :] = jnp.where(block_id == block_of + j, 1.0, 0.0).astype(BF16)

    mine_lat = pl.ds(pl.multiple_of(s * LANES, LANES), LANES)
    owner_row = img_of[:, mine_lat].astype(F32)
    square0 = lax.broadcasted_iota(jnp.int32, (LANES, LANES), 0)
    square1 = lax.broadcasted_iota(jnp.int32, (LANES, LANES), 1)
    diagonal = square0 == square1
    owner = jnp.sum(jnp.where(diagonal, jnp.broadcast_to(owner_row, (LANES, LANES)), 0.0), axis=1, keepdims=True)
    owner_i = owner.astype(jnp.int32)
    pick = jnp.where(lax.broadcasted_iota(jnp.int32, (LANES, img), 1) == owner_i, 1.0, 0.0).astype(BF16)
    pick_t = jnp.where(
        lax.broadcasted_iota(jnp.int32, (img, LANES), 0) == owner_row.astype(jnp.int32), 1.0, 0.0
    )
    count_lat = jnp.sum(
        jnp.where(lax.broadcasted_iota(jnp.int32, (LANES, n_img), 1) == owner_i, jnp.broadcast_to(counts_row, (LANES, n_img)), 0.0),
        axis=1, keepdims=True,
    )
    r.owner[...] = jnp.broadcast_to(count_lat, (LANES, LANES))

    for copy in pixel_copies:
        copy.wait()

    inside = lax.broadcasted_iota(jnp.int32, (img, CELLS), 1) < count
    for channel in range(3):
        rows_of = dot_nn(r.sel[...], r.pb[channel])
        window = jnp.concatenate([rows_of[j * img : (j + 1) * img] for j in range(9)], axis=1)
        for bit in range(7):
            hop = 1 << bit
            moved = pltpu.roll(window, span - hop, 1)
            window = jnp.where((shift_of & hop) != 0, moved, window)
        r.xi[channel] = jnp.where(inside, window[:, :CELLS], 0.0).astype(BF16)

    def gram_row(channel, x):
        base = geo[1 + channel : 2 + channel, :]
        return base, base + gram[channel][0] * x[0] + gram[channel][1] * x[1] + gram[channel][2] * x[2]

    for at in range(0, img, 16):
        x = [r.xi[channel, at : at + 16, :].astype(F32) for channel in range(3)]
        square = jnp.broadcast_to(geo[0:1, :], (16, CELLS))
        for channel in range(3):
            base, u = gram_row(channel, x)
            square = square + x[channel] * (base + u)
        r.ri[at : at + 16, :] = lax.rsqrt(square + TINY)
    for channel in range(3):
        r.xx[channel] = dot_nn(pick, r.xi[channel]).astype(BF16)
    inv_high, inv_low = split(r.ri[...])
    r.rr[...] = dot_nn(pick, inv_high) + dot_nn(pick, inv_low)

    def over_grid(code):
        return jnp.concatenate(split(code), axis=1)

    r.ss[...] = dot_nn(over_grid(query_code), r.ee[...])
    r.side[...] = query_code
    lane = lax.broadcasted_iota(jnp.int32, (tile, LANES), 1)
    place = lax.broadcasted_iota(jnp.int32, (tile, CELLS), 1).astype(F32)

    def side_columns(code, one, sums):
        made = jnp.where(lane == ONE, one, 0.0)
        for channel in range(3):
            made = made + jnp.where(lane == COLOR + channel, sums[channel], 0.0)
        return made

    def attend(at):
        code = r.side[at, :]
        x = [r.xx[channel, at, :].astype(F32) for channel in range(3)]
        inv = r.rr[at, :]
        raw = r.ss[at, :]
        for channel in range(3):
            raw = raw + code[:, COLOR + channel : COLOR + channel + 1] * x[channel]
        r.ss[at, :] = raw
        allowed = place < r.owner[at, :1]
        score = jnp.where(allowed, raw * inv + code[:, ONE : ONE + 1], FLOOR)
        top = jnp.max(score, axis=1, keepdims=True)
        raised = jnp.where(allowed, jnp.exp(score - top), 0.0)
        total = jnp.sum(raised, axis=1, keepdims=True)
        prob = raised / total
        r.pp[at, :] = prob
        weighted = prob * inv
        r.low[at, :] = weighted.astype(BF16)
        sums = [jnp.sum(weighted * x[channel], axis=1, keepdims=True) for channel in range(3)]
        r.side[at, :] = side_columns(code, jnp.sum(prob, axis=1, keepdims=True), sums)

    by_rows(attend)
    value_code = dot_nt(r.low[...], r.ee[:LANES, :]) + r.side[...]
    code_high, code_low = split(value_code)
    code_three = jnp.concatenate([code_high, code_high, code_low], axis=1)
    for j in range(0, width, 256):
        r.merged[:, j : j + 256] = dot_nn(code_three, r.tv[:, j : j + 256]).astype(BF16)
    value_code_low = code_high

    WO.wait()
    for j in range(0, width, 256):
        r.res[:, j : j + 256] = r.lat[:, j : j + 256].astype(F32) + dot_nn(r.merged[...], r.wo[:, j : j + 256])

    def norm_mid(at):
        x = r.res[at, :]
        center = x - jnp.mean(x, axis=-1, keepdims=True)
        inv = lax.rsqrt(jnp.mean(center * center, axis=-1, keepdims=True) + TINY)
        hat = center * inv
        r.xm[at, :] = hat
        r.rm[at, :] = jnp.broadcast_to(inv, (tile, LANES))
        r.nm[at, :] = (hat * mgain[...] + mshift[...]).astype(BF16)

    by_rows(norm_mid)
    WU.wait()
    for j in range(0, width, 256):
        pre = dot_nn(r.nm[...], r.wu[:, j : j + 256])
        phi = 0.5 * (1.0 + lax.erf(pre * math.sqrt(0.5)))
        r.act[:, j : j + 256] = (pre * phi).astype(BF16)
        slope = phi + pre * (jnp.exp(-0.5 * pre * pre) * (1.0 / math.sqrt(2.0 * math.pi)))
        r.bt[UP, mine, j : j + 256] = (r.ag[:, j : j + 256] * slope).astype(BF16)
    part_z = span_of(z, LANES)
    act_copies = exchange(
        n_batch, z, on_z, lambda target: r.act.at[:, span_of(target, tall)], lambda slot: r.az.at[part_z, :], r.az_s, r.az_r
    )
    r.az[part_z, :] = r.act[:, span_of(z, tall)]
    turn(UP, r.nm)
    send_left(UP)
    send_right(UP)
    turn(OUT, r.merged)
    send_left(OUT)

    for j in range(0, width, 256):
        r.nm[:, j : j + 256] = (r.res[:, j : j + 256] + dot_nn(r.act[...], r.wd[:, j : j + 256])).astype(BF16)
    leave(r.nm, o_mixed.at[0])
    for j in range(0, width, 256):
        r.ag[:, j : j + 256] = dot_nt(r.bt[UP, mine, :], r.wu[j : j + 256, :])
    product(UP)
    start(UP, 0)
    zero = jnp.zeros((1, width), F32)

    def norm_back(grad, hat, inv, gain):
        scaled = grad * gain
        return inv * (scaled - jnp.mean(scaled, axis=-1, keepdims=True) - hat * jnp.mean(scaled * hat, axis=-1, keepdims=True))

    def mid_back(i, carry):
        at = pl.ds(pl.multiple_of(i * tile, tile), tile)
        grad, hat = r.ag[at, :], r.xm[at, :]
        total = r.cot[at, :].astype(F32) + norm_back(grad, hat, r.rm[at, :1], mgain[...])
        r.res[at, :] = total
        r.bt[OUT, pl.ds(pl.multiple_of(c * LANES + i * tile, tile), tile), :] = total.astype(BF16)
        return carry[0] + jnp.sum(grad * hat, axis=0, keepdims=True), carry[1] + jnp.sum(grad, axis=0, keepdims=True)

    gain_sum, shift_sum = lax.fori_loop(0, LANES // tile, mid_back, (zero, zero), unroll=8)
    r.vec[...] = jnp.zeros_like(r.vec)
    r.vec[2:3, :] = gain_sum
    r.vec[3:4, :] = shift_sum
    send_right(OUT)
    for j in range(0, width, 256):
        r.da[:, j : j + 256] = dot_nt(r.bt[OUT, mine, :], r.wo[j : j + 256, :]).astype(BF16)

    back_code = dot_nt(r.da[...], r.tv[: 2 * LANES, :])
    back_code = back_code[:, :LANES] + back_code[:, LANES:]
    r.ag[...] = dot_nn(over_grid(back_code), r.ee[...])
    r.side[...] = back_code

    def attend_back(at):
        code = r.side[at, :]
        x = [r.xx[channel, at, :].astype(F32) for channel in range(3)]
        inv = r.rr[at, :]
        prob = r.pp[at, :]
        raw = r.ag[at, :]
        for channel in range(3):
            raw = raw + code[:, COLOR + channel : COLOR + channel + 1] * x[channel]
        grad = raw * inv + code[:, ONE : ONE + 1]
        delta = jnp.sum(prob * grad, axis=1, keepdims=True)
        back = prob * (grad - delta)
        r.ye[at, :] = (back * r.ss[at, :] + prob * raw).astype(BF16)
        weighted = back * inv
        r.low[at, :] = weighted.astype(BF16)
        r.dp[at, :] = back.astype(BF16)
        sums = [jnp.sum(weighted * x[channel], axis=1, keepdims=True) for channel in range(3)]
        r.side[at, :] = side_columns(code, jnp.sum(back, axis=1, keepdims=True), sums)

    by_rows(attend_back)
    r.dp[LANES:, :] = r.pp[...].astype(BF16)
    key_code = (dot_nt(r.low[...], r.ee[:LANES, :]) + r.side[...]) * scale
    code_high, code_low = split(key_code)
    code_three = jnp.concatenate([code_high, code_high, code_low], axis=1)
    for j in range(0, width, 256):
        r.bt[QUERY, mine, j : j + 256] = dot_nn(code_three, r.tk[:, j : j + 256]).astype(BF16)
    if apart:
        part_p = span_of(spot, LANES)
        piece = width // plane
        query_copies = exchange(
            plane, spot, in_plane, lambda target: r.bt.at[QUERY, mine, span_of(target, piece)], lambda slot: r.qp.at[part_p, :],
            r.qp_s, r.qp_r,
        )
        r.qp[part_p, :] = r.bt[QUERY, mine, span_of(spot, piece)]
    else:
        send_right(QUERY)
    kept = SimpleNamespace()
    heap = 256 // (2 * rows * parts["c"])

    def latents_gradient():
        for j in range(0, width, 256):
            r.ag[:, j : j + 256] = dot_nt(r.bt[QUERY, mine, :], r.wq[j : j + 256, :])

        def latents_back(i, carry):
            at = pl.ds(pl.multiple_of(i * tile, tile), tile)
            grad, hat = r.ag[at, :], r.xl[at, :]
            r.res[at, :] = r.res[at, :] + norm_back(grad, hat, r.rl[at, :1], qgain[...])
            return carry[0] + jnp.sum(grad * hat, axis=0, keepdims=True), carry[1] + jnp.sum(grad, axis=0, keepdims=True)

        gain_sum, shift_sum = lax.fori_loop(0, LANES // tile, latents_back, (zero, zero), unroll=8)
        r.vec[0:1, :] = gain_sum
        r.vec[1:2, :] = shift_sum
        leave(r.res, o_lat.at[0])

    def query_product():
        if apart:
            wait_all(norm_copies)
            wait_all(query_copies)
            for j in range(0, width, 256):
                made = dot_tn(r.qp[...], r.np[:, j : j + 256]).astype(BF16)
                r.qc[:, :, j : j + 256] = made.reshape(2, width // n_seq, 256)
            to_core("q", 6, r.qc.at[1 - c], r.qcr)
        else:
            product(QUERY)
            start(QUERY, 0)

    def sums_product():
        for j in range(0, 2 * width, 256):
            if j < width:
                made = dot_tn(r.q[:, j : j + 256], code_high)
            else:
                made = dot_tn(r.da[:, j - width : j - width + 256], value_code_low)
            riding = pltpu.roll(r.vec[:, j // 2 : j // 2 + LANES].T, ONE + 1, 1).reshape(-1, rows, LANES)
            made = made.reshape(-1, 2 * rows, LANES)
            made = jnp.concatenate([made[:, :rows] + riding, made[:, rows:]], axis=1)
            r.zc[heap * (j // 256) : heap * (j // 256 + 1)] = made.astype(BF16).reshape(heap, parts["c"], 2 * rows, LANES)
        to_core("z", 8, r.zc.at[:, part("c", 1 - c)], r.zcr)

    def query_line():
        if apart:
            core_copies.pop("q").wait()
            r.qcr[...] = (r.qc[c].astype(F32) + r.qcr[...].astype(F32)).astype(BF16)
            kept.sum_copies = exchange(
                n_batch, z, on_z, lambda target: r.qcr.at[:, span_of(target, tall)], lambda slot: r.qz.at[slot], r.qz_s, r.qz_r
            )

    def down_product():
        wait_all(cot_copies)
        wait_all(act_copies)
        for j in range(0, width, 256):
            made = dot_tn(r.az[...], r.gz[:, j : j + 256]).astype(BF16)
            r.dc[:, :, :, :, j : j + 256] = made.reshape(parts["a"], parts["b"], parts["c"], rows, 256)
        to_core("d", 7, r.dc.at[:, :, part("c", 1 - c)], r.dcr)

    def pixel_norm():
        in_gain, in_shift = jnp.zeros((feat, 1), F32), jnp.zeros((feat, 1), F32)
        for j in range(0, 2 * width, 256):
            sums = r.zc[heap * (j // 256) : heap * (j // 256 + 1)].reshape(256, LANES)
            spread = dot_nt(r.fct[...], jnp.concatenate([sums, sums], axis=1))
            factor = r.kvw[:, j : j + 256].astype(F32)
            in_gain = in_gain + jnp.sum(factor * spread[:feat], axis=1, keepdims=True)
            in_shift = in_shift + jnp.sum(factor * spread[wide : wide + 1], axis=1, keepdims=True)
        for at, column in ((0, in_gain), (1, in_shift)):
            for j in range(0, feat, LANES):
                some = min(LANES, feat - j)
                eye = lax.broadcasted_iota(jnp.int32, (some, LANES), 0) == lax.broadcasted_iota(jnp.int32, (some, LANES), 1)
                r.ar[0, at : at + 1, j : j + LANES] = jnp.sum(jnp.where(eye, column[j : j + some], 0.0), axis=0, keepdims=True)
        kept.seq_copies = []
        for offset in range(1, n_seq):
            slot = n_seq - offset - 1
            copy = pltpu.make_async_remote_copy(
                src_ref=r.ar.at[0], dst_ref=r.ars.at[slot], send_sem=r.as_s.at[offset - 1], recv_sem=r.as_r.at[slot],
                device_id=(z, lax.rem(s + offset, n_seq)), device_id_type=MESH,
            )
            copy.start()
            kept.seq_copies.append(copy)

    def sums_start():
        core_copies.pop("z").wait()
        both = r.zc[:, part("c", c)].astype(F32) + r.zcr[...].astype(F32)
        r.zs0[0] = both.astype(BF16).reshape(parts["z"], parts["a"], parts["b"], 2 * rows, LANES)
        start(SUMS, 0)

    def down_start():
        core_copies.pop("d").wait()
        r.ds0[0, 0] = (r.dc[:, :, part("c", c)].astype(F32) + r.dcr[...].astype(F32)).astype(BF16)
        start(DOWN, 0)

    def pixel_gradient():
        query_t, back_t = query_code.T, back_code.T
        lifted = jnp.concatenate(
            [
                jnp.concatenate([pick_t * code_t[COLOR + channel : COLOR + channel + 1, :] for code_t in (query_t, back_t)], axis=1)
                for channel in range(3)
            ],
            axis=0,
        ).astype(BF16)
        along = dot_nn(pick_t.astype(BF16), r.ye[...])
        inv = r.ri[...]
        cube = inv * inv * inv * along
        colors = [r.xi[channel].astype(F32) for channel in range(3)]
        for channel in range(3):
            steep = dot_nn(lifted[channel * img : (channel + 1) * img], r.dp[...])
            own_grad = inv * steep - cube * gram_row(channel, colors)[1]
            window = jnp.concatenate([own_grad, jnp.zeros((img, LANES), F32)], axis=1)
            for bit in range(7):
                hop = 1 << bit
                moved = pltpu.roll(window, hop, 1)
                window = jnp.where((shift_of & hop) != 0, moved, window)
            for j in range(9):
                r.pg[j * img : (j + 1) * img, :] = window[:, j * LANES : (j + 1) * LANES]
            grad_high, grad_low = split(r.pg[...])
            r.pgs[channel] = dot_tn(r.sel[...], grad_high) + dot_tn(r.sel[...], grad_low)

    def pixel_send():
        kept.grad_copies = []
        for offset in range(1, n_seq):
            target = lax.rem(s + offset, n_seq)
            copy = pltpu.make_async_remote_copy(
                src_ref=r.pgs.at[:, pl.ds(pl.multiple_of(target * blocks, blocks), blocks), :],
                dst_ref=r.pgr.at[n_seq - offset - 1],
                send_sem=r.pg_s.at[offset - 1], recv_sem=r.pg_r.at[n_seq - offset - 1],
                device_id=(z, target), device_id_type=MESH,
            )
            copy.start()
            kept.grad_copies.append(copy)

    def query_last():
        if apart:
            wait_all(kept.sum_copies)
            made = gathered(r.qcr[:, span_of(z, tall)], r.qz, n_batch)
            for j in range(0, tall, LANES):
                r.qt[j : j + LANES, :] = made[:, j : j + LANES].T
            few = tall // n_seq
            part_q = r.qo.at[:, span_of(s, LANES)]
            kept.last_copies = exchange(
                n_seq, s, in_row, lambda target: r.qt.at[span_of(target, few), :], lambda slot: part_q, r.qo_s, r.qo_r
            )
            r.qo[:, span_of(s, LANES)] = r.qt[span_of(s, few), :]

    def pixel_norm_line():
        wait_all(kept.seq_copies)
        r.ar[1] = gathered(r.ar[0], r.ars, n_seq)
        kept.z_copies = exchange(n_batch, z, on_z, lambda target: r.ar.at[1], lambda slot: r.arz.at[slot], r.ab_s, r.ab_r)

    product(OUT)
    start(OUT, 0)
    latents_gradient()
    sums_product()
    step(UP, 0)
    query_product()
    pixel_norm()
    query_line()
    sums_start()
    pixel_gradient()
    step(OUT, 0)
    step(UP, 1)
    pixel_send()
    pixel_norm_line()
    step(SUMS, 0)
    down_product()
    query_last()
    down_start()
    step(OUT, 1)
    step(SUMS, 1)
    step(DOWN, 0)
    if not apart:
        step(QUERY, 0)
        step(QUERY, 1)

    total_rows = width // (n_batch * n_seq)
    inner = 0
    for name in ("a", "b", "c"):
        if parts[name] < sizes[name]:
            inner = inner * sizes[name] + here[name]

    def finish(mat, made):
        step(mat, 1 if mat == DOWN else 2)
        if total_rows < rows:
            r.out[mat] = pltpu.roll(r.out[mat], lax.rem(rows - inner * total_rows, rows), 0)
        leave(r.out.at[mat, :total_rows], made)

    wait_all(kept.grad_copies)
    o_pix[...] = gathered(r.pgs[:, own, :], r.pgr, n_seq)
    finish(UP, o_wu)
    if apart:
        wait_all(kept.last_copies)
        leave(r.qo, o_wq)
    else:
        finish(QUERY, o_wq)
    wait_all(kept.z_copies)
    o_in[...] = gathered(r.ar[1], r.arz, n_batch)[:, :feat]
    finish(DOWN, o_wd)
    finish(OUT, o_wo)
    step(SUMS, 2)
    sums = r.zout[...]
    turned = sums
    if total_rows < rows:
        turned = pltpu.roll(sums, lax.rem(rows - inner * total_rows, rows), 0)
        sums = pltpu.roll(sums, lax.rem(2 * (rows - inner * total_rows), 2 * rows), 0)
    high, low = split(sums)
    code_high, code_low = split(r.mt[...].T)
    spread_left = jnp.concatenate([code_high, code_high, code_low], axis=1)
    o_kv[...] = dot_nt(jnp.concatenate([high, low, high], axis=1), spread_left)[: 2 * total_rows, :feat]
    square = jnp.concatenate([turned, jnp.zeros((LANES - 2 * rows, LANES), F32)], axis=0)
    o_vec[...] = square.T[COLOR : COLOR + 8, :total_rows]
    wait_all(leaving)


def hand_over(mixed, lat, pix, vec, wq, inner, kv, wo, wu, wd, *refs):
    o_mixed, o_lat, o_pix, o_qg, o_qs, o_wq, o_ig, o_is, o_kv, o_wo, o_mg, o_ms, o_wu, o_wd = refs
    for src, dst in ((mixed, o_mixed), (lat, o_lat), (wq, o_wq), (wo, o_wo), (wu, o_wu), (wd, o_wd), (kv, o_kv)):
        dst[...] = src[...]
    for channel in range(3):
        for j in range(pix.shape[1]):
            o_pix[channel, 0:1, j * LANES : (j + 1) * LANES] = pix[channel, j : j + 1, :]
    for i, dst in enumerate((o_qg, o_qs, o_mg, o_ms)):
        dst[...] = vec[4 + i, :]
    for i, dst in enumerate((o_ig, o_is)):
        dst[...] = inner[i, :]


def solution(mesh):
    n_batch, n_seq = mesh.shape["batch"], mesh.shape["seq"]

    def body(latents, pixels, counts, latent_image, query_gain, query_shift, query_weight, input_gain, input_shift,
             kv_weight, out_weight, mlp_gain, mlp_shift, up_weight, down_weight, cotangent):
        width = query_weight.shape[0]
        feat = kv_weight.shape[0]
        pix_dev = pixels.shape[2]
        n_img = counts.shape[1]
        fc, geo, fct, gram = position_tables(feat)
        scratch = shapes_of(n_batch, n_seq, width, pix_dev, n_img, feat)
        rows = width // (n_batch * n_seq)
        vm = pl.BlockSpec(memory_space=pltpu.VMEM)
        hbm = pl.BlockSpec(memory_space=pl.ANY)
        f32 = lambda *shape: jax.ShapeDtypeStruct(shape, F32)
        mixed, latent_grad, square = jax.ShapeDtypeStruct(latents.shape, BF16), f32(*latents.shape), f32(rows, width)
        kv = f32(2 * rows, feat)
        args = (
            latents, pixels, counts, latent_image,
            query_gain[None], query_shift[None], query_weight, input_gain, input_shift, kv_weight,
            out_weight, mlp_gain[None], mlp_shift[None], up_weight, down_weight, cotangent,
            jnp.asarray(fc), jnp.asarray(geo), jnp.asarray(fct),
        )
        in_hbm = (0, 6, 9, 10, 13, 14, 15, 16, 18)
        big = (0, 1, 4, 7, 8, 9)
        made = pl.pallas_call(
            functools.partial(layer, n_batch, n_seq, width, n_img, feat, gram),
            out_shape=(
                mixed, latent_grad, f32(3, pix_dev // LANES, LANES), f32(8, rows), square, f32(2, feat), kv, square, square, square,
            ),
            in_specs=[hbm if i in in_hbm else vm for i in range(len(args))],
            out_specs=[hbm if i in big else vm for i in range(10)],
            scratch_shapes=[vars(scratch)],
            compiler_params=pltpu.CompilerParams(
                collective_id=0, has_side_effects=True, vmem_limit_bytes=60 * 1024 * 1024
            ),
            name="layer",
        )(*args)
        out_shape = (
            mixed, latent_grad, f32(3, 1, pix_dev), f32(rows), f32(rows), square, f32(feat), f32(feat), kv, square,
            f32(rows), f32(rows), square, square,
        )
        out = pl.pallas_call(
            hand_over,
            out_shape=out_shape,
            in_specs=[vm] * len(made),
            out_specs=[vm] * len(out_shape),
            name="hand_over",
        )(*made)
        return (*out[:2], out[2].transpose(1, 0, 2), *out[3:8], out[8].T, *out[9:])

    whole, vec = P(("batch", "seq"), None), P(("batch", "seq"))
    rowed = P("batch", "seq", None)
    return jax.shard_map(
        body,
        mesh=mesh,
        in_specs=(rowed, P("batch", None, "seq"), P("batch", None), P("batch", None)) + (P(),) * 11 + (rowed,),
        out_specs=(
            rowed, rowed, P("batch", None, "seq"), vec, vec, whole, P(), P(), P(None, ("batch", "seq")), whole,
            vec, vec, whole, whole,
        ),
        check_vma=False,
    )
```

```python
import functools
import math
from types import SimpleNamespace

import jax
import jax.numpy as jnp
import numpy as np
from jax import lax
from jax.experimental import pallas as pl
from jax.experimental.pallas import tpu as pltpu
from jax.sharding import PartitionSpec as P

IMG_W = 32
TOP_FREQ = 112.0
TINY = 1e-05
FLOOR = -1e30
MESH = pl.DeviceIdType.MESH
F32 = jnp.float32
BF16 = jnp.bfloat16
LANES = 128
CELLS = IMG_W * IMG_W
COLOR = 2 * IMG_W
ONE = COLOR + 3


def position_tables(feat):
    bands = (feat - 5) // 4
    freq = np.linspace(1.0, TOP_FREQ, bands).astype(np.float32)
    grid = (np.float32(2.0) * np.arange(IMG_W, dtype=np.float32) / np.float32(IMG_W - 1) - np.float32(1.0)).astype(np.float32)
    phase = ((np.float32(math.pi) * grid)[:, None] * freq[None, :]).astype(np.float64)
    table = np.zeros((LANES, feat), np.float64)
    for axis in range(2):
        rows = slice(axis * IMG_W, (axis + 1) * IMG_W)
        table[rows, 3 + axis] = grid
        table[rows, 5 + axis * bands : 5 + (axis + 1) * bands] = np.sin(phase)
        table[rows, 5 + (2 + axis) * bands : 5 + (3 + axis) * bands] = np.cos(phase)
    for channel in range(3):
        table[COLOR + channel, channel] = 1.0
    centered = table - table.mean(axis=1, keepdims=True)
    gram = centered @ centered.T / feat
    place = np.arange(CELLS)
    row, col = place // IMG_W, IMG_W + place % IMG_W
    geometry = np.zeros((8, CELLS), np.float32)
    geometry[0] = gram[row, row] + gram[col, col] + 2.0 * gram[row, col]
    for channel in range(3):
        geometry[1 + channel] = gram[COLOR + channel, row] + gram[COLOR + channel, col]
    wide = -(-feat // LANES) * LANES
    padded = np.zeros((LANES, wide), np.float32)
    padded[:, :feat] = centered
    turned = np.zeros((wide + 8, LANES), np.float32)
    turned[:feat] = centered.T
    turned[wide, ONE] = 1.0
    high = turned.astype(jnp.bfloat16)
    low = (turned - high.astype(np.float32)).astype(jnp.bfloat16)
    colors = gram[COLOR : COLOR + 3, COLOR : COLOR + 3]
    return padded, geometry, np.concatenate([high, low], axis=1), [[float(v) for v in line] for line in colors]


def split(values):
    high = values.astype(BF16)
    return high, (values - high.astype(F32)).astype(BF16)


def dot_nn(left, right):
    return jnp.dot(left, right, preferred_element_type=F32)


def dot_nt(left, right):
    return lax.dot_general(left, right, (((1,), (1,)), ((), ())), preferred_element_type=F32)


def dot_tn(left, right):
    return lax.dot_general(left, right, (((0,), (0,)), ((), ())), preferred_element_type=F32)


def plan(n_batch, n_seq, width):
    core = 2
    fast = math.isqrt(n_seq // core)
    while (n_seq // core) % fast:
        fast -= 1
    slow = n_seq // core // fast
    sizes = {"z": n_batch, "a": slow, "b": fast, "c": core}
    parts, left = dict(sizes), width
    for name in ("c", "b", "a"):
        if width // math.prod(parts.values()) < 16:
            parts[name] = 1
    orders = (("b", "a") if parts["b"] > 1 else ("a", "b"), ("a", "b"))
    return sizes, parts, width // math.prod(parts.values()), orders


def by_columns(n_seq, width):
    return width // n_seq % LANES == 0


def shapes_of(n_batch, n_seq, width, pix_dev, n_img, feat):
    sizes, parts, rows, orders = plan(n_batch, n_seq, width)
    img = -(-n_img // 16) * 16
    blocks = pix_dev // LANES
    wide = -(-feat // LANES) * LANES
    factor_rows = (width // (2 * rows), 2, rows) if parts["c"] > 1 else (1, 1, width)
    S = SimpleNamespace()
    vm = lambda *shape, dtype=BF16: pltpu.VMEM(shape, dtype)
    S.wq, S.wo, S.wu, S.wd = [vm(width, width)] * 4
    S.tk = vm(3 * LANES, width)
    S.tv = vm(3 * LANES, width)
    S.ee = vm(2 * LANES, CELLS)
    S.mt = vm(LANES, wide, dtype=F32)
    S.xl, S.xm, S.res, S.ag = [vm(LANES, width, dtype=F32)] * 4
    S.rl = vm(LANES, LANES, dtype=F32)
    S.rm = vm(LANES, LANES, dtype=F32)
    S.nl, S.q, S.merged, S.nm, S.act, S.da = [vm(LANES, width)] * 6
    S.pb = vm(3, n_seq * blocks, LANES)
    S.sel = vm(9 * img, n_seq * blocks)
    S.xi = vm(3, img, CELLS)
    S.ri = vm(img, CELLS, dtype=F32)
    S.xx = vm(3, LANES, CELLS)
    S.rr = vm(LANES, CELLS, dtype=F32)
    S.ss = vm(LANES, CELLS, dtype=F32)
    S.pp = vm(LANES, CELLS, dtype=F32)
    S.low = vm(LANES, CELLS)
    S.dp = vm(2 * LANES, CELLS)
    S.ye = vm(LANES, CELLS)
    S.side = vm(LANES, LANES, dtype=F32)
    S.owner = vm(LANES, LANES, dtype=F32)
    S.pg = vm(9 * img, LANES, dtype=F32)
    S.pgs = vm(3, n_seq * blocks, LANES, dtype=F32)
    S.pgr = vm(n_seq - 1, 3, blocks, LANES, dtype=F32)
    tall, plane, apart = width // n_batch, n_seq // 2, by_columns(n_seq, width)
    full = 2 if apart else 3
    S.at = vm(full, *factor_rows, 2 * LANES)
    S.bt = vm(3, 2 * LANES, width)
    S.ms0 = vm(full, parts["z"], parts["a"], parts["b"], rows, width)
    S.ds0 = vm(1, 1, parts["a"], parts["b"], rows, width)
    S.zs0 = vm(1, parts["z"], parts["a"], parts["b"], 2 * rows, LANES)
    S.mr, S.dr, S.zr = [], [], []
    for made, mats, deep, across in ((S.mr, full, parts["z"], width // 2), (S.dr, 1, 1, width // 2), (S.zr, 1, parts["z"], LANES)):
        for first, other in orders:
            made.append([
                vm(mats, sizes[first] - 1, deep, parts[other], rows, across),
                vm(mats, sizes[other] - 1, deep, rows, across),
            ] + [vm(mats, sizes["z"] - 1, rows, across)] * (deep > 1))
    S.gz, S.az = vm(n_batch * LANES, width), vm(n_batch * LANES, tall)
    S.dc = vm(parts["a"], parts["b"], parts["c"], rows, width)
    S.dcr = vm(parts["a"], parts["b"], rows, width)
    if apart:
        S.np, S.qp = vm(plane * LANES, width), vm(plane * LANES, width // plane)
        S.qc, S.qcr = vm(2, width // n_seq, width), vm(width // n_seq, width)
        S.qz = vm(n_batch - 1, width // n_seq, tall)
        S.qt = vm(tall, width // n_seq, dtype=F32)
        S.qo = vm(tall // n_seq, width, dtype=F32)
    S.zc = vm(width // (rows * parts["c"]), parts["c"], 2 * rows, LANES)
    S.zcr = vm(width // (rows * parts["c"]), 2 * rows, LANES)
    S.vec = vm(LANES, width, dtype=F32)
    S.out = vm(4, rows, width, dtype=F32)
    S.zout = vm(2 * rows, LANES, dtype=F32)
    S.ar = vm(2, 2, wide, dtype=F32)
    S.ars = vm(n_seq - 1, 2, wide, dtype=F32)
    S.arz = vm(n_batch - 1, 2, wide, dtype=F32)
    S.lat, S.cot = [vm(LANES, width)] * 2
    S.kvw = vm(feat, 2 * width)
    S.fc = vm(LANES, wide, dtype=F32)
    S.fct = vm(wide + 8, 2 * LANES)
    most = max(sizes.values()) - 1
    sem = lambda *shape: pltpu.SemaphoreType.DMA(shape)
    S.w_sem = sem(9)
    S.o_sem = sem(6)
    S.px_s, S.px_r = sem(n_seq - 1), sem(n_seq - 1)
    S.pg_s, S.pg_r = sem(n_seq - 1), sem(n_seq - 1)
    S.co_s, S.co_r = sem(9), sem(9)
    S.gz_s, S.gz_r, S.az_s, S.az_r, S.qz_s, S.qz_r = [sem(n_batch - 1)] * 6
    S.np_s, S.np_r, S.qp_s, S.qp_r = [sem(plane - 1)] * 4
    S.qo_s, S.qo_r = [sem(n_seq - 1)] * 2
    S.rs_s, S.rs_r = sem(5, 2, 3, most), sem(5, 2, 3, most)
    S.as_s, S.as_r = sem(n_seq - 1), sem(n_seq - 1)
    S.ab_s, S.ab_r = sem(n_batch - 1), sem(n_batch - 1)
    return S


def layer(
    n_batch, n_seq, width, n_img, feat, gram,
    h_lat, px, cnt, img_of, qgain, qshift, h_wq, igain, ishift, h_kvw, h_wo, mgain, mshift, h_wu, h_wd, h_cot, h_fc, geo, h_fct,
    o_mixed, o_lat, o_pix, o_vec, o_wq, o_in, o_kv, o_wo, o_wu, o_wd, r,
):
    r = SimpleNamespace(**r)
    sizes, parts, rows, orders = plan(n_batch, n_seq, width)
    img = r.xi.shape[1]
    blocks = px.shape[2] // LANES
    wide = r.mt.shape[1]
    span = CELLS + LANES
    scale = width ** (-0.5)

    z = lax.axis_index("batch")
    s = lax.axis_index("seq")
    c = lax.rem(s, 2)
    b = lax.rem(s // 2, sizes["b"])
    a = s // (2 * sizes["b"])
    here = {"z": z, "a": a, "b": b, "c": c}

    def device(**moved):
        at = {**here, **moved}
        return (at["z"], (at["a"] * sizes["b"] + at["b"]) * 2 + at["c"])

    def part(name, index):
        return index if parts[name] > 1 else 0

    def peer(name, offset):
        return lax.rem(here[name] + offset, sizes[name])

    barrier = pltpu.get_barrier_semaphore()
    for offset in range(1, n_seq):
        pl.semaphore_signal(barrier, inc=1, device_id=(z, lax.rem(s + offset, n_seq)), device_id_type=MESH)
    for offset in range(1, n_batch):
        pl.semaphore_signal(barrier, inc=1, device_id=(peer("z", offset), s), device_id_type=MESH)

    arriving = []
    for i, (src, dst) in enumerate((
        (h_lat.at[0], r.lat), (h_fc, r.fc), (h_kvw, r.kvw), (h_wq, r.wq), (h_cot.at[0], r.cot), (h_wd, r.wd),
        (h_wo, r.wo), (h_wu, r.wu), (h_fct, r.fct),
    )):
        copy = pltpu.make_async_copy(src, dst, r.w_sem.at[i])
        copy.start()
        arriving.append(copy)
    LAT, FC, KVW, WQ, COT, WD, WO, WU, FCT = arriving
    leaving = []

    def leave(src, dst):
        copy = pltpu.make_async_copy(src, dst, r.o_sem.at[len(leaving)])
        copy.start()
        leaving.append(copy)

    UP, OUT, QUERY, DOWN, SUMS = range(5)
    apart = by_columns(n_seq, width)
    tall, plane = width // n_batch, n_seq // 2
    tile = 16

    def by_rows(step):
        def run(i, carry):
            step(pl.ds(pl.multiple_of(i * tile, tile), tile))
            return carry

        lax.fori_loop(0, LANES // tile, run, 0, unroll=8)

    mine = pl.ds(pl.multiple_of(c * LANES, LANES), LANES)

    def turn(which, factor):
        for j in range(width // LANES):
            block = factor[:, j * LANES : (j + 1) * LANES].astype(F32).T.astype(BF16)
            if parts["c"] > 1:
                deep = LANES // (2 * rows)
                r.at[which, j * deep : (j + 1) * deep, :, :, mine] = block.reshape(deep, 2, rows, LANES)
            else:
                r.at[which, 0, 0, j * LANES : (j + 1) * LANES, mine] = block

    core_copies = {}

    def to_core(key, index, src, dst):
        copy = pltpu.make_async_remote_copy(
            src_ref=src, dst_ref=dst, send_sem=r.co_s.at[index], recv_sem=r.co_r.at[index],
            device_id=device(c=1 - c), device_id_type=MESH,
        )
        copy.start()
        core_copies[key] = copy

    def send_left(which):
        ref = r.at.at[which, :, part("c", 1 - c), :, mine]
        to_core(("left", which), 2 * which, ref, ref)

    def send_right(which):
        ref = r.bt.at[which, mine, :]
        to_core(("right", which), 2 * which + 1, ref, ref)

    def start_stage(key, stage, name, src_of, dst):
        mat, half = key
        copies = []
        for offset in range(1, sizes[name]):
            target = peer(name, offset)
            slot = sizes[name] - offset - 1
            copy = pltpu.make_async_remote_copy(
                src_ref=src_of(part(name, target)), dst_ref=dst.at[slot],
                send_sem=r.rs_s.at[mat, half, stage, offset - 1], recv_sem=r.rs_r.at[mat, half, stage, slot],
                device_id=device(**{name: target}), device_id_type=MESH,
            )
            copy.start()
            copies.append(copy)
        return copies

    def wait_all(copies):
        for copy in copies:
            copy.wait()

    def gathered(own, dst, n):
        total = own.astype(F32)
        for slot in range(n - 1):
            total = total + dst[slot].astype(F32)
        return total

    flying = {}

    def buffers_of(mat):
        if mat == DOWN:
            return r.ds0, r.dr, 0
        return (r.zs0, r.zr, 0) if mat == SUMS else (r.ms0, r.mr, mat)

    def cut(mat, half):
        if mat == SUMS:
            return pl.ds(half * rows, rows), slice(None)
        return slice(None), pl.ds(half * (width // 2), width // 2)

    def renew(values):
        flat = values.reshape(-1, LANES)
        at = lax.broadcasted_iota(jnp.int32, flat.shape, 1)
        joined = flat + pltpu.roll(flat, LANES - 4, 1)
        high = joined.astype(BF16).astype(F32)
        rest = pltpu.roll(joined - high, 4, 1)
        riders = (at > ONE) & (at <= ONE + 4)
        flat = jnp.where(riders, high, jnp.where((at > ONE + 4) & (at <= ONE + 8), rest, flat))
        return flat.reshape(values.shape)

    def blocks_at(mat, half, stage, target=None):
        s0, received, i = buffers_of(mat)
        at = {"z": slice(None), "a": slice(None), "b": slice(None)}
        path = orders[half] + ("z",)
        for done in path[:stage]:
            at[done] = part(done, here[done])
        at[path[stage]] = part(path[stage], here[path[stage]]) if target is None else target
        return (i, at["z"], at["a"], at["b"]) + cut(mat, half)

    def start(mat, stage):
        s0, received, i = buffers_of(mat)
        for half in range(2):
            name = (orders[half] + ("z",))[stage]
            flying[mat, half] = start_stage(
                (mat, half), stage, name,
                lambda p: s0.at[blocks_at(mat, half, stage, p)],
                received[half][stage].at[i],
            )

    def step(mat, stage):
        s0, received, i = buffers_of(mat)
        last = 1 if mat == DOWN else 2
        for half in range(2):
            wait_all(flying[mat, half])
            name = (orders[half] + ("z",))[stage]
            keep = blocks_at(mat, half, stage)
            total = gathered(s0[keep], received[half][stage].at[i], sizes[name])
            if stage < last:
                s0[keep] = (renew(total) if mat == SUMS else total).astype(BF16)
            elif mat == SUMS:
                r.zout[cut(mat, half)] = total
            else:
                r.out[(mat,) + cut(mat, half)] = total[0] if mat == DOWN else total
        if stage < last:
            start(mat, stage + 1)

    def exchange(n, index, device_at, src_of, dst, sends, receives):
        copies = []
        for offset in range(1, n):
            target = lax.rem(index + offset, n)
            copy = pltpu.make_async_remote_copy(
                src_ref=src_of(target), dst_ref=dst(n - offset - 1), send_sem=sends.at[offset - 1],
                recv_sem=receives.at[n - offset - 1], device_id=device_at(target), device_id_type=MESH,
            )
            copy.start()
            copies.append(copy)
        return copies

    def span_of(index, size):
        return pl.ds(pl.multiple_of(index * size, size), size)

    on_z = lambda target: (target, s)
    in_plane = lambda target: (z, target * 2 + c)
    in_row = lambda target: (z, target)
    spot = s // 2

    def product(mat):
        core_copies.pop(("left", mat)).wait()
        core_copies.pop(("right", mat)).wait()
        left = r.at[mat, :, part("c", c)].reshape(-1, 2 * LANES)
        for j in range(0, width, 256):
            made = dot_nn(left, r.bt[mat, :, j : j + 256]).astype(BF16)
            r.ms0[mat, :, :, :, :, j : j + 256] = made.reshape(parts["z"], parts["a"], parts["b"], rows, 256)

    def norm_latents(at):
        x = r.lat[at, :].astype(F32)
        center = x - jnp.mean(x, axis=-1, keepdims=True)
        inv = lax.rsqrt(jnp.mean(center * center, axis=-1, keepdims=True) + TINY)
        hat = center * inv
        r.xl[at, :] = hat
        r.rl[at, :] = jnp.broadcast_to(inv, (tile, LANES))
        r.nl[at, :] = (hat * qgain[...] + qshift[...]).astype(BF16)

    LAT.wait()
    by_rows(norm_latents)
    COT.wait()
    r.gz[span_of(z, LANES), :] = r.cot[...]
    if apart:
        r.np[span_of(spot, LANES), :] = r.nl[...]
    else:
        turn(QUERY, r.nl)

    own = pl.ds(pl.multiple_of(s * blocks, blocks), blocks)
    colors = px[0].astype(F32)
    for channel in range(3):
        line = colors[channel : channel + 1]
        stacked = jnp.concatenate([line[:, j * LANES : (j + 1) * LANES] for j in range(blocks)], axis=0)
        r.pb[channel, own, :] = stacked.astype(BF16)
    pl.semaphore_wait(barrier, n_seq - 1 + n_batch - 1)
    pixel_copies = []
    for offset in range(1, n_seq):
        copy = pltpu.make_async_remote_copy(
            src_ref=r.pb.at[:, own, :], dst_ref=r.pb.at[:, own, :],
            send_sem=r.px_s.at[offset - 1], recv_sem=r.px_r.at[n_seq - offset - 1],
            device_id=(z, lax.rem(s + offset, n_seq)), device_id_type=MESH,
        )
        copy.start()
        pixel_copies.append(copy)
    if apart:
        own_norm = r.np.at[span_of(spot, LANES), :]
        norm_copies = exchange(plane, spot, in_plane, lambda target: own_norm, lambda slot: own_norm, r.np_s, r.np_r)
    else:
        send_left(QUERY)
    own_cot = r.gz.at[span_of(z, LANES), :]
    cot_copies = exchange(n_batch, z, on_z, lambda target: own_cot, lambda slot: own_cot, r.gz_s, r.gz_r)

    FCT.wait()
    FC.wait()
    KVW.wait()
    row_of = lax.broadcasted_iota(jnp.int32, (LANES, feat), 0)
    code = r.fc[:, :feat] * igain[...][None] + jnp.where(row_of == ONE, ishift[...][None], 0.0)
    r.mt[...] = jnp.zeros_like(r.mt)
    r.mt[:, :feat] = code
    code_high, code_low = split(code)
    code_both = jnp.concatenate([code_high, code_low], axis=0)
    for table, base in ((r.tk, 0), (r.tv, width)):
        for j in range(0, width, 256):
            both = dot_nn(code_both, r.kvw[:, base + j : base + j + 256])
            high, low = split(both[:LANES] + both[LANES:])
            table[:LANES, j : j + 256] = high
            table[LANES : 2 * LANES, j : j + 256] = low
            table[2 * LANES :, j : j + 256] = high
    cell = lax.broadcasted_iota(jnp.int32, (LANES, CELLS), 1)
    line = lax.broadcasted_iota(jnp.int32, (LANES, CELLS), 0)
    hit = (line == cell // IMG_W) | (line == IMG_W + lax.rem(cell, IMG_W))
    grid_code = jnp.where(hit, 1.0, 0.0).astype(BF16)
    r.ee[:LANES, :] = grid_code
    r.ee[LANES:, :] = grid_code

    WQ.wait()
    for j in range(0, width, 256):
        r.q[:, j : j + 256] = dot_nn(r.nl[...], r.wq[:, j : j + 256]).astype(BF16)
    query_code = dot_nt(r.q[...], r.tk[: 2 * LANES, :])
    query_code = (query_code[:, :LANES] + query_code[:, LANES:]) * scale

    WD.wait()
    for j in range(0, width, 256):
        r.ag[:, j : j + 256] = dot_nt(r.cot[...], r.wd[j : j + 256, :])

    counts_row = cnt[...].astype(F32)
    number = lax.broadcasted_iota(jnp.int32, (img, n_img), 0)
    against = lax.broadcasted_iota(jnp.int32, (img, n_img), 1)
    counts_all = jnp.broadcast_to(counts_row, (img, n_img))
    first = jnp.sum(jnp.where(against < number, counts_all, 0.0), axis=1, keepdims=True).astype(jnp.int32)
    count = jnp.sum(jnp.where(against == number, counts_all, 0.0), axis=1, keepdims=True).astype(jnp.int32)
    block_of = first // LANES
    shift_of = lax.rem(first, LANES)
    block_id = lax.broadcasted_iota(jnp.int32, (img, n_seq * blocks), 1)
    for j in range(9):
        r.sel[j * img : (j + 1) * img, :] = jnp.where(block_id == block_of + j, 1.0, 0.0).astype(BF16)

    mine_lat = pl.ds(pl.multiple_of(s * LANES, LANES), LANES)
    owner_row = img_of[:, mine_lat].astype(F32)
    square0 = lax.broadcasted_iota(jnp.int32, (LANES, LANES), 0)
    square1 = lax.broadcasted_iota(jnp.int32, (LANES, LANES), 1)
    diagonal = square0 == square1
    owner = jnp.sum(jnp.where(diagonal, jnp.broadcast_to(owner_row, (LANES, LANES)), 0.0), axis=1, keepdims=True)
    owner_i = owner.astype(jnp.int32)
    pick = jnp.where(lax.broadcasted_iota(jnp.int32, (LANES, img), 1) == owner_i, 1.0, 0.0).astype(BF16)
    pick_t = jnp.where(
        lax.broadcasted_iota(jnp.int32, (img, LANES), 0) == owner_row.astype(jnp.int32), 1.0, 0.0
    )
    count_lat = jnp.sum(
        jnp.where(lax.broadcasted_iota(jnp.int32, (LANES, n_img), 1) == owner_i, jnp.broadcast_to(counts_row, (LANES, n_img)), 0.0),
        axis=1, keepdims=True,
    )
    r.owner[...] = jnp.broadcast_to(count_lat, (LANES, LANES))

    for copy in pixel_copies:
        copy.wait()

    inside = lax.broadcasted_iota(jnp.int32, (img, CELLS), 1) < count
    for channel in range(3):
        rows_of = dot_nn(r.sel[...], r.pb[channel])
        window = jnp.concatenate([rows_of[j * img : (j + 1) * img] for j in range(9)], axis=1)
        for bit in range(7):
            hop = 1 << bit
            moved = pltpu.roll(window, span - hop, 1)
            window = jnp.where((shift_of & hop) != 0, moved, window)
        r.xi[channel] = jnp.where(inside, window[:, :CELLS], 0.0).astype(BF16)

    def gram_row(channel, x):
        base = geo[1 + channel : 2 + channel, :]
        return base, base + gram[channel][0] * x[0] + gram[channel][1] * x[1] + gram[channel][2] * x[2]

    for at in range(0, img, 16):
        x = [r.xi[channel, at : at + 16, :].astype(F32) for channel in range(3)]
        square = jnp.broadcast_to(geo[0:1, :], (16, CELLS))
        for channel in range(3):
            base, u = gram_row(channel, x)
            square = square + x[channel] * (base + u)
        r.ri[at : at + 16, :] = lax.rsqrt(square + TINY)
    for channel in range(3):
        r.xx[channel] = dot_nn(pick, r.xi[channel]).astype(BF16)
    inv_high, inv_low = split(r.ri[...])
    r.rr[...] = dot_nn(pick, inv_high) + dot_nn(pick, inv_low)

    def over_grid(code):
        return jnp.concatenate(split(code), axis=1)

    r.ss[...] = dot_nn(over_grid(query_code), r.ee[...])
    r.side[...] = query_code
    lane = lax.broadcasted_iota(jnp.int32, (tile, LANES), 1)
    place = lax.broadcasted_iota(jnp.int32, (tile, CELLS), 1).astype(F32)

    def side_columns(code, one, sums):
        made = jnp.where(lane == ONE, one, 0.0)
        for channel in range(3):
            made = made + jnp.where(lane == COLOR + channel, sums[channel], 0.0)
        return made

    def attend(at):
        code = r.side[at, :]
        x = [r.xx[channel, at, :].astype(F32) for channel in range(3)]
        inv = r.rr[at, :]
        raw = r.ss[at, :]
        for channel in range(3):
            raw = raw + code[:, COLOR + channel : COLOR + channel + 1] * x[channel]
        r.ss[at, :] = raw
        allowed = place < r.owner[at, :1]
        score = jnp.where(allowed, raw * inv + code[:, ONE : ONE + 1], FLOOR)
        top = jnp.max(score, axis=1, keepdims=True)
        raised = jnp.where(allowed, jnp.exp(score - top), 0.0)
        total = jnp.sum(raised, axis=1, keepdims=True)
        prob = raised / total
        r.pp[at, :] = prob
        weighted = prob * inv
        r.low[at, :] = weighted.astype(BF16)
        sums = [jnp.sum(weighted * x[channel], axis=1, keepdims=True) for channel in range(3)]
        r.side[at, :] = side_columns(code, jnp.sum(prob, axis=1, keepdims=True), sums)

    by_rows(attend)
    value_code = dot_nt(r.low[...], r.ee[:LANES, :]) + r.side[...]
    code_high, code_low = split(value_code)
    code_three = jnp.concatenate([code_high, code_high, code_low], axis=1)
    for j in range(0, width, 256):
        r.merged[:, j : j + 256] = dot_nn(code_three, r.tv[:, j : j + 256]).astype(BF16)
    value_code_low = code_high

    WO.wait()
    for j in range(0, width, 256):
        r.res[:, j : j + 256] = r.lat[:, j : j + 256].astype(F32) + dot_nn(r.merged[...], r.wo[:, j : j + 256])

    def norm_mid(at):
        x = r.res[at, :]
        center = x - jnp.mean(x, axis=-1, keepdims=True)
        inv = lax.rsqrt(jnp.mean(center * center, axis=-1, keepdims=True) + TINY)
        hat = center * inv
        r.xm[at, :] = hat
        r.rm[at, :] = jnp.broadcast_to(inv, (tile, LANES))
        r.nm[at, :] = (hat * mgain[...] + mshift[...]).astype(BF16)

    by_rows(norm_mid)
    WU.wait()
    for j in range(0, width, 256):
        pre = dot_nn(r.nm[...], r.wu[:, j : j + 256])
        phi = 0.5 * (1.0 + lax.erf(pre * math.sqrt(0.5)))
        r.act[:, j : j + 256] = (pre * phi).astype(BF16)
        slope = phi + pre * (jnp.exp(-0.5 * pre * pre) * (1.0 / math.sqrt(2.0 * math.pi)))
        r.bt[UP, mine, j : j + 256] = (r.ag[:, j : j + 256] * slope).astype(BF16)
    part_z = span_of(z, LANES)
    act_copies = exchange(
        n_batch, z, on_z, lambda target: r.act.at[:, span_of(target, tall)], lambda slot: r.az.at[part_z, :], r.az_s, r.az_r
    )
    r.az[part_z, :] = r.act[:, span_of(z, tall)]
    turn(UP, r.nm)
    send_left(UP)
    send_right(UP)
    turn(OUT, r.merged)
    send_left(OUT)

    for j in range(0, width, 256):
        r.nm[:, j : j + 256] = (r.res[:, j : j + 256] + dot_nn(r.act[...], r.wd[:, j : j + 256])).astype(BF16)
    leave(r.nm, o_mixed.at[0])
    for j in range(0, width, 256):
        r.ag[:, j : j + 256] = dot_nt(r.bt[UP, mine, :], r.wu[j : j + 256, :])
    product(UP)
    start(UP, 0)
    zero = jnp.zeros((1, width), F32)

    def norm_back(grad, hat, inv, gain):
        scaled = grad * gain
        return inv * (scaled - jnp.mean(scaled, axis=-1, keepdims=True) - hat * jnp.mean(scaled * hat, axis=-1, keepdims=True))

    def mid_back(i, carry):
        at = pl.ds(pl.multiple_of(i * tile, tile), tile)
        grad, hat = r.ag[at, :], r.xm[at, :]
        total = r.cot[at, :].astype(F32) + norm_back(grad, hat, r.rm[at, :1], mgain[...])
        r.res[at, :] = total
        r.bt[OUT, pl.ds(pl.multiple_of(c * LANES + i * tile, tile), tile), :] = total.astype(BF16)
        return carry[0] + jnp.sum(grad * hat, axis=0, keepdims=True), carry[1] + jnp.sum(grad, axis=0, keepdims=True)

    gain_sum, shift_sum = lax.fori_loop(0, LANES // tile, mid_back, (zero, zero), unroll=8)
    r.vec[...] = jnp.zeros_like(r.vec)
    r.vec[2:3, :] = gain_sum
    r.vec[3:4, :] = shift_sum
    send_right(OUT)
    for j in range(0, width, 256):
        r.da[:, j : j + 256] = dot_nt(r.bt[OUT, mine, :], r.wo[j : j + 256, :]).astype(BF16)

    back_code = dot_nt(r.da[...], r.tv[: 2 * LANES, :])
    back_code = back_code[:, :LANES] + back_code[:, LANES:]
    r.ag[...] = dot_nn(over_grid(back_code), r.ee[...])
    r.side[...] = back_code

    def attend_back(at):
        code = r.side[at, :]
        x = [r.xx[channel, at, :].astype(F32) for channel in range(3)]
        inv = r.rr[at, :]
        prob = r.pp[at, :]
        raw = r.ag[at, :]
        for channel in range(3):
            raw = raw + code[:, COLOR + channel : COLOR + channel + 1] * x[channel]
        grad = raw * inv + code[:, ONE : ONE + 1]
        delta = jnp.sum(prob * grad, axis=1, keepdims=True)
        back = prob * (grad - delta)
        r.ye[at, :] = (back * r.ss[at, :] + prob * raw).astype(BF16)
        weighted = back * inv
        r.low[at, :] = weighted.astype(BF16)
        r.dp[at, :] = back.astype(BF16)
        sums = [jnp.sum(weighted * x[channel], axis=1, keepdims=True) for channel in range(3)]
        r.side[at, :] = side_columns(code, jnp.sum(back, axis=1, keepdims=True), sums)

    by_rows(attend_back)
    r.dp[LANES:, :] = r.pp[...].astype(BF16)
    key_code = (dot_nt(r.low[...], r.ee[:LANES, :]) + r.side[...]) * scale
    code_high, code_low = split(key_code)
    code_three = jnp.concatenate([code_high, code_high, code_low], axis=1)
    for j in range(0, width, 256):
        r.bt[QUERY, mine, j : j + 256] = dot_nn(code_three, r.tk[:, j : j + 256]).astype(BF16)
    if apart:
        part_p = span_of(spot, LANES)
        piece = width // plane
        query_copies = exchange(
            plane, spot, in_plane, lambda target: r.bt.at[QUERY, mine, span_of(target, piece)], lambda slot: r.qp.at[part_p, :],
            r.qp_s, r.qp_r,
        )
        r.qp[part_p, :] = r.bt[QUERY, mine, span_of(spot, piece)]
    else:
        send_right(QUERY)
    kept = SimpleNamespace()
    heap = 256 // (2 * rows * parts["c"])

    def latents_gradient():
        for j in range(0, width, 256):
            r.ag[:, j : j + 256] = dot_nt(r.bt[QUERY, mine, :], r.wq[j : j + 256, :])

        def latents_back(i, carry):
            at = pl.ds(pl.multiple_of(i * tile, tile), tile)
            grad, hat = r.ag[at, :], r.xl[at, :]
            r.res[at, :] = r.res[at, :] + norm_back(grad, hat, r.rl[at, :1], qgain[...])
            return carry[0] + jnp.sum(grad * hat, axis=0, keepdims=True), carry[1] + jnp.sum(grad, axis=0, keepdims=True)

        gain_sum, shift_sum = lax.fori_loop(0, LANES // tile, latents_back, (zero, zero), unroll=8)
        r.vec[0:1, :] = gain_sum
        r.vec[1:2, :] = shift_sum
        leave(r.res, o_lat.at[0])

    def query_product():
        if apart:
            wait_all(norm_copies)
            wait_all(query_copies)
            for j in range(0, width, 256):
                made = dot_tn(r.qp[...], r.np[:, j : j + 256]).astype(BF16)
                r.qc[:, :, j : j + 256] = made.reshape(2, width // n_seq, 256)
            to_core("q", 6, r.qc.at[1 - c], r.qcr)
        else:
            product(QUERY)
            start(QUERY, 0)

    def sums_product():
        for j in range(0, 2 * width, 256):
            if j < width:
                made = dot_tn(r.q[:, j : j + 256], code_high)
            else:
                made = dot_tn(r.da[:, j - width : j - width + 256], value_code_low)
            riding = pltpu.roll(r.vec[:, j // 2 : j // 2 + LANES].T, ONE + 1, 1).reshape(-1, rows, LANES)
            made = made.reshape(-1, 2 * rows, LANES)
            made = jnp.concatenate([made[:, :rows] + riding, made[:, rows:]], axis=1)
            r.zc[heap * (j // 256) : heap * (j // 256 + 1)] = renew(made).astype(BF16).reshape(heap, parts["c"], 2 * rows, LANES)
        to_core("z", 8, r.zc.at[:, part("c", 1 - c)], r.zcr)

    def query_line():
        if apart:
            core_copies.pop("q").wait()
            r.qcr[...] = (r.qc[c].astype(F32) + r.qcr[...].astype(F32)).astype(BF16)
            kept.sum_copies = exchange(
                n_batch, z, on_z, lambda target: r.qcr.at[:, span_of(target, tall)], lambda slot: r.qz.at[slot], r.qz_s, r.qz_r
            )

    def down_product():
        wait_all(cot_copies)
        wait_all(act_copies)
        for j in range(0, width, 256):
            made = dot_tn(r.az[...], r.gz[:, j : j + 256]).astype(BF16)
            r.dc[:, :, :, :, j : j + 256] = made.reshape(parts["a"], parts["b"], parts["c"], rows, 256)
        to_core("d", 7, r.dc.at[:, :, part("c", 1 - c)], r.dcr)

    def pixel_norm():
        in_gain, in_shift = jnp.zeros((feat, 1), F32), jnp.zeros((feat, 1), F32)
        for j in range(0, 2 * width, 256):
            sums = r.zc[heap * (j // 256) : heap * (j // 256 + 1)].reshape(256, LANES)
            spread = dot_nt(r.fct[...], jnp.concatenate([sums, sums], axis=1))
            factor = r.kvw[:, j : j + 256].astype(F32)
            in_gain = in_gain + jnp.sum(factor * spread[:feat], axis=1, keepdims=True)
            in_shift = in_shift + jnp.sum(factor * spread[wide : wide + 1], axis=1, keepdims=True)
        for at, column in ((0, in_gain), (1, in_shift)):
            for j in range(0, feat, LANES):
                some = min(LANES, feat - j)
                eye = lax.broadcasted_iota(jnp.int32, (some, LANES), 0) == lax.broadcasted_iota(jnp.int32, (some, LANES), 1)
                r.ar[0, at : at + 1, j : j + LANES] = jnp.sum(jnp.where(eye, column[j : j + some], 0.0), axis=0, keepdims=True)
        kept.seq_copies = []
        for offset in range(1, n_seq):
            slot = n_seq - offset - 1
            copy = pltpu.make_async_remote_copy(
                src_ref=r.ar.at[0], dst_ref=r.ars.at[slot], send_sem=r.as_s.at[offset - 1], recv_sem=r.as_r.at[slot],
                device_id=(z, lax.rem(s + offset, n_seq)), device_id_type=MESH,
            )
            copy.start()
            kept.seq_copies.append(copy)

    def sums_start():
        core_copies.pop("z").wait()
        both = r.zc[:, part("c", c)].astype(F32) + r.zcr[...].astype(F32)
        r.zs0[0] = renew(both).astype(BF16).reshape(parts["z"], parts["a"], parts["b"], 2 * rows, LANES)
        start(SUMS, 0)

    def down_start():
        core_copies.pop("d").wait()
        r.ds0[0, 0] = (r.dc[:, :, part("c", c)].astype(F32) + r.dcr[...].astype(F32)).astype(BF16)
        start(DOWN, 0)

    def pixel_gradient():
        query_t, back_t = query_code.T, back_code.T
        lifted = jnp.concatenate(
            [
                jnp.concatenate([pick_t * code_t[COLOR + channel : COLOR + channel + 1, :] for code_t in (query_t, back_t)], axis=1)
                for channel in range(3)
            ],
            axis=0,
        ).astype(BF16)
        along = dot_nn(pick_t.astype(BF16), r.ye[...])
        inv = r.ri[...]
        cube = inv * inv * inv * along
        colors = [r.xi[channel].astype(F32) for channel in range(3)]
        for channel in range(3):
            steep = dot_nn(lifted[channel * img : (channel + 1) * img], r.dp[...])
            own_grad = inv * steep - cube * gram_row(channel, colors)[1]
            window = jnp.concatenate([own_grad, jnp.zeros((img, LANES), F32)], axis=1)
            for bit in range(7):
                hop = 1 << bit
                moved = pltpu.roll(window, hop, 1)
                window = jnp.where((shift_of & hop) != 0, moved, window)
            for j in range(9):
                r.pg[j * img : (j + 1) * img, :] = window[:, j * LANES : (j + 1) * LANES]
            grad_high, grad_low = split(r.pg[...])
            r.pgs[channel] = dot_tn(r.sel[...], grad_high) + dot_tn(r.sel[...], grad_low)

    def pixel_send():
        kept.grad_copies = []
        for offset in range(1, n_seq):
            target = lax.rem(s + offset, n_seq)
            copy = pltpu.make_async_remote_copy(
                src_ref=r.pgs.at[:, pl.ds(pl.multiple_of(target * blocks, blocks), blocks), :],
                dst_ref=r.pgr.at[n_seq - offset - 1],
                send_sem=r.pg_s.at[offset - 1], recv_sem=r.pg_r.at[n_seq - offset - 1],
                device_id=(z, target), device_id_type=MESH,
            )
            copy.start()
            kept.grad_copies.append(copy)

    def query_last():
        if apart:
            wait_all(kept.sum_copies)
            made = gathered(r.qcr[:, span_of(z, tall)], r.qz, n_batch)
            for j in range(0, tall, LANES):
                r.qt[j : j + LANES, :] = made[:, j : j + LANES].T
            few = tall // n_seq
            part_q = r.qo.at[:, span_of(s, LANES)]
            kept.last_copies = exchange(
                n_seq, s, in_row, lambda target: r.qt.at[span_of(target, few), :], lambda slot: part_q, r.qo_s, r.qo_r
            )
            r.qo[:, span_of(s, LANES)] = r.qt[span_of(s, few), :]

    def pixel_norm_line():
        wait_all(kept.seq_copies)
        r.ar[1] = gathered(r.ar[0], r.ars, n_seq)
        kept.z_copies = exchange(n_batch, z, on_z, lambda target: r.ar.at[1], lambda slot: r.arz.at[slot], r.ab_s, r.ab_r)

    product(OUT)
    start(OUT, 0)
    latents_gradient()
    sums_product()
    step(UP, 0)
    query_product()
    pixel_norm()
    query_line()
    sums_start()
    pixel_gradient()
    step(OUT, 0)
    step(UP, 1)
    pixel_send()
    pixel_norm_line()
    step(SUMS, 0)
    down_product()
    query_last()
    down_start()
    step(OUT, 1)
    step(SUMS, 1)
    step(DOWN, 0)
    if not apart:
        step(QUERY, 0)
        step(QUERY, 1)

    total_rows = width // (n_batch * n_seq)
    inner = 0
    for name in ("a", "b", "c"):
        if parts[name] < sizes[name]:
            inner = inner * sizes[name] + here[name]

    def finish(mat, made):
        step(mat, 1 if mat == DOWN else 2)
        if total_rows < rows:
            r.out[mat] = pltpu.roll(r.out[mat], lax.rem(rows - inner * total_rows, rows), 0)
        leave(r.out.at[mat, :total_rows], made)

    wait_all(kept.grad_copies)
    o_pix[...] = gathered(r.pgs[:, own, :], r.pgr, n_seq)
    finish(UP, o_wu)
    if apart:
        wait_all(kept.last_copies)
        leave(r.qo, o_wq)
    else:
        finish(QUERY, o_wq)
    wait_all(kept.z_copies)
    o_in[...] = gathered(r.ar[1], r.arz, n_batch)[:, :feat]
    finish(DOWN, o_wd)
    finish(OUT, o_wo)
    step(SUMS, 2)
    sums = r.zout[...]
    turned = sums
    if total_rows < rows:
        turned = pltpu.roll(sums, lax.rem(rows - inner * total_rows, rows), 0)
        sums = pltpu.roll(sums, lax.rem(2 * (rows - inner * total_rows), 2 * rows), 0)
    high, low = split(sums)
    code_high, code_low = split(r.mt[...].T)
    spread_left = jnp.concatenate([code_high, code_high, code_low], axis=1)
    o_kv[...] = dot_nt(jnp.concatenate([high, low, high], axis=1), spread_left)[: 2 * total_rows, :feat]
    square = jnp.concatenate([turned, jnp.zeros((LANES - 2 * rows, LANES), F32)], axis=0)
    square = square + pltpu.roll(square, LANES - 4, 1)
    o_vec[...] = square.T[COLOR : COLOR + 8, :total_rows]
    wait_all(leaving)


def hand_over(mixed, lat, pix, vec, wq, inner, kv, wo, wu, wd, *refs):
    o_mixed, o_lat, o_pix, o_qg, o_qs, o_wq, o_ig, o_is, o_kv, o_wo, o_mg, o_ms, o_wu, o_wd = refs
    for src, dst in ((mixed, o_mixed), (lat, o_lat), (wq, o_wq), (wo, o_wo), (wu, o_wu), (wd, o_wd), (kv, o_kv)):
        dst[...] = src[...]
    for channel in range(3):
        for j in range(pix.shape[1]):
            o_pix[channel, 0:1, j * LANES : (j + 1) * LANES] = pix[channel, j : j + 1, :]
    for i, dst in enumerate((o_qg, o_qs, o_mg, o_ms)):
        dst[...] = vec[4 + i, :]
    for i, dst in enumerate((o_ig, o_is)):
        dst[...] = inner[i, :]


def solution(mesh):
    n_batch, n_seq = mesh.shape["batch"], mesh.shape["seq"]

    def body(latents, pixels, counts, latent_image, query_gain, query_shift, query_weight, input_gain, input_shift,
             kv_weight, out_weight, mlp_gain, mlp_shift, up_weight, down_weight, cotangent):
        width = query_weight.shape[0]
        feat = kv_weight.shape[0]
        pix_dev = pixels.shape[2]
        n_img = counts.shape[1]
        fc, geo, fct, gram = position_tables(feat)
        scratch = shapes_of(n_batch, n_seq, width, pix_dev, n_img, feat)
        rows = width // (n_batch * n_seq)
        vm = pl.BlockSpec(memory_space=pltpu.VMEM)
        hbm = pl.BlockSpec(memory_space=pl.ANY)
        f32 = lambda *shape: jax.ShapeDtypeStruct(shape, F32)
        mixed, latent_grad, square = jax.ShapeDtypeStruct(latents.shape, BF16), f32(*latents.shape), f32(rows, width)
        kv = f32(2 * rows, feat)
        args = (
            latents, pixels, counts, latent_image,
            query_gain[None], query_shift[None], query_weight, input_gain, input_shift, kv_weight,
            out_weight, mlp_gain[None], mlp_shift[None], up_weight, down_weight, cotangent,
            jnp.asarray(fc), jnp.asarray(geo), jnp.asarray(fct),
        )
        in_hbm = (0, 6, 9, 10, 13, 14, 15, 16, 18)
        big = (0, 1, 4, 7, 8, 9)
        made = pl.pallas_call(
            functools.partial(layer, n_batch, n_seq, width, n_img, feat, gram),
            out_shape=(
                mixed, latent_grad, f32(3, pix_dev // LANES, LANES), f32(8, rows), square, f32(2, feat), kv, square, square, square,
            ),
            in_specs=[hbm if i in in_hbm else vm for i in range(len(args))],
            out_specs=[hbm if i in big else vm for i in range(10)],
            scratch_shapes=[vars(scratch)],
            compiler_params=pltpu.CompilerParams(
                collective_id=0, has_side_effects=True, vmem_limit_bytes=60 * 1024 * 1024
            ),
            name="layer",
        )(*args)
        out_shape = (
            mixed, latent_grad, f32(3, 1, pix_dev), f32(rows), f32(rows), square, f32(feat), f32(feat), kv, square,
            f32(rows), f32(rows), square, square,
        )
        out = pl.pallas_call(
            hand_over,
            out_shape=out_shape,
            in_specs=[vm] * len(made),
            out_specs=[vm] * len(out_shape),
            name="hand_over",
        )(*made)
        return (*out[:2], out[2].transpose(1, 0, 2), *out[3:8], out[8].T, *out[9:])

    whole, vec = P(("batch", "seq"), None), P(("batch", "seq"))
    rowed = P("batch", "seq", None)
    return jax.shard_map(
        body,
        mesh=mesh,
        in_specs=(rowed, P("batch", None, "seq"), P("batch", None), P("batch", None)) + (P(),) * 11 + (rowed,),
        out_specs=(
            rowed, rowed, P("batch", None, "seq"), vec, vec, whole, P(), P(), P(None, ("batch", "seq")), whole,
            vec, vec, whole, whole,
        ),
        check_vma=False,
    )
```

```python
import functools
import math
from types import SimpleNamespace

import jax
import jax.numpy as jnp
import numpy as np
from jax import lax
from jax.experimental import pallas as pl
from jax.experimental.pallas import tpu as pltpu
from jax.sharding import PartitionSpec as P

IMG_W = 32
TOP_FREQ = 112.0
TINY = 1e-05
FLOOR = -1e30
MESH = pl.DeviceIdType.MESH
F32 = jnp.float32
BF16 = jnp.bfloat16
LANES = 128
CELLS = IMG_W * IMG_W
COLOR = 2 * IMG_W
ONE = COLOR + 3


def position_tables(feat):
    bands = (feat - 5) // 4
    freq = np.linspace(1.0, TOP_FREQ, bands).astype(np.float32)
    grid = (np.float32(2.0) * np.arange(IMG_W, dtype=np.float32) / np.float32(IMG_W - 1) - np.float32(1.0)).astype(np.float32)
    phase = ((np.float32(math.pi) * grid)[:, None] * freq[None, :]).astype(np.float64)
    table = np.zeros((LANES, feat), np.float64)
    for axis in range(2):
        rows = slice(axis * IMG_W, (axis + 1) * IMG_W)
        table[rows, 3 + axis] = grid
        table[rows, 5 + axis * bands : 5 + (axis + 1) * bands] = np.sin(phase)
        table[rows, 5 + (2 + axis) * bands : 5 + (3 + axis) * bands] = np.cos(phase)
    for channel in range(3):
        table[COLOR + channel, channel] = 1.0
    centered = table - table.mean(axis=1, keepdims=True)
    gram = centered @ centered.T / feat
    place = np.arange(CELLS)
    row, col = place // IMG_W, IMG_W + place % IMG_W
    geometry = np.zeros((8, CELLS), np.float32)
    geometry[0] = gram[row, row] + gram[col, col] + 2.0 * gram[row, col]
    for channel in range(3):
        geometry[1 + channel] = gram[COLOR + channel, row] + gram[COLOR + channel, col]
    wide = -(-feat // LANES) * LANES
    padded = np.zeros((LANES, wide), np.float32)
    padded[:, :feat] = centered
    turned = np.zeros((wide + 8, LANES), np.float32)
    turned[:feat] = centered.T
    turned[wide, ONE] = 1.0
    high = turned.astype(jnp.bfloat16)
    low = (turned - high.astype(np.float32)).astype(jnp.bfloat16)
    colors = gram[COLOR : COLOR + 3, COLOR : COLOR + 3]
    return padded, geometry, np.concatenate([high, low], axis=1), [[float(v) for v in line] for line in colors]


def split(values):
    high = values.astype(BF16)
    return high, (values - high.astype(F32)).astype(BF16)


def dot_nn(left, right):
    return jnp.dot(left, right, preferred_element_type=F32)


def dot_nt(left, right):
    return lax.dot_general(left, right, (((1,), (1,)), ((), ())), preferred_element_type=F32)


def dot_tn(left, right):
    return lax.dot_general(left, right, (((0,), (0,)), ((), ())), preferred_element_type=F32)


def plan(n_batch, n_seq, width):
    core = 2
    fast = math.isqrt(n_seq // core)
    while (n_seq // core) % fast:
        fast -= 1
    slow = n_seq // core // fast
    sizes = {"z": n_batch, "a": slow, "b": fast, "c": core}
    parts, left = dict(sizes), width
    for name in ("c", "b", "a"):
        if width // math.prod(parts.values()) < 16:
            parts[name] = 1
    orders = (("b", "a") if parts["b"] > 1 else ("a", "b"), ("a", "b"))
    return sizes, parts, width // math.prod(parts.values()), orders


def by_columns(n_seq, width):
    return width // n_seq % LANES == 0


def shapes_of(n_batch, n_seq, width, pix_dev, n_img, feat):
    sizes, parts, rows, orders = plan(n_batch, n_seq, width)
    img = -(-n_img // 16) * 16
    blocks = pix_dev // LANES
    wide = -(-feat // LANES) * LANES
    factor_rows = (width // (2 * rows), 2, rows) if parts["c"] > 1 else (1, 1, width)
    S = SimpleNamespace()
    vm = lambda *shape, dtype=BF16: pltpu.VMEM(shape, dtype)
    S.wq, S.wo, S.wu, S.wd = [vm(width, width)] * 4
    S.tk = vm(3 * LANES, width)
    S.tv = vm(3 * LANES, width)
    S.ee = vm(2 * LANES, CELLS)
    S.mt = vm(LANES, wide, dtype=F32)
    S.xl, S.xm, S.res, S.ag = [vm(LANES, width, dtype=F32)] * 4
    S.rl = vm(LANES, LANES, dtype=F32)
    S.rm = vm(LANES, LANES, dtype=F32)
    S.nl, S.q, S.merged, S.nm, S.act, S.da = [vm(LANES, width)] * 6
    S.pb = vm(3, n_seq * blocks, LANES)
    S.sel = vm(9 * img, n_seq * blocks)
    S.xi = vm(3, img, CELLS)
    S.ri = vm(img, CELLS, dtype=F32)
    S.xx = vm(3, LANES, CELLS)
    S.rr = vm(LANES, CELLS, dtype=F32)
    S.ss = vm(LANES, CELLS, dtype=F32)
    S.pp = vm(LANES, CELLS, dtype=F32)
    S.low = vm(LANES, CELLS)
    S.dp = vm(2 * LANES, CELLS)
    S.ye = vm(LANES, CELLS)
    S.side = vm(LANES, LANES, dtype=F32)
    S.owner = vm(LANES, LANES, dtype=F32)
    S.pg = vm(9 * img, LANES, dtype=F32)
    S.pgs = vm(3, n_seq * blocks, LANES, dtype=F32)
    S.pgr = vm(n_seq - 1, 3, blocks, LANES, dtype=F32)
    tall, plane, apart = width // n_batch, n_seq // 2, by_columns(n_seq, width)
    full = 2 if apart else 3
    S.at = vm(full, *factor_rows, 2 * LANES)
    S.bt = vm(3, 2 * LANES, width)
    S.ms0 = vm(full, parts["z"], parts["a"], parts["b"], rows, width)
    S.ds0 = vm(1, 1, parts["a"], parts["b"], rows, width)
    S.zs0 = vm(1, parts["z"], parts["a"], parts["b"], 2 * rows, LANES)
    S.mr, S.dr, S.zr = [], [], []
    for made, mats, deep, across in ((S.mr, full, parts["z"], width // 2), (S.dr, 1, 1, width // 2), (S.zr, 1, parts["z"], LANES)):
        for first, other in orders:
            made.append([
                vm(mats, sizes[first] - 1, deep, parts[other], rows, across),
                vm(mats, sizes[other] - 1, deep, rows, across),
            ] + [vm(mats, sizes["z"] - 1, rows, across)] * (deep > 1))
    S.gz, S.az = vm(n_batch * LANES, width), vm(n_batch * LANES, tall)
    S.dc = vm(parts["a"], parts["b"], parts["c"], rows, width)
    S.dcr = vm(parts["a"], parts["b"], rows, width)
    if apart:
        S.np, S.qp = vm(plane * LANES, width), vm(plane * LANES, width // plane)
        S.qc, S.qcr = vm(2, width // n_seq, width), vm(width // n_seq, width)
        S.qz = vm(n_batch - 1, width // n_seq, tall)
        S.qt = vm(tall, width // n_seq, dtype=F32)
        S.qo = vm(tall // n_seq, width, dtype=F32)
    S.zc = vm(width // (rows * parts["c"]), parts["c"], 2 * rows, LANES)
    S.zcr = vm(width // (rows * parts["c"]), 2 * rows, LANES)
    S.vec = vm(LANES, width, dtype=F32)
    S.out = vm(4, rows, width, dtype=F32)
    S.zout = vm(2 * rows, LANES, dtype=F32)
    S.ar = vm(2, 2, wide, dtype=F32)
    S.ars = vm(n_seq - 1, 2, wide, dtype=F32)
    S.arz = vm(n_batch - 1, 2, wide, dtype=F32)
    S.lat, S.cot = [vm(LANES, width)] * 2
    S.kvw = vm(feat, 2 * width)
    S.fc = vm(LANES, wide, dtype=F32)
    S.fct = vm(wide + 8, 2 * LANES)
    most = max(sizes.values()) - 1
    sem = lambda *shape: pltpu.SemaphoreType.DMA(shape)
    S.w_sem = sem(9)
    S.o_sem = sem(6)
    S.px_s, S.px_r = sem(n_seq - 1), sem(n_seq - 1)
    S.pg_s, S.pg_r = sem(n_seq - 1), sem(n_seq - 1)
    S.co_s, S.co_r = sem(9), sem(9)
    S.gz_s, S.gz_r, S.az_s, S.az_r, S.qz_s, S.qz_r = [sem(n_batch - 1)] * 6
    S.np_s, S.np_r, S.qp_s, S.qp_r = [sem(plane - 1)] * 4
    S.qo_s, S.qo_r = [sem(n_seq - 1)] * 2
    S.rs_s, S.rs_r = sem(5, 2, 3, most), sem(5, 2, 3, most)
    S.as_s, S.as_r = sem(n_seq - 1), sem(n_seq - 1)
    S.ab_s, S.ab_r = sem(n_batch - 1), sem(n_batch - 1)
    return S


def layer(
    n_batch, n_seq, width, n_img, feat, gram,
    h_lat, px, cnt, img_of, qgain, qshift, h_wq, igain, ishift, h_kvw, h_wo, mgain, mshift, h_wu, h_wd, h_cot, h_fc, geo, h_fct,
    o_mixed, o_lat, o_pix, o_vec, o_wq, o_in, o_kv, o_wo, o_wu, o_wd, r,
):
    r = SimpleNamespace(**r)
    sizes, parts, rows, orders = plan(n_batch, n_seq, width)
    img = r.xi.shape[1]
    blocks = px.shape[2] // LANES
    wide = r.mt.shape[1]
    span = CELLS + LANES
    scale = width ** (-0.5)

    z = lax.axis_index("batch")
    s = lax.axis_index("seq")
    c = lax.rem(s, 2)
    b = lax.rem(s // 2, sizes["b"])
    a = s // (2 * sizes["b"])
    here = {"z": z, "a": a, "b": b, "c": c}

    def device(**moved):
        at = {**here, **moved}
        return (at["z"], (at["a"] * sizes["b"] + at["b"]) * 2 + at["c"])

    def part(name, index):
        return index if parts[name] > 1 else 0

    def peer(name, offset):
        return lax.rem(here[name] + offset, sizes[name])

    barrier = pltpu.get_barrier_semaphore()
    for offset in range(1, n_seq):
        pl.semaphore_signal(barrier, inc=1, device_id=(z, lax.rem(s + offset, n_seq)), device_id_type=MESH)
    for offset in range(1, n_batch):
        pl.semaphore_signal(barrier, inc=1, device_id=(peer("z", offset), s), device_id_type=MESH)

    arriving = []
    for i, (src, dst) in enumerate((
        (h_lat.at[0], r.lat), (h_fc, r.fc), (h_kvw, r.kvw), (h_wq, r.wq), (h_cot.at[0], r.cot), (h_wd, r.wd),
        (h_wo, r.wo), (h_wu, r.wu), (h_fct, r.fct),
    )):
        copy = pltpu.make_async_copy(src, dst, r.w_sem.at[i])
        copy.start()
        arriving.append(copy)
    LAT, FC, KVW, WQ, COT, WD, WO, WU, FCT = arriving
    leaving = []

    def leave(src, dst):
        copy = pltpu.make_async_copy(src, dst, r.o_sem.at[len(leaving)])
        copy.start()
        leaving.append(copy)

    UP, OUT, QUERY, DOWN, SUMS = range(5)
    apart = by_columns(n_seq, width)
    tall, plane = width // n_batch, n_seq // 2
    tile = 16

    def by_rows(step):
        def run(i, carry):
            step(pl.ds(pl.multiple_of(i * tile, tile), tile))
            return carry

        lax.fori_loop(0, LANES // tile, run, 0, unroll=8)

    mine = pl.ds(pl.multiple_of(c * LANES, LANES), LANES)

    def turn(which, factor):
        for j in range(width // LANES):
            block = factor[:, j * LANES : (j + 1) * LANES].astype(F32).T.astype(BF16)
            if parts["c"] > 1:
                deep = LANES // (2 * rows)
                r.at[which, j * deep : (j + 1) * deep, :, :, mine] = block.reshape(deep, 2, rows, LANES)
            else:
                r.at[which, 0, 0, j * LANES : (j + 1) * LANES, mine] = block

    core_copies = {}

    def to_core(key, index, src, dst):
        copy = pltpu.make_async_remote_copy(
            src_ref=src, dst_ref=dst, send_sem=r.co_s.at[index], recv_sem=r.co_r.at[index],
            device_id=device(c=1 - c), device_id_type=MESH,
        )
        copy.start()
        core_copies[key] = copy

    def send_left(which):
        ref = r.at.at[which, :, part("c", 1 - c), :, mine]
        to_core(("left", which), 2 * which, ref, ref)

    def send_right(which):
        ref = r.bt.at[which, mine, :]
        to_core(("right", which), 2 * which + 1, ref, ref)

    def start_stage(key, stage, name, src_of, dst):
        mat, half = key
        copies = []
        for offset in range(1, sizes[name]):
            target = peer(name, offset)
            slot = sizes[name] - offset - 1
            copy = pltpu.make_async_remote_copy(
                src_ref=src_of(part(name, target)), dst_ref=dst.at[slot],
                send_sem=r.rs_s.at[mat, half, stage, offset - 1], recv_sem=r.rs_r.at[mat, half, stage, slot],
                device_id=device(**{name: target}), device_id_type=MESH,
            )
            copy.start()
            copies.append(copy)
        return copies

    def wait_all(copies):
        for copy in copies:
            copy.wait()

    def gathered(own, dst, n):
        total = own.astype(F32)
        for slot in range(n - 1):
            total = total + dst[slot].astype(F32)
        return total

    flying = {}

    def buffers_of(mat):
        if mat == DOWN:
            return r.ds0, r.dr, 0
        return (r.zs0, r.zr, 0) if mat == SUMS else (r.ms0, r.mr, mat)

    def cut(mat, half):
        if mat == SUMS:
            return pl.ds(half * rows, rows), slice(None)
        return slice(None), pl.ds(half * (width // 2), width // 2)

    def renew(values):
        flat = values.reshape(-1, LANES)
        at = lax.broadcasted_iota(jnp.int32, flat.shape, 1)
        joined = flat + pltpu.roll(flat, LANES - 4, 1)
        high = joined.astype(BF16).astype(F32)
        rest = pltpu.roll(joined - high, 4, 1)
        riders = (at > ONE) & (at <= ONE + 4)
        flat = jnp.where(riders, high, jnp.where((at > ONE + 4) & (at <= ONE + 8), rest, flat))
        return flat.reshape(values.shape)

    def blocks_at(mat, half, stage, target=None):
        s0, received, i = buffers_of(mat)
        at = {"z": slice(None), "a": slice(None), "b": slice(None)}
        path = orders[half] + ("z",)
        for done in path[:stage]:
            at[done] = part(done, here[done])
        at[path[stage]] = part(path[stage], here[path[stage]]) if target is None else target
        return (i, at["z"], at["a"], at["b"]) + cut(mat, half)

    def start(mat, stage, halves=(0, 1)):
        s0, received, i = buffers_of(mat)
        for half in halves:
            name = (orders[half] + ("z",))[stage]
            flying[mat, half] = start_stage(
                (mat, half), stage, name,
                lambda p: s0.at[blocks_at(mat, half, stage, p)],
                received[half][stage].at[i],
            )

    def step(mat, stage):
        s0, received, i = buffers_of(mat)
        last = 1 if mat == DOWN else 2
        for half in range(2):
            wait_all(flying[mat, half])
            name = (orders[half] + ("z",))[stage]
            keep = blocks_at(mat, half, stage)
            total = gathered(s0[keep], received[half][stage].at[i], sizes[name])
            if stage < last:
                s0[keep] = (renew(total) if mat == SUMS else total).astype(BF16)
            elif mat == SUMS:
                r.zout[cut(mat, half)] = total
            else:
                r.out[(mat,) + cut(mat, half)] = total[0] if mat == DOWN else total
            if stage < last:
                start(mat, stage + 1, (half,))

    def exchange(n, index, device_at, src_of, dst, sends, receives):
        copies = []
        for offset in range(1, n):
            target = lax.rem(index + offset, n)
            copy = pltpu.make_async_remote_copy(
                src_ref=src_of(target), dst_ref=dst(n - offset - 1), send_sem=sends.at[offset - 1],
                recv_sem=receives.at[n - offset - 1], device_id=device_at(target), device_id_type=MESH,
            )
            copy.start()
            copies.append(copy)
        return copies

    def span_of(index, size):
        return pl.ds(pl.multiple_of(index * size, size), size)

    on_z = lambda target: (target, s)
    in_plane = lambda target: (z, target * 2 + c)
    in_row = lambda target: (z, target)
    spot = s // 2

    def product(mat):
        core_copies.pop(("left", mat)).wait()
        core_copies.pop(("right", mat)).wait()
        left = r.at[mat, :, part("c", c)].reshape(-1, 2 * LANES)
        for j in range(0, width, 256):
            made = dot_nn(left, r.bt[mat, :, j : j + 256]).astype(BF16)
            r.ms0[mat, :, :, :, :, j : j + 256] = made.reshape(parts["z"], parts["a"], parts["b"], rows, 256)

    def norm_latents(at):
        x = r.lat[at, :].astype(F32)
        center = x - jnp.mean(x, axis=-1, keepdims=True)
        inv = lax.rsqrt(jnp.mean(center * center, axis=-1, keepdims=True) + TINY)
        hat = center * inv
        r.xl[at, :] = hat
        r.rl[at, :] = jnp.broadcast_to(inv, (tile, LANES))
        r.nl[at, :] = (hat * qgain[...] + qshift[...]).astype(BF16)

    LAT.wait()
    by_rows(norm_latents)
    COT.wait()
    r.gz[span_of(z, LANES), :] = r.cot[...]
    if apart:
        r.np[span_of(spot, LANES), :] = r.nl[...]
    else:
        turn(QUERY, r.nl)

    own = pl.ds(pl.multiple_of(s * blocks, blocks), blocks)
    colors = px[0].astype(F32)
    for channel in range(3):
        line = colors[channel : channel + 1]
        stacked = jnp.concatenate([line[:, j * LANES : (j + 1) * LANES] for j in range(blocks)], axis=0)
        r.pb[channel, own, :] = stacked.astype(BF16)
    pl.semaphore_wait(barrier, n_seq - 1 + n_batch - 1)
    pixel_copies = []
    for offset in range(1, n_seq):
        copy = pltpu.make_async_remote_copy(
            src_ref=r.pb.at[:, own, :], dst_ref=r.pb.at[:, own, :],
            send_sem=r.px_s.at[offset - 1], recv_sem=r.px_r.at[n_seq - offset - 1],
            device_id=(z, lax.rem(s + offset, n_seq)), device_id_type=MESH,
        )
        copy.start()
        pixel_copies.append(copy)
    if apart:
        own_norm = r.np.at[span_of(spot, LANES), :]
        norm_copies = exchange(plane, spot, in_plane, lambda target: own_norm, lambda slot: own_norm, r.np_s, r.np_r)
    else:
        send_left(QUERY)
    own_cot = r.gz.at[span_of(z, LANES), :]
    cot_copies = exchange(n_batch, z, on_z, lambda target: own_cot, lambda slot: own_cot, r.gz_s, r.gz_r)

    FCT.wait()
    FC.wait()
    KVW.wait()
    row_of = lax.broadcasted_iota(jnp.int32, (LANES, feat), 0)
    code = r.fc[:, :feat] * igain[...][None] + jnp.where(row_of == ONE, ishift[...][None], 0.0)
    r.mt[...] = jnp.zeros_like(r.mt)
    r.mt[:, :feat] = code
    code_high, code_low = split(code)
    code_both = jnp.concatenate([code_high, code_low], axis=0)
    for table, base in ((r.tk, 0), (r.tv, width)):
        for j in range(0, width, 256):
            both = dot_nn(code_both, r.kvw[:, base + j : base + j + 256])
            high, low = split(both[:LANES] + both[LANES:])
            table[:LANES, j : j + 256] = high
            table[LANES : 2 * LANES, j : j + 256] = low
            table[2 * LANES :, j : j + 256] = high
    cell = lax.broadcasted_iota(jnp.int32, (LANES, CELLS), 1)
    line = lax.broadcasted_iota(jnp.int32, (LANES, CELLS), 0)
    hit = (line == cell // IMG_W) | (line == IMG_W + lax.rem(cell, IMG_W))
    grid_code = jnp.where(hit, 1.0, 0.0).astype(BF16)
    r.ee[:LANES, :] = grid_code
    r.ee[LANES:, :] = grid_code

    WQ.wait()
    for j in range(0, width, 256):
        r.q[:, j : j + 256] = dot_nn(r.nl[...], r.wq[:, j : j + 256]).astype(BF16)
    query_code = dot_nt(r.q[...], r.tk[: 2 * LANES, :])
    query_code = (query_code[:, :LANES] + query_code[:, LANES:]) * scale

    WD.wait()
    for j in range(0, width, 256):
        r.ag[:, j : j + 256] = dot_nt(r.cot[...], r.wd[j : j + 256, :])

    counts_row = cnt[...].astype(F32)
    number = lax.broadcasted_iota(jnp.int32, (img, n_img), 0)
    against = lax.broadcasted_iota(jnp.int32, (img, n_img), 1)
    counts_all = jnp.broadcast_to(counts_row, (img, n_img))
    first = jnp.sum(jnp.where(against < number, counts_all, 0.0), axis=1, keepdims=True).astype(jnp.int32)
    count = jnp.sum(jnp.where(against == number, counts_all, 0.0), axis=1, keepdims=True).astype(jnp.int32)
    block_of = first // LANES
    shift_of = lax.rem(first, LANES)
    block_id = lax.broadcasted_iota(jnp.int32, (img, n_seq * blocks), 1)
    for j in range(9):
        r.sel[j * img : (j + 1) * img, :] = jnp.where(block_id == block_of + j, 1.0, 0.0).astype(BF16)

    mine_lat = pl.ds(pl.multiple_of(s * LANES, LANES), LANES)
    owner_row = img_of[:, mine_lat].astype(F32)
    square0 = lax.broadcasted_iota(jnp.int32, (LANES, LANES), 0)
    square1 = lax.broadcasted_iota(jnp.int32, (LANES, LANES), 1)
    diagonal = square0 == square1
    owner = jnp.sum(jnp.where(diagonal, jnp.broadcast_to(owner_row, (LANES, LANES)), 0.0), axis=1, keepdims=True)
    owner_i = owner.astype(jnp.int32)
    pick = jnp.where(lax.broadcasted_iota(jnp.int32, (LANES, img), 1) == owner_i, 1.0, 0.0).astype(BF16)
    pick_t = jnp.where(
        lax.broadcasted_iota(jnp.int32, (img, LANES), 0) == owner_row.astype(jnp.int32), 1.0, 0.0
    )
    count_lat = jnp.sum(
        jnp.where(lax.broadcasted_iota(jnp.int32, (LANES, n_img), 1) == owner_i, jnp.broadcast_to(counts_row, (LANES, n_img)), 0.0),
        axis=1, keepdims=True,
    )
    r.owner[...] = jnp.broadcast_to(count_lat, (LANES, LANES))

    for copy in pixel_copies:
        copy.wait()

    inside = lax.broadcasted_iota(jnp.int32, (img, CELLS), 1) < count
    for channel in range(3):
        rows_of = dot_nn(r.sel[...], r.pb[channel])
        window = jnp.concatenate([rows_of[j * img : (j + 1) * img] for j in range(9)], axis=1)
        for bit in range(7):
            hop = 1 << bit
            moved = pltpu.roll(window, span - hop, 1)
            window = jnp.where((shift_of & hop) != 0, moved, window)
        r.xi[channel] = jnp.where(inside, window[:, :CELLS], 0.0).astype(BF16)

    def gram_row(channel, x):
        base = geo[1 + channel : 2 + channel, :]
        return base, base + gram[channel][0] * x[0] + gram[channel][1] * x[1] + gram[channel][2] * x[2]

    for at in range(0, img, 16):
        x = [r.xi[channel, at : at + 16, :].astype(F32) for channel in range(3)]
        square = jnp.broadcast_to(geo[0:1, :], (16, CELLS))
        for channel in range(3):
            base, u = gram_row(channel, x)
            square = square + x[channel] * (base + u)
        r.ri[at : at + 16, :] = lax.rsqrt(square + TINY)
    for channel in range(3):
        r.xx[channel] = dot_nn(pick, r.xi[channel]).astype(BF16)
    inv_high, inv_low = split(r.ri[...])
    r.rr[...] = dot_nn(pick, inv_high) + dot_nn(pick, inv_low)

    def over_grid(code):
        return jnp.concatenate(split(code), axis=1)

    r.ss[...] = dot_nn(over_grid(query_code), r.ee[...])
    r.side[...] = query_code
    lane = lax.broadcasted_iota(jnp.int32, (tile, LANES), 1)
    place = lax.broadcasted_iota(jnp.int32, (tile, CELLS), 1).astype(F32)

    def side_columns(code, one, sums):
        made = jnp.where(lane == ONE, one, 0.0)
        for channel in range(3):
            made = made + jnp.where(lane == COLOR + channel, sums[channel], 0.0)
        return made

    def attend(at):
        code = r.side[at, :]
        x = [r.xx[channel, at, :].astype(F32) for channel in range(3)]
        inv = r.rr[at, :]
        raw = r.ss[at, :]
        for channel in range(3):
            raw = raw + code[:, COLOR + channel : COLOR + channel + 1] * x[channel]
        r.ss[at, :] = raw
        allowed = place < r.owner[at, :1]
        score = jnp.where(allowed, raw * inv + code[:, ONE : ONE + 1], FLOOR)
        top = jnp.max(score, axis=1, keepdims=True)
        raised = jnp.where(allowed, jnp.exp(score - top), 0.0)
        total = jnp.sum(raised, axis=1, keepdims=True)
        prob = raised / total
        r.pp[at, :] = prob
        weighted = prob * inv
        r.low[at, :] = weighted.astype(BF16)
        sums = [jnp.sum(weighted * x[channel], axis=1, keepdims=True) for channel in range(3)]
        r.side[at, :] = side_columns(code, jnp.sum(prob, axis=1, keepdims=True), sums)

    by_rows(attend)
    value_code = dot_nt(r.low[...], r.ee[:LANES, :]) + r.side[...]
    code_high, code_low = split(value_code)
    code_three = jnp.concatenate([code_high, code_high, code_low], axis=1)
    for j in range(0, width, 256):
        r.merged[:, j : j + 256] = dot_nn(code_three, r.tv[:, j : j + 256]).astype(BF16)
    value_code_low = code_high

    WO.wait()
    for j in range(0, width, 256):
        r.res[:, j : j + 256] = r.lat[:, j : j + 256].astype(F32) + dot_nn(r.merged[...], r.wo[:, j : j + 256])

    def norm_mid(at):
        x = r.res[at, :]
        center = x - jnp.mean(x, axis=-1, keepdims=True)
        inv = lax.rsqrt(jnp.mean(center * center, axis=-1, keepdims=True) + TINY)
        hat = center * inv
        r.xm[at, :] = hat
        r.rm[at, :] = jnp.broadcast_to(inv, (tile, LANES))
        r.nm[at, :] = (hat * mgain[...] + mshift[...]).astype(BF16)

    by_rows(norm_mid)
    WU.wait()
    for j in range(0, width, 256):
        pre = dot_nn(r.nm[...], r.wu[:, j : j + 256])
        phi = 0.5 * (1.0 + lax.erf(pre * math.sqrt(0.5)))
        r.act[:, j : j + 256] = (pre * phi).astype(BF16)
        slope = phi + pre * (jnp.exp(-0.5 * pre * pre) * (1.0 / math.sqrt(2.0 * math.pi)))
        r.bt[UP, mine, j : j + 256] = (r.ag[:, j : j + 256] * slope).astype(BF16)
    part_z = span_of(z, LANES)
    act_copies = exchange(
        n_batch, z, on_z, lambda target: r.act.at[:, span_of(target, tall)], lambda slot: r.az.at[part_z, :], r.az_s, r.az_r
    )
    r.az[part_z, :] = r.act[:, span_of(z, tall)]
    turn(UP, r.nm)
    send_left(UP)
    send_right(UP)
    turn(OUT, r.merged)
    send_left(OUT)

    for j in range(0, width, 256):
        r.nm[:, j : j + 256] = (r.res[:, j : j + 256] + dot_nn(r.act[...], r.wd[:, j : j + 256])).astype(BF16)
    leave(r.nm, o_mixed.at[0])
    for j in range(0, width, 256):
        r.ag[:, j : j + 256] = dot_nt(r.bt[UP, mine, :], r.wu[j : j + 256, :])
    product(UP)
    start(UP, 0)
    zero = jnp.zeros((1, width), F32)

    def norm_back(grad, hat, inv, gain):
        scaled = grad * gain
        return inv * (scaled - jnp.mean(scaled, axis=-1, keepdims=True) - hat * jnp.mean(scaled * hat, axis=-1, keepdims=True))

    def mid_back(i, carry):
        at = pl.ds(pl.multiple_of(i * tile, tile), tile)
        grad, hat = r.ag[at, :], r.xm[at, :]
        total = r.cot[at, :].astype(F32) + norm_back(grad, hat, r.rm[at, :1], mgain[...])
        r.res[at, :] = total
        r.bt[OUT, pl.ds(pl.multiple_of(c * LANES + i * tile, tile), tile), :] = total.astype(BF16)
        return carry[0] + jnp.sum(grad * hat, axis=0, keepdims=True), carry[1] + jnp.sum(grad, axis=0, keepdims=True)

    gain_sum, shift_sum = lax.fori_loop(0, LANES // tile, mid_back, (zero, zero), unroll=8)
    r.vec[...] = jnp.zeros_like(r.vec)
    r.vec[2:3, :] = gain_sum
    r.vec[3:4, :] = shift_sum
    send_right(OUT)
    for j in range(0, width, 256):
        r.da[:, j : j + 256] = dot_nt(r.bt[OUT, mine, :], r.wo[j : j + 256, :]).astype(BF16)

    back_code = dot_nt(r.da[...], r.tv[: 2 * LANES, :])
    back_code = back_code[:, :LANES] + back_code[:, LANES:]
    r.ag[...] = dot_nn(over_grid(back_code), r.ee[...])
    r.side[...] = back_code

    def attend_back(at):
        code = r.side[at, :]
        x = [r.xx[channel, at, :].astype(F32) for channel in range(3)]
        inv = r.rr[at, :]
        prob = r.pp[at, :]
        raw = r.ag[at, :]
        for channel in range(3):
            raw = raw + code[:, COLOR + channel : COLOR + channel + 1] * x[channel]
        grad = raw * inv + code[:, ONE : ONE + 1]
        delta = jnp.sum(prob * grad, axis=1, keepdims=True)
        back = prob * (grad - delta)
        r.ye[at, :] = (back * r.ss[at, :] + prob * raw).astype(BF16)
        weighted = back * inv
        r.low[at, :] = weighted.astype(BF16)
        r.dp[at, :] = back.astype(BF16)
        sums = [jnp.sum(weighted * x[channel], axis=1, keepdims=True) for channel in range(3)]
        r.side[at, :] = side_columns(code, jnp.sum(back, axis=1, keepdims=True), sums)

    by_rows(attend_back)
    r.dp[LANES:, :] = r.pp[...].astype(BF16)
    key_code = (dot_nt(r.low[...], r.ee[:LANES, :]) + r.side[...]) * scale
    code_high, code_low = split(key_code)
    code_three = jnp.concatenate([code_high, code_high, code_low], axis=1)
    for j in range(0, width, 256):
        r.bt[QUERY, mine, j : j + 256] = dot_nn(code_three, r.tk[:, j : j + 256]).astype(BF16)
    if apart:
        part_p = span_of(spot, LANES)
        piece = width // plane
        query_copies = exchange(
            plane, spot, in_plane, lambda target: r.bt.at[QUERY, mine, span_of(target, piece)], lambda slot: r.qp.at[part_p, :],
            r.qp_s, r.qp_r,
        )
        r.qp[part_p, :] = r.bt[QUERY, mine, span_of(spot, piece)]
    else:
        send_right(QUERY)
    kept = SimpleNamespace()
    heap = 256 // (2 * rows * parts["c"])

    def latents_gradient():
        for j in range(0, width, 256):
            r.ag[:, j : j + 256] = dot_nt(r.bt[QUERY, mine, :], r.wq[j : j + 256, :])

        def latents_back(i, carry):
            at = pl.ds(pl.multiple_of(i * tile, tile), tile)
            grad, hat = r.ag[at, :], r.xl[at, :]
            r.res[at, :] = r.res[at, :] + norm_back(grad, hat, r.rl[at, :1], qgain[...])
            return carry[0] + jnp.sum(grad * hat, axis=0, keepdims=True), carry[1] + jnp.sum(grad, axis=0, keepdims=True)

        gain_sum, shift_sum = lax.fori_loop(0, LANES // tile, latents_back, (zero, zero), unroll=8)
        r.vec[0:1, :] = gain_sum
        r.vec[1:2, :] = shift_sum
        leave(r.res, o_lat.at[0])

    def query_product():
        if apart:
            wait_all(norm_copies)
            wait_all(query_copies)
            for j in range(0, width, 256):
                made = dot_tn(r.qp[...], r.np[:, j : j + 256]).astype(BF16)
                r.qc[:, :, j : j + 256] = made.reshape(2, width // n_seq, 256)
            to_core("q", 6, r.qc.at[1 - c], r.qcr)
        else:
            product(QUERY)
            start(QUERY, 0)

    def sums_product():
        for j in range(0, 2 * width, 256):
            if j < width:
                made = dot_tn(r.q[:, j : j + 256], code_high)
            else:
                made = dot_tn(r.da[:, j - width : j - width + 256], value_code_low)
            riding = pltpu.roll(r.vec[:, j // 2 : j // 2 + LANES].T, ONE + 1, 1).reshape(-1, rows, LANES)
            made = made.reshape(-1, 2 * rows, LANES)
            made = jnp.concatenate([made[:, :rows] + riding, made[:, rows:]], axis=1)
            r.zc[heap * (j // 256) : heap * (j // 256 + 1)] = renew(made).astype(BF16).reshape(heap, parts["c"], 2 * rows, LANES)
        to_core("z", 8, r.zc.at[:, part("c", 1 - c)], r.zcr)

    def query_line():
        if apart:
            core_copies.pop("q").wait()
            r.qcr[...] = (r.qc[c].astype(F32) + r.qcr[...].astype(F32)).astype(BF16)
            kept.sum_copies = exchange(
                n_batch, z, on_z, lambda target: r.qcr.at[:, span_of(target, tall)], lambda slot: r.qz.at[slot], r.qz_s, r.qz_r
            )

    def down_product():
        wait_all(cot_copies)
        wait_all(act_copies)
        for j in range(0, width, 256):
            made = dot_tn(r.az[...], r.gz[:, j : j + 256]).astype(BF16)
            r.dc[:, :, :, :, j : j + 256] = made.reshape(parts["a"], parts["b"], parts["c"], rows, 256)
        to_core("d", 7, r.dc.at[:, :, part("c", 1 - c)], r.dcr)

    def pixel_norm():
        in_gain, in_shift = jnp.zeros((feat, 1), F32), jnp.zeros((feat, 1), F32)
        for j in range(0, 2 * width, 256):
            sums = r.zc[heap * (j // 256) : heap * (j // 256 + 1)].reshape(256, LANES)
            spread = dot_nt(r.fct[...], jnp.concatenate([sums, sums], axis=1))
            factor = r.kvw[:, j : j + 256].astype(F32)
            in_gain = in_gain + jnp.sum(factor * spread[:feat], axis=1, keepdims=True)
            in_shift = in_shift + jnp.sum(factor * spread[wide : wide + 1], axis=1, keepdims=True)
        for at, column in ((0, in_gain), (1, in_shift)):
            for j in range(0, feat, LANES):
                some = min(LANES, feat - j)
                eye = lax.broadcasted_iota(jnp.int32, (some, LANES), 0) == lax.broadcasted_iota(jnp.int32, (some, LANES), 1)
                r.ar[0, at : at + 1, j : j + LANES] = jnp.sum(jnp.where(eye, column[j : j + some], 0.0), axis=0, keepdims=True)
        kept.seq_copies = []
        for offset in range(1, n_seq):
            slot = n_seq - offset - 1
            copy = pltpu.make_async_remote_copy(
                src_ref=r.ar.at[0], dst_ref=r.ars.at[slot], send_sem=r.as_s.at[offset - 1], recv_sem=r.as_r.at[slot],
                device_id=(z, lax.rem(s + offset, n_seq)), device_id_type=MESH,
            )
            copy.start()
            kept.seq_copies.append(copy)

    def sums_start():
        core_copies.pop("z").wait()
        both = r.zc[:, part("c", c)].astype(F32) + r.zcr[...].astype(F32)
        r.zs0[0] = renew(both).astype(BF16).reshape(parts["z"], parts["a"], parts["b"], 2 * rows, LANES)
        start(SUMS, 0)

    def down_start():
        core_copies.pop("d").wait()
        r.ds0[0, 0] = (r.dc[:, :, part("c", c)].astype(F32) + r.dcr[...].astype(F32)).astype(BF16)
        start(DOWN, 0)

    def pixel_gradient():
        query_t, back_t = query_code.T, back_code.T
        lifted = jnp.concatenate(
            [
                jnp.concatenate([pick_t * code_t[COLOR + channel : COLOR + channel + 1, :] for code_t in (query_t, back_t)], axis=1)
                for channel in range(3)
            ],
            axis=0,
        ).astype(BF16)
        along = dot_nn(pick_t.astype(BF16), r.ye[...])
        inv = r.ri[...]
        cube = inv * inv * inv * along
        colors = [r.xi[channel].astype(F32) for channel in range(3)]
        for channel in range(3):
            steep = dot_nn(lifted[channel * img : (channel + 1) * img], r.dp[...])
            own_grad = inv * steep - cube * gram_row(channel, colors)[1]
            window = jnp.concatenate([own_grad, jnp.zeros((img, LANES), F32)], axis=1)
            for bit in range(7):
                hop = 1 << bit
                moved = pltpu.roll(window, hop, 1)
                window = jnp.where((shift_of & hop) != 0, moved, window)
            for j in range(9):
                r.pg[j * img : (j + 1) * img, :] = window[:, j * LANES : (j + 1) * LANES]
            grad_high, grad_low = split(r.pg[...])
            r.pgs[channel] = dot_tn(r.sel[...], grad_high) + dot_tn(r.sel[...], grad_low)

    def pixel_send():
        kept.grad_copies = []
        for offset in range(1, n_seq):
            target = lax.rem(s + offset, n_seq)
            copy = pltpu.make_async_remote_copy(
                src_ref=r.pgs.at[:, pl.ds(pl.multiple_of(target * blocks, blocks), blocks), :],
                dst_ref=r.pgr.at[n_seq - offset - 1],
                send_sem=r.pg_s.at[offset - 1], recv_sem=r.pg_r.at[n_seq - offset - 1],
                device_id=(z, target), device_id_type=MESH,
            )
            copy.start()
            kept.grad_copies.append(copy)

    def query_last():
        if apart:
            wait_all(kept.sum_copies)
            made = gathered(r.qcr[:, span_of(z, tall)], r.qz, n_batch)
            for j in range(0, tall, LANES):
                r.qt[j : j + LANES, :] = made[:, j : j + LANES].T
            few = tall // n_seq
            part_q = r.qo.at[:, span_of(s, LANES)]
            kept.last_copies = exchange(
                n_seq, s, in_row, lambda target: r.qt.at[span_of(target, few), :], lambda slot: part_q, r.qo_s, r.qo_r
            )
            r.qo[:, span_of(s, LANES)] = r.qt[span_of(s, few), :]

    def pixel_norm_line():
        wait_all(kept.seq_copies)
        r.ar[1] = gathered(r.ar[0], r.ars, n_seq)
        kept.z_copies = exchange(n_batch, z, on_z, lambda target: r.ar.at[1], lambda slot: r.arz.at[slot], r.ab_s, r.ab_r)

    product(OUT)
    start(OUT, 0)
    latents_gradient()
    sums_product()
    step(UP, 0)
    query_product()
    query_line()
    pixel_norm()
    sums_start()
    pixel_gradient()
    step(OUT, 0)
    step(UP, 1)
    pixel_send()
    pixel_norm_line()
    step(SUMS, 0)
    down_product()
    query_last()
    down_start()
    step(OUT, 1)
    step(SUMS, 1)
    step(DOWN, 0)
    if not apart:
        step(QUERY, 0)
        step(QUERY, 1)

    total_rows = width // (n_batch * n_seq)
    inner = 0
    for name in ("a", "b", "c"):
        if parts[name] < sizes[name]:
            inner = inner * sizes[name] + here[name]

    def finish(mat, made):
        step(mat, 1 if mat == DOWN else 2)
        if total_rows < rows:
            r.out[mat] = pltpu.roll(r.out[mat], lax.rem(rows - inner * total_rows, rows), 0)
        leave(r.out.at[mat, :total_rows], made)

    wait_all(kept.grad_copies)
    o_pix[...] = gathered(r.pgs[:, own, :], r.pgr, n_seq)
    finish(UP, o_wu)
    if apart:
        wait_all(kept.last_copies)
        leave(r.qo, o_wq)
    else:
        finish(QUERY, o_wq)
    wait_all(kept.z_copies)
    o_in[...] = gathered(r.ar[1], r.arz, n_batch)[:, :feat]
    finish(DOWN, o_wd)
    finish(OUT, o_wo)
    step(SUMS, 2)
    sums = r.zout[...]
    turned = sums
    if total_rows < rows:
        turned = pltpu.roll(sums, lax.rem(rows - inner * total_rows, rows), 0)
        sums = pltpu.roll(sums, lax.rem(2 * (rows - inner * total_rows), 2 * rows), 0)
    high, low = split(sums)
    code_high, code_low = split(r.mt[...].T)
    spread_left = jnp.concatenate([code_high, code_high, code_low], axis=1)
    o_kv[...] = dot_nt(jnp.concatenate([high, low, high], axis=1), spread_left)[: 2 * total_rows, :feat]
    square = jnp.concatenate([turned, jnp.zeros((LANES - 2 * rows, LANES), F32)], axis=0)
    square = square + pltpu.roll(square, LANES - 4, 1)
    o_vec[...] = square.T[COLOR : COLOR + 8, :total_rows]
    wait_all(leaving)


def hand_over(mixed, lat, pix, vec, wq, inner, kv, wo, wu, wd, *refs):
    o_mixed, o_lat, o_pix, o_qg, o_qs, o_wq, o_ig, o_is, o_kv, o_wo, o_mg, o_ms, o_wu, o_wd = refs
    for src, dst in ((mixed, o_mixed), (lat, o_lat), (wq, o_wq), (wo, o_wo), (wu, o_wu), (wd, o_wd), (kv, o_kv)):
        dst[...] = src[...]
    for channel in range(3):
        for j in range(pix.shape[1]):
            o_pix[channel, 0:1, j * LANES : (j + 1) * LANES] = pix[channel, j : j + 1, :]
    for i, dst in enumerate((o_qg, o_qs, o_mg, o_ms)):
        dst[...] = vec[4 + i, :]
    for i, dst in enumerate((o_ig, o_is)):
        dst[...] = inner[i, :]


def solution(mesh):
    n_batch, n_seq = mesh.shape["batch"], mesh.shape["seq"]

    def body(latents, pixels, counts, latent_image, query_gain, query_shift, query_weight, input_gain, input_shift,
             kv_weight, out_weight, mlp_gain, mlp_shift, up_weight, down_weight, cotangent):
        width = query_weight.shape[0]
        feat = kv_weight.shape[0]
        pix_dev = pixels.shape[2]
        n_img = counts.shape[1]
        fc, geo, fct, gram = position_tables(feat)
        scratch = shapes_of(n_batch, n_seq, width, pix_dev, n_img, feat)
        rows = width // (n_batch * n_seq)
        vm = pl.BlockSpec(memory_space=pltpu.VMEM)
        hbm = pl.BlockSpec(memory_space=pl.ANY)
        f32 = lambda *shape: jax.ShapeDtypeStruct(shape, F32)
        mixed, latent_grad, square = jax.ShapeDtypeStruct(latents.shape, BF16), f32(*latents.shape), f32(rows, width)
        kv = f32(2 * rows, feat)
        args = (
            latents, pixels, counts, latent_image,
            query_gain[None], query_shift[None], query_weight, input_gain, input_shift, kv_weight,
            out_weight, mlp_gain[None], mlp_shift[None], up_weight, down_weight, cotangent,
            jnp.asarray(fc), jnp.asarray(geo), jnp.asarray(fct),
        )
        in_hbm = (0, 6, 9, 10, 13, 14, 15, 16, 18)
        big = (0, 1, 4, 7, 8, 9)
        made = pl.pallas_call(
            functools.partial(layer, n_batch, n_seq, width, n_img, feat, gram),
            out_shape=(
                mixed, latent_grad, f32(3, pix_dev // LANES, LANES), f32(8, rows), square, f32(2, feat), kv, square, square, square,
            ),
            in_specs=[hbm if i in in_hbm else vm for i in range(len(args))],
            out_specs=[hbm if i in big else vm for i in range(10)],
            scratch_shapes=[vars(scratch)],
            compiler_params=pltpu.CompilerParams(
                collective_id=0, has_side_effects=True, vmem_limit_bytes=60 * 1024 * 1024
            ),
            name="layer",
        )(*args)
        out_shape = (
            mixed, latent_grad, f32(3, 1, pix_dev), f32(rows), f32(rows), square, f32(feat), f32(feat), kv, square,
            f32(rows), f32(rows), square, square,
        )
        out = pl.pallas_call(
            hand_over,
            out_shape=out_shape,
            in_specs=[vm] * len(made),
            out_specs=[vm] * len(out_shape),
            name="hand_over",
        )(*made)
        return (*out[:2], out[2].transpose(1, 0, 2), *out[3:8], out[8].T, *out[9:])

    whole, vec = P(("batch", "seq"), None), P(("batch", "seq"))
    rowed = P("batch", "seq", None)
    return jax.shard_map(
        body,
        mesh=mesh,
        in_specs=(rowed, P("batch", None, "seq"), P("batch", None), P("batch", None)) + (P(),) * 11 + (rowed,),
        out_specs=(
            rowed, rowed, P("batch", None, "seq"), vec, vec, whole, P(), P(), P(None, ("batch", "seq")), whole,
            vec, vec, whole, whole,
        ),
        check_vma=False,
    )
```
